32 devices in a mesh: section: 4 (over y, x), dp: 8 (over z, core).
Axes of the slice: x: 2, y: 2, z: 4, core: 2. Of those that a mesh axis runs over, the one named last changes fastest.
Arguments:
- patches: bfloat16 [8192, 3072], P('dp'), may hold values from -6 to 6
- dec_input: bfloat16 [8192, 768], P('dp'), may hold values from -6 to 6
- lengths: int32 [128], P('dp'), may hold values from 1 to 64, as said below
- out_grad: bfloat16 [8192, 768], P('dp'), may hold values from -6 to 6
- wide: bfloat16 [4, 768, 3072], P('section'), may hold values from -0.3125 to 0.3125
- tall: bfloat16 [4, 3072, 768], P('section'), may hold values from -0.21875 to 0.21875
- gain: float32 [4, 2, 768], P('section'), may hold values from 0.5 to 1.5
- shift: float32 [4, 2, 768], P('section'), may hold values from -1.5 to 1.5
Outputs:
- section_out: bfloat16 [4, 8192, 768], P('section', 'dp')
- section_grads: float32 [4, 8192, 768], P('section', 'dp')
- wide_grad: float32 [4, 768, 3072], P('section', 'dp')
- tall_grad: float32 [4, 3072, 768], P('section', 'dp')
- gain_grad: float32 [4, 2, 768], P('section', None, 'dp')
- shift_grad: float32 [4, 2, 768], P('section', None, 'dp')
The draws below stay inside these ranges and needn't reach their ends.
Inputs may be any that keep to these rules, and one draw needn't show every extreme that they name: `lengths`: among each index of dp's 16 consecutive sequences at least one has length 64.
All inputs are finite; a program needn't handle non-finite values.
Results may differ from the reference program's by a relative error of at most 0.015.
Values may be sent and summed in bfloat16 or wider, within the bound.
No kernel may reach another device: no remote copies, remote signals or barrier semaphores. Data moves between devices by JAX's collectives and lax.ppermute only.
A program may use at most 192 MiB of HBM per device.

```python
from functools import partial
import jax
import jax.numpy as jnp
from jax import lax

D = 768
HEADS = 12
FF = 3072
HEAD_DIM = 64
PREFIX = 64
SEQ_DEV = 16
SEQS = 128
TOKENS = 8192
N_SECTION = 4


def draw_lengths(key, part):
    key = jax.random.fold_in(key, 7)
    key_one, key_two, key_three = jax.random.split(key, 3)
    left_draw = jax.random.randint(key_one, (SEQS,), 0, PREFIX)
    right_draw = jax.random.randint(key_two, (SEQS,), 0, PREFIX)
    drawn = 1 + left_draw * right_draw // PREFIX
    block_count = SEQS // SEQ_DEV
    full_places = jnp.arange(block_count) * SEQ_DEV + jax.random.randint(key_three, (block_count,), 0, SEQ_DEV)
    return drawn.at[full_places].set(PREFIX).astype(jnp.int32)


def shard_levels(rng, extent, shards, least, top_value):
    level, own = 1.0, jax.random.fold_in(rng, 6)
    for axis_at, shards_of in shards:
        steps = jnp.exp(jax.random.uniform(jax.random.fold_in(own, axis_at), (shards_of,), jnp.float32, least / len(shards), top_value / len(shards)))
        level = level * jnp.repeat(steps, extent[axis_at] // shards_of).reshape([-1 if axis == axis_at else 1 for axis in range(len(extent))])
    return level


def scatter_about(stream_key, extent, width, limit, shards=(), kind=jnp.bfloat16):
    values = width * jax.random.normal(stream_key, extent, jnp.float32)
    if shards:
        values = values * shard_levels(stream_key, extent, shards, -0.22, 0.18)
    return jnp.clip(values, -limit, limit).astype(kind)


def setup_inputs(seed: int = 0) -> dict:
    keys = jax.random.split(jax.random.key(seed), 9)
    patches = scatter_about(keys[0], (TOKENS, FF), 1.0, 6.0, ((0, 8),))
    dec_input = scatter_about(keys[1], (TOKENS, D), 1.0, 6.0, ((0, 8),))
    lengths = draw_lengths(jax.random.fold_in(keys[8], 71), 0)
    out_grad = scatter_about(keys[3], (TOKENS, D), 1.0, 6.0, ((0, 8),))
    wide = scatter_about(keys[4], (N_SECTION, D, FF), (D // 2) ** -0.5, 0.3125, ((0, 4),))
    tall = scatter_about(keys[5], (N_SECTION, FF, D), D ** -0.5, 0.21875, ((0, 4),))
    gain = jnp.clip(1.0 + 0.1 * jax.random.normal(keys[6], (N_SECTION, 2, D), jnp.float32), 0.5, 1.5)
    shift = scatter_about(keys[7], (N_SECTION, 2, D), 0.3, 1.5, ((0, 4),), jnp.float32)
    return dict(patches=patches, dec_input=dec_input, lengths=lengths, out_grad=out_grad, wide=wide, tall=tall, gain=gain, shift=shift)


EPS = 1e-05
NEG = -1e+30
HIGH = lax.Precision.HIGHEST

@jax.custom_vjp
def low(v):
    return lax.optimization_barrier(v.astype(jnp.bfloat16)).astype(jnp.float32)

@jax.custom_vjp
def low_back(v):
    return v

def low_keep(v):
    return (low(v), None)

def low_pass(kept, grad):
    return (grad,)

def back_keep(v):
    return (v, None)

def back_low(kept, grad):
    return (low(grad),)
low.defvjp(low_keep, low_pass)
low_back.defvjp(back_keep, back_low)

def layer_norm(values, gain_row, shift_row):
    center = values - lax.optimization_barrier(jnp.mean(values, -1, keepdims=True))
    spread = lax.optimization_barrier(jnp.mean(center * center, -1, keepdims=True))
    return center * lax.rsqrt(spread + EPS) * gain_row + shift_row

def product(left_op, right_op):
    return jnp.dot(left_op, right_op, precision=HIGH)

def attend(queries, key_rows, value_rows, allowed, seq_count):
    split_query = queries.reshape(seq_count, -1, HEADS, HEAD_DIM)
    split_key = key_rows.reshape(seq_count, -1, HEADS, HEAD_DIM)
    split_value = value_rows.reshape(seq_count, -1, HEADS, HEAD_DIM)
    scores = low_back(jnp.einsum('bqhd,bkhd->bhqk', split_query, split_key, precision=HIGH) * HEAD_DIM ** (-0.5))
    masked = scores if allowed is None else jnp.where(allowed, scores, NEG)
    row_max = lax.optimization_barrier(jnp.max(masked, -1, keepdims=True))
    shifted_exp = jnp.exp(masked - row_max)
    attn_probs = low(shifted_exp / lax.optimization_barrier(jnp.sum(shifted_exp, -1, keepdims=True)))
    mixed = jnp.einsum('bhqk,bkhd->bqhd', attn_probs, split_value, precision=HIGH)
    return low(low_back(mixed.reshape(-1, D)))

def reference(patches, dec_input, lengths, out_grad, wide, tall, gain, shift):
    seq_total = lengths.shape[0]
    group_size = 32
    while seq_total % group_size:
        group_size = group_size // 2
    group_count = seq_total // group_size
    places = jnp.arange(PREFIX, dtype=jnp.int32)
    causal = places[:, None] >= places[None, :]
    row_valid = (places[None, :] < lengths[:, None]).astype(jnp.float32).reshape(-1, 1)
    gelu_tanh = partial(jax.nn.gelu, approximate=True)

    def forward(wide_f, tall_f, gain_f, shift_f, dec_f, probe_embed, probe_first, probe_second):

        def group_step(unused, inputs):
            patch_g, dec_g, length_g, embed_g, first_g, second_g = inputs
            embedded = low_back(product(patch_g, tall_f[0]) + embed_g)
            stream = layer_norm(embedded, gain_f[0, 0], shift_f[0, 0])
            normed = low(layer_norm(stream, gain_f[0, 1], shift_f[0, 1]))
            projected = low(low_back(product(normed, wide_f[0][:, :3 * D])))
            attended = attend(projected[:, :D], projected[:, D:2 * D], projected[:, 2 * D:], None, group_size)
            first = low_back(low(stream + low_back(product(attended, wide_f[0][:, 3 * D:]))) + first_g)
            normed = low(layer_norm(first, gain_f[1, 0], shift_f[1, 0]))
            hidden = low_back(product(normed, wide_f[1]))
            active = low(gelu_tanh(hidden))
            summed = first + low_back(product(active, tall_f[1]))
            memory = low_back(low(layer_norm(summed, gain_f[1, 1], shift_f[1, 1])))
            is_valid = places[None, :] < length_g[:, None]
            allowed = (causal[None] & is_valid[:, None, :])[:, None]
            normed = low(layer_norm(dec_g, gain_f[2, 0], shift_f[2, 0]))
            projected = low(low_back(product(normed, wide_f[2][:, :3 * D])))
            attended = attend(projected[:, :D], projected[:, D:2 * D], projected[:, 2 * D:], allowed, group_size)
            middle = dec_g + low_back(product(attended, wide_f[2][:, 3 * D:]))
            normed_cross = low(layer_norm(middle, gain_f[2, 1], shift_f[2, 1]))
            queries = low(low_back(product(normed_cross, tall_f[2][:D])))
            key_value = low(low_back(product(memory, jnp.concatenate([tall_f[2][D:2 * D], tall_f[2][2 * D:3 * D]], axis=1))))
            crossed = attend(queries, key_value[:, :D], key_value[:, D:], None, group_size)
            second = low_back(low(middle + low_back(product(crossed, tall_f[2][3 * D:]))) + second_g)
            normed = low(layer_norm(second, gain_f[3, 0], shift_f[3, 0]))
            hidden = low_back(product(normed, wide_f[3]))
            active = low(gelu_tanh(hidden))
            summed = second + low_back(product(active, tall_f[3]))
            final = layer_norm(summed, gain_f[3, 1], shift_f[3, 1])
            return (unused, (final, (first, memory, second)))
        inputs = (patches.astype(jnp.float32).reshape(group_count, group_size * PREFIX, FF), dec_f.reshape(group_count, group_size * PREFIX, D), lengths.reshape(group_count, group_size), probe_embed.reshape(group_count, group_size * PREFIX, D), probe_first.reshape(group_count, group_size * PREFIX, D), probe_second.reshape(group_count, group_size * PREFIX, D))
        unused, results = lax.scan(jax.checkpoint(group_step), None, inputs)
        return (results[0], results[1])
    zero_probe = jnp.zeros((seq_total * PREFIX, D), jnp.float32)
    final, pullback, middles = jax.vjp(forward, wide.astype(jnp.float32), tall.astype(jnp.float32), gain, shift, dec_input.astype(jnp.float32), zero_probe, zero_probe, zero_probe, has_aux=True)
    cotangent = (out_grad.astype(jnp.float32) * row_valid).reshape(final.shape)
    grads = pullback(cotangent)
    section_out = jnp.stack([middles[0].reshape(-1, D), middles[1].reshape(-1, D), middles[2].reshape(-1, D), final.reshape(-1, D)]).astype(jnp.bfloat16)
    section_grads = jnp.stack([grads[5], grads[6], grads[4], grads[7]])
    return (section_out, section_grads, grads[0], grads[1], grads[2], grads[3])
```

```python
import functools

import jax
import jax.numpy as jnp
from jax import lax
from jax.experimental import pallas as pl
from jax.experimental.pallas import tpu as pltpu
from jax.sharding import PartitionSpec as P

D = 768
HEADS = 12
FF = 3072
HEAD_DIM = 64
PREFIX = 64
PANELS = FF // D
GROUP = 4
LANES = GROUP * HEAD_DIM
GROUPS = HEADS // GROUP
EPS = 1e-05
NEG = -1e30
SCALE = HEAD_DIM ** (-0.5)
MICRO = 4
SLOTS = 15
VMEM_LIMIT = 48 * 1024 * 1024
BF = jnp.bfloat16
F32 = jnp.float32

ENC = dict(u=0, q=1, k=2, v=3, p=4, att=5, gfirst=6, gemb=7)
MLP = dict(u=0, x=1, gb=2, a=3, gh=7)
DEC = dict(u=0, q=1, k=2, v=3, p=4, att=5, c=6, qc=7, mem=8, kc=9, vc=10, pc=11, cross=12, gsec=13, gmid=14)


def nn(left, right):
    return lax.dot_general(left, right, (((1,), (0,)), ((), ())), preferred_element_type=F32)


def nt(left, right):
    return lax.dot_general(left, right, (((1,), (1,)), ((), ())), preferred_element_type=F32)


def tn(left, right):
    return lax.dot_general(left, right, (((0,), (0,)), ((), ())), preferred_element_type=F32)


def standardize(values):
    center = values - jnp.mean(values, -1, keepdims=True)
    rstd = lax.rsqrt(jnp.mean(center * center, -1, keepdims=True) + EPS)
    return center * rstd, rstd


def norm_back(upstream, unit, rstd, gain_row):
    scaled = upstream * gain_row
    mean_one = jnp.mean(scaled, -1, keepdims=True)
    mean_two = jnp.mean(scaled * unit, -1, keepdims=True)
    grad = rstd * (scaled - mean_one - unit * mean_two)
    return grad, jnp.sum(upstream * unit, 0, keepdims=True), jnp.sum(upstream, 0, keepdims=True)


def gelu_pair(hidden):
    c = 0.7978845608028654
    square = hidden * hidden
    t = jnp.tanh(hidden * (c + (c * 0.044715) * square))
    half = 0.5 + 0.5 * t
    active = hidden * half
    slope = half + active * (1.0 - t) * (c + (3.0 * c * 0.044715) * square)
    return active, slope


def block_diagonal(rows):
    tiled = jnp.concatenate([rows] * GROUP, axis=0)
    at_row = lax.broadcasted_iota(jnp.int32, tiled.shape, 0) // HEAD_DIM
    at_lane = lax.broadcasted_iota(jnp.int32, tiled.shape, 1) // HEAD_DIM
    return jnp.where(at_row == at_lane, tiled, jnp.zeros_like(tiled))


def head_rows(pairs):
    low = lax.broadcasted_iota(jnp.int32, (PREFIX, 2 * HEAD_DIM), 1) < HEAD_DIM
    return jnp.concatenate([jnp.where(low, p[:PREFIX], p[PREFIX:]) for p in pairs], axis=1)


def attend(q_ref, k_ref, v_ref, p_ref, out_ref, length_of):
    def one(b, carry):
        rows = pl.ds(pl.multiple_of(b * PREFIX, PREFIX), PREFIX)
        if length_of is not None:
            key_at = lax.broadcasted_iota(jnp.int32, (PREFIX, LANES), 0)
            query_at = lax.broadcasted_iota(jnp.int32, (PREFIX, LANES), 1) % PREFIX
            allowed = (key_at <= query_at) & (key_at < length_of(b))
        for g in range(GROUPS):
            lanes = slice(g * LANES, (g + 1) * LANES)
            q, k, v = q_ref[rows, lanes], k_ref[rows, lanes], v_ref[rows, lanes]
            scores = nt(k, block_diagonal(q)) * SCALE
            if length_of is not None:
                scores = jnp.where(allowed, scores, NEG)
            e = jnp.exp(scores - jnp.max(scores, 0, keepdims=True))
            p = (e / jnp.sum(e, 0, keepdims=True)).astype(BF)
            p_ref[rows, lanes] = p
            pairs = [tn(p[:, i : i + 128], v[:, i : i + 128]) for i in range(0, LANES, 128)]
            out_ref[rows, lanes] = head_rows(pairs).astype(BF)
        return carry

    lax.fori_loop(0, q_ref.shape[0] // PREFIX, one, 0)


def attend_back(q_ref, k_ref, v_ref, p_ref, up_ref, gq_ref, gk_ref, gv_ref):
    def one(b, carry):
        rows = pl.ds(pl.multiple_of(b * PREFIX, PREFIX), PREFIX)
        for g in range(GROUPS):
            lanes = slice(g * LANES, (g + 1) * LANES)
            q, k, v, p, up = (r[rows, lanes] for r in (q_ref, k_ref, v_ref, p_ref, up_ref))
            up_diag = block_diagonal(up)
            grad_p = nt(v, up_diag)
            wide_p = p.astype(F32)
            grad_s = (wide_p * (grad_p - jnp.sum(grad_p * wide_p, 0, keepdims=True))).astype(BF)
            gv_ref[rows, lanes] = nn(p, up_diag).astype(BF)
            gk_ref[rows, lanes] = (nn(grad_s, block_diagonal(q)) * SCALE).astype(BF)
            pairs = [tn(grad_s[:, i : i + 128], k[:, i : i + 128]) for i in range(0, LANES, 128)]
            gq_ref[rows, lanes] = (head_rows(pairs) * SCALE).astype(BF)
        return carry

    lax.fori_loop(0, q_ref.shape[0] // PREFIX, one, 0)


class Copies:
    def __init__(self, sems):
        self.sems, self.used, self.stores = sems, 0, []

    def start(self, source, target):
        copy = pltpu.make_async_copy(source, target, self.sems.at[self.used])
        self.used += 1
        copy.start()
        return copy

    def store(self, source, target):
        self.stores.append(self.start(source, target))

    def finish(self):
        for copy in self.stores:
            copy.wait()


def slot_kernel(work, rows, *refs):
    (lengths, patches, text, cotangent, wide, tall, gain, shift, message, kept_in, kept32_in, out_in, grads_in, small_in,
     sent, kept, kept32, out, grads, small, wide_v, tall_v, big_a, big_b, big_c, one, f32_a, f32_b, small_v, sems) = refs
    del kept_in, kept32_in, out_in, grads_in, small_in
    section = lax.axis_index("section")
    seqs = rows // PREFIX

    def panel(big, p):
        return big.at[:, p * D : (p + 1) * D]

    def wide_panel(cp, p):
        cols = slice(p * D, (p + 1) * D)
        return cp.start(wide.at[:, cols], wide_v.at[:, cols])

    def tall_panel(cp, p):
        at = slice(p * D, (p + 1) * D)
        return cp.start(tall.at[at], tall_v.at[at])

    def norm_rows(at):
        return gain[at : at + 1, :], shift[at : at + 1, :]

    def put_small(cp, m, early, late):
        small_v[0:1, :], small_v[1:2, :] = early[0], late[0]
        small_v[2:3, :], small_v[3:4, :] = early[1], late[1]
        cp.store(small_v, small.at[m])

    def encode(m):
        cp, mine = Copies(sems), slice(m * rows, (m + 1) * rows)
        loads = [(cp.start(patches.at[mine, p * D : (p + 1) * D], panel(big_a, p)), tall_panel(cp, p)) for p in range(PANELS)]
        wides = [wide_panel(cp, p) for p in range(PANELS)]
        for p in range(PANELS):
            for copy in loads[p]:
                copy.wait()
            cols = slice(p * D, (p + 1) * D)
            part = nn(big_a[:, cols], tall_v[cols, :])
            f32_a[...] = part if p == 0 else f32_a[...] + part
        cp.store(f32_a, kept32.at[mine])
        (gain_0, shift_0), (gain_1, shift_1) = norm_rows(0), norm_rows(1)
        stream = standardize(f32_a[...])[0] * gain_0 + shift_0
        f32_b[...] = stream
        one[0] = (standardize(stream)[0] * gain_1 + shift_1).astype(BF)
        cp.store(one.at[0], kept.at[ENC["u"], mine])
        for p in range(3):
            wides[p].wait()
            cols = slice(p * D, (p + 1) * D)
            big_b[:, cols] = nn(one[0], wide_v[:, cols]).astype(BF)
            cp.store(panel(big_b, p), kept.at[ENC["q"] + p, mine])
        attend(panel(big_b, 0), panel(big_b, 1), panel(big_b, 2), panel(big_b, 3), one.at[1], None)
        cp.store(panel(big_b, 3), kept.at[ENC["p"], mine])
        cp.store(one.at[1], kept.at[ENC["att"], mine])
        wides[3].wait()
        sent[...] = (f32_b[...] + nn(one[1], wide_v[:, 3 * D :])).astype(BF)
        cp.store(sent, out.at[mine])
        cp.finish()

    def encode_back(m):
        cp, mine = Copies(sems), slice(m * rows, (m + 1) * rows)
        wides = [wide_panel(cp, p) for p in (3, 0, 1, 2)]
        wides = wides[1:] + wides[:1]
        loads = [cp.start(kept.at[ENC["q"] + p, mine], panel(big_b, p)) for p in range(4)]
        load_embedded = cp.start(kept32.at[mine], f32_a)
        cp.store(message, kept.at[ENC["gfirst"], mine])
        wides[3].wait()
        one[0] = nt(message[...], wide_v[:, 3 * D :]).astype(BF)
        for copy in loads:
            copy.wait()
        attend_back(*(panel(big_b, p) for p in range(4)), one.at[0], *(panel(big_a, p) for p in range(3)))
        for p in range(3):
            cp.store(panel(big_a, p), kept.at[ENC["q"] + p, mine])
            wides[p].wait()
        upstream = nt(big_a[:, : 3 * D], wide_v[:, : 3 * D])
        load_embedded.wait()
        (gain_0, shift_0), (gain_1, shift_1) = norm_rows(0), norm_rows(1)
        unit_0, rstd_0 = standardize(f32_a[...])
        unit_1, rstd_1 = standardize(unit_0 * gain_0 + shift_0)
        grad, *late = norm_back(upstream, unit_1, rstd_1, gain_1)
        grad, *early = norm_back(grad + message[...].astype(F32), unit_0, rstd_0, gain_0)
        one[1] = grad.astype(BF)
        f32_b[...] = one[1].astype(F32)
        cp.store(one.at[1], kept.at[ENC["gemb"], mine])
        cp.store(f32_b, grads.at[mine])
        put_small(cp, m, early, late)
        cp.finish()

    def mlp_forward(cp, m, keep, wides, talls):
        mine = slice(m * rows, (m + 1) * rows)
        gain_0, shift_0 = norm_rows(0)
        stream = message[...].astype(F32)
        one[0] = (standardize(stream)[0] * gain_0 + shift_0).astype(BF)
        cp.store(one.at[0], kept.at[MLP["u"], mine])
        for p in range(PANELS):
            wides[p].wait()
            cols = slice(p * D, (p + 1) * D)
            active, slope = gelu_pair(nn(one[0], wide_v[:, cols]))
            big_a[:, cols] = active.astype(BF)
            big_b[:, cols] = slope.astype(BF)
            cp.store(panel(big_a, p), kept.at[MLP["a"] + p, mine])
            if keep:
                cp.store(panel(big_b, p), kept.at[MLP["gh"] + p, mine])
        for p in range(PANELS):
            talls[p].wait()
        return message[...].astype(F32) + nn(big_a[...], tall_v[...])

    def mlp_backward(cp, m, upstream, summed, wides, talls, slopes):
        mine = slice(m * rows, (m + 1) * rows)
        gain_0, gain_1 = norm_rows(0)[0], norm_rows(1)[0]
        grad, *late = norm_back(upstream, *standardize(summed), gain_1)
        f32_b[...] = grad
        one[1] = grad.astype(BF)
        cp.store(one.at[1], kept.at[MLP["gb"], mine])
        for p in range(PANELS):
            for copy in (talls[p], slopes[p]):
                if copy is not None:
                    copy.wait()
            cols = slice(p * D, (p + 1) * D)
            back = nt(one[1], tall_v[cols, :])
            big_c[:, cols] = (back * big_b[:, cols].astype(F32)).astype(BF)
            cp.store(panel(big_c, p), kept.at[MLP["gh"] + p, mine])
        for copy in wides:
            if copy is not None:
                copy.wait()
        upstream = nt(big_c[...], wide_v[...])
        return upstream, late

    def mlp_finish(cp, m, upstream, late, stream):
        mine = slice(m * rows, (m + 1) * rows)
        grad, *early = norm_back(upstream, *standardize(stream), norm_rows(0)[0])
        sent[...] = (grad + f32_b[...]).astype(BF)
        f32_a[...] = sent[...].astype(F32)
        cp.store(f32_a, grads.at[mine])
        put_small(cp, m, early, late)

    def encode_mlp(m):
        cp, mine = Copies(sems), slice(m * rows, (m + 1) * rows)
        wides = [wide_panel(cp, p) for p in range(PANELS)]
        talls = [tall_panel(cp, p) for p in range(PANELS)]
        cp.store(message, kept.at[MLP["x"], mine])
        summed = mlp_forward(cp, m, True, wides, talls)
        f32_a[...] = summed
        cp.store(f32_a, kept32.at[mine])
        gain_1, shift_1 = norm_rows(1)
        sent[...] = (standardize(f32_a[...])[0] * gain_1 + shift_1).astype(BF)
        cp.store(sent, out.at[mine])
        cp.finish()

    def encode_mlp_back(m):
        cp, mine = Copies(sems), slice(m * rows, (m + 1) * rows)
        load_summed = cp.start(kept32.at[mine], f32_a)
        both = [(tall_panel(cp, p), cp.start(kept.at[MLP["gh"] + p, mine], panel(big_b, p))) for p in range(PANELS)]
        wides = [wide_panel(cp, p) for p in range(PANELS)]
        load_stream = cp.start(kept.at[MLP["x"], mine], one.at[0])
        load_summed.wait()
        upstream, late = mlp_backward(
            cp, m, message[...].astype(F32), f32_a[...], wides, [a for a, b in both], [b for a, b in both]
        )
        load_stream.wait()
        mlp_finish(cp, m, upstream, late, one[0].astype(F32))
        cp.finish()

    def decode_mlp(m):
        cp, mine = Copies(sems), slice(m * rows, (m + 1) * rows)
        wides = [wide_panel(cp, p) for p in range(PANELS)]
        talls = [tall_panel(cp, p) for p in range(PANELS)]
        load = cp.start(cotangent.at[mine], one.at[2])
        f32_a[...] = mlp_forward(cp, m, False, wides, talls)
        gain_1, shift_1 = norm_rows(1)
        one[3] = (standardize(f32_a[...])[0] * gain_1 + shift_1).astype(BF)
        cp.store(one.at[3], out.at[mine])
        load.wait()
        place = lax.broadcasted_iota(jnp.int32, (PREFIX, D), 0)
        for b in range(seqs):
            at = slice(b * PREFIX, (b + 1) * PREFIX)
            one[2, at, :] = jnp.where(place < lengths[m * seqs + b], one[2, at, :].astype(F32), 0.0).astype(BF)
        none = [None] * PANELS
        upstream, late = mlp_backward(cp, m, one[2].astype(F32), f32_a[...], none, none, none)
        mlp_finish(cp, m, upstream, late, message[...].astype(F32))
        cp.finish()

    def decode_early(m):
        cp, mine = Copies(sems), slice(m * rows, (m + 1) * rows)
        load = cp.start(text.at[mine], one.at[3])
        wides = [wide_panel(cp, p) for p in range(PANELS)]
        load_query = tall_panel(cp, 0)
        (gain_0, shift_0), (gain_1, shift_1) = norm_rows(0), norm_rows(1)
        load.wait()
        one[0] = (standardize(one[3].astype(F32))[0] * gain_0 + shift_0).astype(BF)
        cp.store(one.at[0], kept.at[DEC["u"], mine])
        for p in range(3):
            wides[p].wait()
            cols = slice(p * D, (p + 1) * D)
            big_b[:, cols] = nn(one[0], wide_v[:, cols]).astype(BF)
            cp.store(panel(big_b, p), kept.at[DEC["q"] + p, mine])
        attend(*(panel(big_b, p) for p in range(4)), one.at[1], lambda b: lengths[m * seqs + b])
        cp.store(panel(big_b, 3), kept.at[DEC["p"], mine])
        cp.store(one.at[1], kept.at[DEC["att"], mine])
        wides[3].wait()
        f32_a[...] = one[3].astype(F32) + nn(one[1], wide_v[:, 3 * D :])
        cp.store(f32_a, kept32.at[mine])
        one[2] = (standardize(f32_a[...])[0] * gain_1 + shift_1).astype(BF)
        cp.store(one.at[2], kept.at[DEC["c"], mine])
        load_query.wait()
        big_c[:, :D] = nn(one[2], tall_v[:D, :]).astype(BF)
        cp.store(panel(big_c, 0), kept.at[DEC["qc"], mine])
        cp.finish()

    def decode_cross(m):
        cp, mine = Copies(sems), slice(m * rows, (m + 1) * rows)
        talls = [tall_panel(cp, p) for p in (1, 2, 3)]
        load_query = cp.start(kept.at[DEC["qc"], mine], panel(big_a, 0))
        load_middle = cp.start(kept32.at[mine], f32_a)
        cp.store(message, kept.at[DEC["mem"], mine])
        for p in (1, 2):
            talls[p - 1].wait()
            cols = slice(p * D, (p + 1) * D)
            big_a[:, cols] = nn(message[...], tall_v[cols, :]).astype(BF)
            cp.store(panel(big_a, p), kept.at[DEC["kc"] + p - 1, mine])
        load_query.wait()
        attend(*(panel(big_a, p) for p in range(4)), one.at[1], None)
        cp.store(panel(big_a, 3), kept.at[DEC["pc"], mine])
        cp.store(one.at[1], kept.at[DEC["cross"], mine])
        talls[2].wait()
        load_middle.wait()
        sent[...] = (f32_a[...] + nn(one[1], tall_v[3 * D :, :])).astype(BF)
        cp.store(sent, out.at[mine])
        cp.finish()

    def decode_cross_back(m):
        cp, mine = Copies(sems), slice(m * rows, (m + 1) * rows)
        talls = [tall_panel(cp, p) for p in (3, 1, 2)]
        places = (DEC["qc"], DEC["kc"], DEC["vc"], DEC["pc"])
        loads = [cp.start(kept.at[place, mine], panel(big_b, p)) for p, place in enumerate(places)]
        cp.store(message, kept.at[DEC["gsec"], mine])
        talls[0].wait()
        one[0] = nt(message[...], tall_v[3 * D :, :]).astype(BF)
        for copy in loads:
            copy.wait()
        attend_back(*(panel(big_b, p) for p in range(4)), one.at[0], *(panel(big_a, p) for p in range(3)))
        for p in range(3):
            cp.store(panel(big_a, p), kept.at[places[p], mine])
        talls[1].wait()
        talls[2].wait()
        back = nt(big_a[:, D : 2 * D], tall_v[D : 2 * D, :]) + nt(big_a[:, 2 * D : 3 * D], tall_v[2 * D : 3 * D, :])
        sent[...] = back.astype(BF)
        cp.finish()

    def decode_late(m):
        cp, mine = Copies(sems), slice(m * rows, (m + 1) * rows)
        load_query = cp.start(kept.at[DEC["qc"], mine], one.at[0])
        tall_0 = tall_panel(cp, 0)
        load_middle = cp.start(kept32.at[mine], f32_a)
        load_second = cp.start(kept.at[DEC["gsec"], mine], one.at[1])
        wides = [wide_panel(cp, p) for p in (3, 0, 1, 2)]
        loads = [cp.start(kept.at[DEC["q"] + p, mine], panel(big_b, p)) for p in range(4)]
        load_text = cp.start(text.at[mine], one.at[3])
        for copy in (load_query, tall_0):
            copy.wait()
        upstream = nt(one[0], tall_v[:D, :])
        load_middle.wait()
        load_second.wait()
        grad, *late = norm_back(upstream, *standardize(f32_a[...]), norm_rows(1)[0])
        f32_b[...] = grad + one[1].astype(F32)
        one[2] = f32_b[...].astype(BF)
        cp.store(one.at[2], kept.at[DEC["gmid"], mine])
        wides[0].wait()
        one[0] = nt(one[2], wide_v[:, 3 * D :]).astype(BF)
        for copy in loads:
            copy.wait()
        attend_back(*(panel(big_b, p) for p in range(4)), one.at[0], *(panel(big_a, p) for p in range(3)))
        for p in range(3):
            cp.store(panel(big_a, p), kept.at[DEC["q"] + p, mine])
            wides[p + 1].wait()
        upstream = nt(big_a[:, : 3 * D], wide_v[:, : 3 * D])
        load_text.wait()
        grad, *early = norm_back(upstream, *standardize(one[3].astype(F32)), norm_rows(0)[0])
        f32_a[...] = grad + f32_b[...]
        cp.store(f32_a, grads.at[mine])
        put_small(cp, m, early, late)
        cp.finish()

    steps = dict(encode=encode, encode_back=encode_back, encode_mlp=encode_mlp, encode_mlp_back=encode_mlp_back,
                 decode_early=decode_early, decode_cross=decode_cross, decode_cross_back=decode_cross_back,
                 decode_late=decode_late, decode_mlp=decode_mlp)
    for at, todo in work.items():

        @pl.when(section == at)
        def _():
            for name, m in todo:
                steps[name](m)


def weight_operands(section):
    e, m, d = ENC, MLP, DEC
    left = (
        [e["u"]] * 3 + [e["att"]] + [-1] * 4,
        [m["u"]] * 4 + [m["a"] + p for p in range(4)],
        [d["u"]] * 3 + [d["att"], d["c"], d["mem"], d["mem"], d["cross"]],
    )
    right = (
        [e["q"], e["k"], e["v"], e["gfirst"]] + [e["gemb"]] * 4,
        [m["gh"] + p for p in range(4)] + [m["gb"]] * 4,
        [d["q"], d["k"], d["v"], d["gmid"], d["qc"], d["kc"], d["vc"], d["gsec"]],
    )
    which = jnp.array([0, 1, 2, 1], jnp.int32)[section]
    return jnp.array(left, jnp.int32)[which], jnp.array(right, jnp.int32)[which]


def weight_kernel(shards, left, right, kept, patches, out, left_v, right_v, done_v, load_sems, store_sems):
    parts = 2 * PANELS
    share = D // shards
    direct = share % 16 == 0

    def loads(i):
        slot = i % 2
        from_patches = left[i] < 0
        sources = (left_v.at[slot], right_v.at[slot])

        def begin():
            @pl.when(from_patches)
            def _():
                column = pl.multiple_of(jnp.maximum(i - PANELS, 0) * D, D)
                pltpu.make_async_copy(patches.at[:, pl.ds(column, D)], sources[0], load_sems.at[slot, 0]).start()

            @pl.when(jnp.logical_not(from_patches))
            def _():
                pltpu.make_async_copy(kept.at[jnp.maximum(left[i], 0)], sources[0], load_sems.at[slot, 0]).start()

            pltpu.make_async_copy(kept.at[right[i]], sources[1], load_sems.at[slot, 1]).start()

        def wait():
            pltpu.make_async_copy(kept.at[0], sources[0], load_sems.at[slot, 0]).wait()
            pltpu.make_async_copy(kept.at[0], sources[1], load_sems.at[slot, 1]).wait()

        return begin, wait

    def stores(i):
        slot = i % 2
        if not direct:
            return [pltpu.make_async_copy(done_v.at[slot], out.at[i], store_sems.at[slot, 0])]
        copies = []
        if i < PANELS:
            for d in range(shards):
                copies.append((done_v.at[slot, d * share : (d + 1) * share], out.at[d, i * share : (i + 1) * share]))
        else:
            block = PANELS * share
            for d in range(shards):
                first, last = d * block, (d + 1) * block
                low, high = max(first, (i - PANELS) * D), min(last, (i - PANELS + 1) * D)
                if low < high:
                    base = (i - PANELS) * D
                    copies.append((done_v.at[slot, low - base : high - base], out.at[d, block + low - first : block + high - first]))
        return [pltpu.make_async_copy(a, b, store_sems.at[slot, n]) for n, (a, b) in enumerate(copies)]

    loads(0)[0]()
    for i in range(parts):
        if i + 1 < parts:
            loads(i + 1)[0]()
        loads(i)[1]()
        if i >= 2:
            for copy in stores(i - 2):
                copy.wait()
        slot = i % 2
        done_v[slot] = tn(left_v[slot], right_v[slot]).astype(BF)
        for copy in stores(i):
            copy.start()
    for i in (parts - 2, parts - 1):
        for copy in stores(i):
            copy.wait()


def schedule():
    slots = []
    for k in range(MICRO + 12):
        work, sends = {}, {}
        plan = [(0, 0, "encode", 1), (1, 2, "encode_mlp", 1), (2, 4, "decode_cross", 1), (3, 6, "decode_mlp", -1),
                (2, 8, "decode_cross_back", -1), (1, 10, "encode_mlp_back", -1), (0, 12, "encode_back", 0),
                (2, 0, "decode_early", 0), (2, 12, "decode_late", 0)]
        for section, begin, name, way in plan:
            m = k - begin
            if 0 <= m < MICRO:
                work.setdefault(section, []).append((name, m))
                if way:
                    sends[section] = section + way
        slots.append((work, sorted(sends.items())))
    return slots


def on_device(patches, text, lengths, cotangent, wide, tall, gain, shift):
    total = patches.shape[0]
    rows = total // MICRO
    shards = lax.axis_size("dp")
    section = lax.axis_index("section")
    wide, tall, gain, shift = wide[0], tall[0], gain[0], shift[0]
    anywhere = pl.BlockSpec(memory_space=pl.ANY)
    in_vmem = pl.BlockSpec(memory_space=pltpu.VMEM)
    in_smem = pl.BlockSpec(memory_space=pltpu.SMEM)
    state_shapes = (
        jax.ShapeDtypeStruct((SLOTS, total, D), BF),
        jax.ShapeDtypeStruct((total, D), F32),
        jax.ShapeDtypeStruct((total, D), BF),
        jax.ShapeDtypeStruct((total, D), F32),
        jax.ShapeDtypeStruct((MICRO, 8, D), F32),
    )
    state = [jnp.zeros((8, 128), F32)] * 5
    messages = [jnp.zeros((rows, D), BF)] * 2
    for k, (work, sends) in enumerate(schedule()):
        results = pl.pallas_call(
            functools.partial(slot_kernel, work, rows),
            out_shape=(jax.ShapeDtypeStruct((rows, D), BF),) + state_shapes,
            in_specs=[in_smem] + [anywhere] * 5 + [in_vmem] * 3 + [anywhere] * 5,
            out_specs=[in_vmem] + [anywhere] * 5,
            input_output_aliases={9 + i: 1 + i for i in range(5)} if k else {},
            scratch_shapes=[
                pltpu.VMEM((D, FF), BF),
                pltpu.VMEM((FF, D), BF),
                pltpu.VMEM((rows, FF), BF),
                pltpu.VMEM((rows, FF), BF),
                pltpu.VMEM((rows, FF), BF),
                pltpu.VMEM((4, rows, D), BF),
                pltpu.VMEM((rows, D), F32),
                pltpu.VMEM((rows, D), F32),
                pltpu.VMEM((8, D), F32),
                pltpu.SemaphoreType.DMA((40,)),
            ],
            compiler_params=pltpu.CompilerParams(vmem_limit_bytes=VMEM_LIMIT, has_side_effects=True),
            name=f"slot_{k}",
        )(lengths, patches, text, cotangent, wide, tall, gain, shift, messages[-2], *state)
        state = results[1:]
        if sends:
            messages.append(lax.ppermute(results[0], "section", sends))
        else:
            messages.append(messages[-1])
    kept, kept32, out, grads, small = state

    share = D // shards
    direct = share % 16 == 0
    left, right = weight_operands(section)
    small_rows = 16
    deep = 2 * PANELS * share
    part_shape = (shards, deep + small_rows, D) if direct else (2 * PANELS, D, D)
    parts = pl.pallas_call(
        functools.partial(weight_kernel, shards),
        out_shape=jax.ShapeDtypeStruct(part_shape, BF),
        in_specs=[in_smem, in_smem, anywhere, anywhere],
        out_specs=anywhere,
        scratch_shapes=[
            pltpu.VMEM((2, total, D), BF),
            pltpu.VMEM((2, total, D), BF),
            pltpu.VMEM((2, D, D), BF),
            pltpu.SemaphoreType.DMA((2, 2)),
            pltpu.SemaphoreType.DMA((2, max(shards, 1))),
        ],
        compiler_params=pltpu.CompilerParams(vmem_limit_bytes=VMEM_LIMIT, has_side_effects=True),
        name="weights",
    )(left, right, kept, patches)
    little = jnp.sum(small, 0)
    high = little.astype(BF)
    low = (little - high.astype(F32)).astype(BF)
    little = jnp.concatenate([high, low], axis=0)
    if direct:
        parts = lax.dynamic_update_slice(parts, jnp.broadcast_to(little, (shards, small_rows, D)), (0, deep, 0))
        mine = lax.psum_scatter(parts, "dp", scatter_dimension=0, tiled=True)[0]
        wide_grad = mine[: PANELS * share].reshape(PANELS, share, D).transpose(1, 0, 2).reshape(share, FF)
        tall_grad = mine[PANELS * share : deep]
        little = mine[deep:]
    else:
        wide_part = parts[:PANELS].transpose(1, 0, 2).reshape(D, FF)
        wide_grad = lax.psum_scatter(wide_part, "dp", scatter_dimension=0, tiled=True)
        tall_grad = lax.psum_scatter(parts[PANELS:].reshape(FF, D), "dp", scatter_dimension=0, tiled=True)
        little = lax.psum(little, "dp")
    little = little[:4].astype(F32) + little[8:12].astype(F32)
    little = lax.dynamic_slice_in_dim(little, lax.axis_index("dp") * share, share, axis=1)
    return (
        out[None],
        grads[None],
        wide_grad.astype(F32)[None],
        tall_grad.astype(F32)[None],
        little[None, :2],
        little[None, 2:],
    )


def solution(mesh):
    return jax.shard_map(
        on_device,
        mesh=mesh,
        in_specs=(
            P("dp", None),
            P("dp", None),
            P("dp"),
            P("dp", None),
            P("section", None, None),
            P("section", None, None),
            P("section", None, None),
            P("section", None, None),
        ),
        out_specs=(
            P("section", "dp", None),
            P("section", "dp", None),
            P("section", "dp", None),
            P("section", "dp", None),
            P("section", None, "dp"),
            P("section", None, "dp"),
        ),
        check_vma=False,
    )
```

```python
import functools

import jax
import jax.numpy as jnp
from jax import lax
from jax.experimental import pallas as pl
from jax.experimental.pallas import tpu as pltpu
from jax.sharding import PartitionSpec as P

D = 768
HEADS = 12
FF = 3072
HEAD_DIM = 64
PREFIX = 64
PANELS = FF // D
GROUP = 4
LANES = GROUP * HEAD_DIM
GROUPS = HEADS // GROUP
EPS = 1e-05
NEG = -1e30
SCALE = HEAD_DIM ** (-0.5)
MICRO = 4
SLOTS = 15
VMEM_LIMIT = 24 * 1024 * 1024
FIRST_LIMIT = 38 * 1024 * 1024
WEIGHT_LIMIT = 32 * 1024 * 1024
BF = jnp.bfloat16
F32 = jnp.float32

SECTION, DP = "section", "dp"
ENCODE, ENCODE_MLP, CROSS, DECODE_MLP, CROSS_BACK, ENCODE_MLP_BACK, ENCODE_BACK, EARLY, LATE = range(9)


class Enc:
    u, q, k, v, p, att, gfirst, gemb, x = range(9)


class Mlp:
    u, x, gb, a, gh = 0, 1, 2, 3, 7


class Dec:
    u, q, k, v, p, att, c, qc, mem, kc, vc, pc, cross, gsec, gmid = range(15)


def nn(left, right):
    return lax.dot_general(left, right, (((1,), (0,)), ((), ())), preferred_element_type=F32)


def nt(left, right):
    return lax.dot_general(left, right, (((1,), (1,)), ((), ())), preferred_element_type=F32)


def tn(left, right):
    return lax.dot_general(left, right, (((0,), (0,)), ((), ())), preferred_element_type=F32)


def standardize(values):
    center = values - jnp.mean(values, -1, keepdims=True)
    rstd = lax.rsqrt(jnp.mean(center * center, -1, keepdims=True) + EPS)
    return center * rstd, rstd


def norm_back(upstream, unit, rstd, gain_row):
    scaled = upstream * gain_row
    mean_one = jnp.mean(scaled, -1, keepdims=True)
    mean_two = jnp.mean(scaled * unit, -1, keepdims=True)
    grad = rstd * (scaled - mean_one - unit * mean_two)
    return grad, jnp.sum(upstream * unit, 0, keepdims=True), jnp.sum(upstream, 0, keepdims=True)


def gelu_pair(hidden):
    c = 0.7978845608028654
    square = hidden * hidden
    t = jnp.tanh(hidden * (c + (c * 0.044715) * square))
    half = 0.5 + 0.5 * t
    active = hidden * half
    slope = half + active * (1.0 - t) * (c + (3.0 * c * 0.044715) * square)
    return active, slope


def block_diagonal(rows):
    tiled = jnp.concatenate([rows] * GROUP, axis=0)
    at_row = lax.broadcasted_iota(jnp.int32, tiled.shape, 0) // HEAD_DIM
    at_lane = lax.broadcasted_iota(jnp.int32, tiled.shape, 1) // HEAD_DIM
    return jnp.where(at_row == at_lane, tiled, jnp.zeros_like(tiled))


def head_rows(pairs):
    low = lax.broadcasted_iota(jnp.int32, (PREFIX, 2 * HEAD_DIM), 1) < HEAD_DIM
    return jnp.concatenate([jnp.where(low, p[:PREFIX], p[PREFIX:]) for p in pairs], axis=1)


def units(count):
    return [
        (slice(b * PREFIX, (b + 1) * PREFIX), slice(g * LANES, (g + 1) * LANES)) for b in range(count) for g in range(GROUPS)
    ]


def pair_product(left, right):
    return head_rows([tn(left[:, i : i + 128], right[:, i : i + 128]) for i in range(0, LANES, 128)])


def attend(count, q_ref, k_ref, v_ref, p_ref, out_ref, length_of):
    at = units(count)
    scores = [nt(k_ref[u], block_diagonal(q_ref[u])) * SCALE for u in at]
    if length_of is not None:
        key_at = lax.broadcasted_iota(jnp.int32, (PREFIX, LANES), 0)
        query_at = lax.broadcasted_iota(jnp.int32, (PREFIX, LANES), 1) % PREFIX
        allowed = [(key_at <= query_at) & (key_at < length_of(b)) for b in range(count)]
        scores = [jnp.where(allowed[i // GROUPS], values, NEG) for i, values in enumerate(scores)]
    probs = []
    for u, values in zip(at, scores):
        e = jnp.exp(values - jnp.max(values, 0, keepdims=True))
        probs.append((e * (1.0 / jnp.sum(e, 0, keepdims=True))).astype(BF))
        p_ref[u] = probs[-1]
    for u, p in zip(at, probs):
        out_ref[u] = pair_product(p, v_ref[u]).astype(BF)


def attend_back(count, q_ref, k_ref, v_ref, p_ref, up_ref, gq_ref, gk_ref, gv_ref):
    at = units(count)
    ups = [block_diagonal(up_ref[u]) for u in at]
    grads = [nt(v_ref[u], up) for u, up in zip(at, ups)]
    for u, up in zip(at, ups):
        gv_ref[u] = nn(p_ref[u], up).astype(BF)
    scores = []
    for u, grad in zip(at, grads):
        p = p_ref[u].astype(F32)
        scores.append((p * (grad - jnp.sum(grad * p, 0, keepdims=True))).astype(BF))
    for u, grad in zip(at, scores):
        gk_ref[u] = (nn(grad, block_diagonal(q_ref[u])) * SCALE).astype(BF)
    for u, grad in zip(at, scores):
        gq_ref[u] = (pair_product(grad, k_ref[u]) * SCALE).astype(BF)


class Copies:
    def __init__(self, sems):
        self.sems, self.used, self.stores = sems, 0, []

    def start(self, source, target):
        copy = pltpu.make_async_copy(source, target, self.sems.at[self.used])
        self.used += 1
        copy.start()
        return copy

    def store(self, source, target):
        self.stores.append(self.start(source, target))

    def finish(self):
        for copy in self.stores:
            copy.wait()
        self.stores = []


def slot_kernel(work, before, last, rows, present, *refs):
    taken = iter(refs)
    given = [next(taken) if here else None for here in present]
    lengths, patches, text, cotangent, wide, tall, gain, shift, message, done = given[:10]
    kept, kept32, out, grads, sent, small, wide_out, tall_out = given[14:]
    first = wide_out is not None
    big_a, big_b, big_c, one, f32_a, f32_b, f32_c, sems = taken
    section = lax.axis_index(SECTION)
    seqs = rows // PREFIX

    def panel(big, p):
        return big.at[:, p * D : (p + 1) * D]

    def norm_rows(at):
        return gain[at : at + 1, :], shift[at : at + 1, :]

    def put_small(early, late):
        for i, row in enumerate((early[0], late[0], early[1], late[1])):
            small[i : i + 1, :] = small[i : i + 1, :] + row

    def finish_before(cp, name, m):
        mine = slice(m * rows, (m + 1) * rows)
        if name in (ENCODE, ENCODE_MLP, CROSS):
            cp.store(done, out.at[mine])
        if name in (DECODE_MLP, ENCODE_MLP_BACK, ENCODE_BACK):
            if name == ENCODE_BACK:
                cp.store(done, kept.at[Enc.gemb, mine])
            f32_c[...] = done[...].astype(F32)
            cp.store(f32_c, grads.at[mine])

    def encode(cp, m, loads=None):
        mine = slice(m * rows, (m + 1) * rows)
        (gain_0, shift_0), (gain_1, shift_1) = norm_rows(0), norm_rows(1)
        if first:
            for p in range(PANELS):
                cols = slice(p * D, (p + 1) * D)
                for copy in loads[p]:
                    copy.wait()
                part = nn(big_a[:, cols], tall[cols, :])
                f32_a[...] = part if p == 0 else f32_a[...] + part
            for p in range(PANELS):
                cp.store(panel(big_a, p), kept.at[Enc.x + p, mine])
            for copy in loads[PANELS]:
                copy.wait()
        else:
            load = cp.start(patches.at[mine], big_a)
            load.wait()
            for p in range(PANELS):
                cp.store(panel(big_a, p), kept.at[Enc.x + p, mine])
            f32_a[...] = nn(big_a[...], tall[...])
        cp.store(f32_a, kept32.at[mine])
        stream = standardize(f32_a[...])[0] * gain_0 + shift_0
        f32_b[...] = stream
        one[0] = (standardize(stream)[0] * gain_1 + shift_1).astype(BF)
        cp.store(one.at[0], kept.at[Enc.u, mine])
        for p in range(3):
            cols = slice(p * D, (p + 1) * D)
            big_b[:, cols] = nn(one[0], wide[:, cols]).astype(BF)
            cp.store(panel(big_b, p), kept.at[Enc.q + p, mine])
        attend(seqs, *(panel(big_b, p) for p in range(4)), one.at[1], None)
        cp.store(panel(big_b, 3), kept.at[Enc.p, mine])
        cp.store(one.at[1], kept.at[Enc.att, mine])
        sent[...] = (f32_b[...] + nn(one[1], wide[:, 3 * D :])).astype(BF)

    def encode_back(cp, m):
        mine = slice(m * rows, (m + 1) * rows)
        loads = [cp.start(kept.at[Enc.q + p, mine], panel(big_b, p)) for p in range(4)]
        load_embedded = cp.start(kept32.at[mine], f32_a)
        cp.store(message, kept.at[Enc.gfirst, mine])
        (gain_0, shift_0), (gain_1, shift_1) = norm_rows(0), norm_rows(1)
        one[0] = nt(message[...], wide[:, 3 * D :]).astype(BF)
        load_embedded.wait()
        for copy in loads:
            copy.wait()
        unit_0, rstd_0 = standardize(f32_a[...])
        f32_a[...] = unit_0
        unit_1, rstd_1 = standardize(unit_0 * gain_0 + shift_0)
        f32_b[...] = unit_1
        attend_back(seqs, *(panel(big_b, p) for p in range(4)), one.at[0], *(panel(big_a, p) for p in range(3)))
        for p in range(3):
            cp.store(panel(big_a, p), kept.at[Enc.q + p, mine])
        upstream = nt(big_a[:, : 3 * D], wide[:, : 3 * D])
        grad, *late = norm_back(upstream, f32_b[...], rstd_1, gain_1)
        grad, *early = norm_back(grad + message[...].astype(F32), f32_a[...], rstd_0, gain_0)
        sent[...] = grad.astype(BF)
        put_small(early, late)
        if last:
            cp.store(sent, kept.at[Enc.gemb, mine])
            f32_b[...] = sent[...].astype(F32)
            cp.store(f32_b, grads.at[mine])

    def mlp_forward(cp, mine, keep):
        gain_0, shift_0 = norm_rows(0)
        unit, rstd = standardize(message[...].astype(F32))
        if not keep:
            f32_b[...] = unit
        one[0] = (unit * gain_0 + shift_0).astype(BF)
        cp.store(one.at[0], kept.at[Mlp.u, mine])
        for p in range(PANELS):
            cols = slice(p * D, (p + 1) * D)
            active, slope = gelu_pair(nn(one[0], wide[:, cols]))
            big_a[:, cols] = active.astype(BF)
            big_b[:, cols] = slope.astype(BF)
            cp.store(panel(big_a, p), kept.at[Mlp.a + p, mine])
            if keep:
                cp.store(panel(big_b, p), kept.at[Mlp.gh + p, mine])
        return message[...].astype(F32) + nn(big_a[...], tall[...]), rstd

    def mlp_backward(cp, mine, upstream, unit, rstd, loads):
        grad, *late = norm_back(upstream, unit, rstd, norm_rows(1)[0])
        f32_a[...] = grad
        one[1] = grad.astype(BF)
        cp.store(one.at[1], kept.at[Mlp.gb, mine])
        for copy in loads:
            copy.wait()
        for p in range(PANELS):
            cols = slice(p * D, (p + 1) * D)
            back = nt(one[1], tall[cols, :])
            big_c[:, cols] = (back * big_b[:, cols].astype(F32)).astype(BF)
            cp.store(panel(big_c, p), kept.at[Mlp.gh + p, mine])
        return nt(big_c[...], wide[...]), late

    def encode_mlp(cp, m):
        mine = slice(m * rows, (m + 1) * rows)
        cp.store(message, kept.at[Mlp.x, mine])
        summed, _ = mlp_forward(cp, mine, True)
        f32_a[...] = summed
        cp.store(f32_a, kept32.at[mine])
        gain_1, shift_1 = norm_rows(1)
        sent[...] = (standardize(f32_a[...])[0] * gain_1 + shift_1).astype(BF)

    def encode_mlp_back(cp, m):
        mine = slice(m * rows, (m + 1) * rows)
        load_summed = cp.start(kept32.at[mine], f32_a)
        loads = [cp.start(kept.at[Mlp.gh + p, mine], panel(big_b, p)) for p in range(PANELS)]
        loads.append(cp.start(kept.at[Mlp.x, mine], one.at[0]))
        load_summed.wait()
        unit, rstd = standardize(f32_a[...])
        upstream, late = mlp_backward(cp, mine, message[...].astype(F32), unit, rstd, loads)
        unit, rstd = standardize(one[0].astype(F32))
        grad, *early = norm_back(upstream, unit, rstd, norm_rows(0)[0])
        sent[...] = (grad + f32_a[...]).astype(BF)
        put_small(early, late)

    def decode_mlp(cp, m):
        mine = slice(m * rows, (m + 1) * rows)
        load = cp.start(cotangent.at[mine], one.at[2])
        summed, rstd_0 = mlp_forward(cp, mine, False)
        gain_1, shift_1 = norm_rows(1)
        unit, rstd = standardize(summed)
        one[3] = (unit * gain_1 + shift_1).astype(BF)
        cp.store(one.at[3], out.at[mine])
        load.wait()
        place = lax.broadcasted_iota(jnp.int32, (PREFIX, D), 0)
        masked = []
        for b in range(seqs):
            at = slice(b * PREFIX, (b + 1) * PREFIX)
            masked.append(jnp.where(place < lengths[m * seqs + b], one[2, at, :].astype(F32), 0.0))
        upstream, late = mlp_backward(cp, mine, jnp.concatenate(masked, axis=0), unit, rstd, [])
        grad, *early = norm_back(upstream, f32_b[...], rstd_0, norm_rows(0)[0])
        sent[...] = (grad + f32_a[...]).astype(BF)
        put_small(early, late)

    def decode_early(cp, m):
        if m == MICRO - 2:
            decode_early_one(cp, m)
            cp.finish()
            m += 1
        decode_early_one(cp, m)

    def decode_early_one(cp, m):
        mine = slice(m * rows, (m + 1) * rows)
        load = cp.start(text.at[mine], one.at[3])
        (gain_0, shift_0), (gain_1, shift_1) = norm_rows(0), norm_rows(1)
        load.wait()
        one[0] = (standardize(one[3].astype(F32))[0] * gain_0 + shift_0).astype(BF)
        cp.store(one.at[0], kept.at[Dec.u, mine])
        for p in range(3):
            cols = slice(p * D, (p + 1) * D)
            big_b[:, cols] = nn(one[0], wide[:, cols]).astype(BF)
            cp.store(panel(big_b, p), kept.at[Dec.q + p, mine])
        attend(seqs, *(panel(big_b, p) for p in range(4)), one.at[1], lambda b: lengths[m * seqs + b])
        cp.store(panel(big_b, 3), kept.at[Dec.p, mine])
        cp.store(one.at[1], kept.at[Dec.att, mine])
        f32_a[...] = one[3].astype(F32) + nn(one[1], wide[:, 3 * D :])
        cp.store(f32_a, kept32.at[mine])
        one[2] = (standardize(f32_a[...])[0] * gain_1 + shift_1).astype(BF)
        cp.store(one.at[2], kept.at[Dec.c, mine])
        big_c[:, :D] = nn(one[2], tall[:D, :]).astype(BF)
        cp.store(panel(big_c, 0), kept.at[Dec.qc, mine])

    def decode_cross(cp, m):
        mine = slice(m * rows, (m + 1) * rows)
        load_query = cp.start(kept.at[Dec.qc, mine], panel(big_a, 0))
        load_middle = cp.start(kept32.at[mine], f32_a)
        cp.store(message, kept.at[Dec.mem, mine])
        for p in (1, 2):
            cols = slice(p * D, (p + 1) * D)
            big_a[:, cols] = nn(message[...], tall[cols, :]).astype(BF)
            cp.store(panel(big_a, p), kept.at[Dec.kc + p - 1, mine])
        load_query.wait()
        attend(seqs, *(panel(big_a, p) for p in range(4)), one.at[1], None)
        cp.store(panel(big_a, 3), kept.at[Dec.pc, mine])
        cp.store(one.at[1], kept.at[Dec.cross, mine])
        load_middle.wait()
        sent[...] = (f32_a[...] + nn(one[1], tall[3 * D :, :])).astype(BF)

    def decode_cross_back(cp, m):
        mine = slice(m * rows, (m + 1) * rows)
        places = (Dec.qc, Dec.kc, Dec.vc, Dec.pc)
        loads = [cp.start(kept.at[place, mine], panel(big_b, p)) for p, place in enumerate(places)]
        cp.store(message, kept.at[Dec.gsec, mine])
        one[0] = nt(message[...], tall[3 * D :, :]).astype(BF)
        for copy in loads:
            copy.wait()
        attend_back(seqs, *(panel(big_b, p) for p in range(4)), one.at[0], *(panel(big_c, p) for p in range(3)))
        for p in range(3):
            cp.store(panel(big_c, p), kept.at[places[p], mine])
        back = nt(big_c[:, D : 2 * D], tall[D : 2 * D, :]) + nt(big_c[:, 2 * D : 3 * D], tall[2 * D : 3 * D, :])
        sent[...] = back.astype(BF)

    def decode_late(cp, m):
        mine = slice(m * rows, (m + 1) * rows)
        load_query = cp.start(kept.at[Dec.qc, mine], one.at[0])
        load_middle = cp.start(kept32.at[mine], f32_a)
        load_second = cp.start(kept.at[Dec.gsec, mine], one.at[1])
        loads = [cp.start(kept.at[Dec.q + p, mine], panel(big_b, p)) for p in range(4)]
        load_text = cp.start(text.at[mine], one.at[3])
        load_query.wait()
        upstream = nt(one[0], tall[:D, :])
        load_middle.wait()
        load_second.wait()
        grad, *late = norm_back(upstream, *standardize(f32_a[...]), norm_rows(1)[0])
        f32_b[...] = grad + one[1].astype(F32)
        one[2] = f32_b[...].astype(BF)
        cp.store(one.at[2], kept.at[Dec.gmid, mine])
        one[0] = nt(one[2], wide[:, 3 * D :]).astype(BF)
        for copy in loads:
            copy.wait()
        attend_back(seqs, *(panel(big_b, p) for p in range(4)), one.at[0], *(panel(big_a, p) for p in range(3)))
        for p in range(3):
            cp.store(panel(big_a, p), kept.at[Dec.q + p, mine])
        upstream = nt(big_a[:, : 3 * D], wide[:, : 3 * D])
        load_text.wait()
        grad, *early = norm_back(upstream, *standardize(one[3].astype(F32)), norm_rows(0)[0])
        f32_a[...] = grad + f32_b[...]
        cp.store(f32_a, grads.at[mine])
        put_small(early, late)

    steps = {
        ENCODE: encode, ENCODE_MLP: encode_mlp, CROSS: decode_cross, DECODE_MLP: decode_mlp, CROSS_BACK: decode_cross_back,
        ENCODE_MLP_BACK: encode_mlp_back, ENCODE_BACK: encode_back, EARLY: decode_early, LATE: decode_late,
    }
    if small is not None:
        small[...] = jnp.zeros_like(small)
    if first:
        wide_in, tall_in, wide, tall = wide, tall, wide_out, tall_out

        def weight_loads(cp):
            for p in range(PANELS):
                at = slice(p * D, (p + 1) * D)
                yield [cp.start(tall_in.at[at], tall.at[at])]
            yield [cp.start(wide_in.at[:, p * D : (p + 1) * D], wide.at[:, p * D : (p + 1) * D]) for p in range(PANELS)]

        @pl.when(section == 0)
        def _():
            cp = Copies(sems)
            loads = [[cp.start(patches.at[:rows, p * D : (p + 1) * D], panel(big_a, p))] for p in range(PANELS)]
            loads.append([])
            for mine, more in zip(loads, weight_loads(cp)):
                mine.extend(more)
            encode(cp, 0, loads)
            cp.finish()

        @pl.when(section != 0)
        def _():
            for loads in list(weight_loads(Copies(sems))):
                for copy in loads:
                    copy.wait()

        return
    for at in sorted(set(work) | set(before)):

        @pl.when(section == at)
        def _():
            cp = Copies(sems)
            if at in before:
                finish_before(cp, *before[at])
            if at in work:
                name, m = work[at]
                steps[name](cp, m)
            cp.finish()


def weight_operands():
    e, m, d = Enc, Mlp, Dec
    mlp = ([m.u] * 4 + [m.a + p for p in range(4)], [m.gh + p for p in range(4)] + [m.gb] * 4)
    encode = ([e.u] * 3 + [e.att] + [e.x + p for p in range(4)], [e.q, e.k, e.v, e.gfirst] + [e.gemb] * 4)
    decode = ([d.u] * 3 + [d.att, d.c, d.mem, d.mem, d.cross], [d.q, d.k, d.v, d.gmid, d.qc, d.kc, d.vc, d.gsec])
    return encode, mlp, decode, mlp


def by_section(values):
    section, chosen = lax.axis_index(SECTION), values[0]
    for at, value in enumerate(values[1:], 1):
        if value != values[0]:
            chosen = jnp.where(section == at, value, chosen)
    return chosen


def weight_kernel(tall_half, shards, *refs):
    refs = list(refs)
    kept = refs.pop(0)
    extra = refs.pop(0) if tall_half else None
    keep = refs.pop(0)
    give = [refs.pop(0) for _ in range(shards // 2)]
    left_v, right_v, sems = refs
    section, core = lax.axis_index(SECTION), lax.axis_index(DP) % 2
    base = PANELS if tall_half else 0
    lefts = [[t[0][base + p] for t in weight_operands()] for p in range(PANELS)]
    rights = [[t[1][base + p] for t in weight_operands()] for p in range(PANELS)]
    alone = (section == 2) if tall_half else (section % 2 == 0)
    chips, share = shards // 2, (FF if tall_half else D) // shards

    def left(p, begin):
        copy = pltpu.make_async_copy(kept.at[by_section(lefts[p])], left_v.at[p], sems.at[0, p])
        copy.start() if begin else copy.wait()

    def right(p, begin):
        copy = pltpu.make_async_copy(kept.at[by_section(rights[p])], right_v.at[p], sems.at[1, p])
        copy.start() if begin else copy.wait()

    def operands(p, begin):
        if tall_half:
            left(p, begin)
            right(p, begin) if p == 0 else pl.when(alone)(lambda: right(p, begin))
        else:
            right(p, begin)
            if p == 0:
                left(p, begin)
            elif p == PANELS - 1:
                pl.when(alone)(lambda: left(p, begin))

    chip = lax.axis_index(DP) // 2

    def put(at, rows, blocks):
        mine = jnp.where(core == 0, blocks[0], blocks[1])
        theirs = jnp.where(core == 0, blocks[1], blocks[0])
        keep[(chip - at + chips - 1) % chips, rows] = mine
        for here in range(chips):

            @pl.when(chip == here)
            def _():
                give[(here - at + chips - 1) % chips][rows] = theirs

    for p in range(PANELS):
        operands(p, True)
    for p in range(PANELS):
        operands(p, False)
        from_left = p if tall_half else (jnp.where(alone, p, 0) if p == PANELS - 1 else 0)
        from_right = p if not tall_half else (jnp.where(alone, p, 0) if p else 0)
        done = tn(left_v[from_left], right_v[from_right]).astype(BF)
        if not tall_half:
            done = done.reshape(chips, 2, share, D)
            for at in range(chips):
                put(at, slice(p * share, (p + 1) * share), done[at])
        else:
            done = done.reshape(D // share // 2, 2, share, D)
            for n in range(D // share // 2):
                put(p * (D // share // 2) + n, slice(0, share), done[n])
    if extra is not None:
        for at in range(chips):
            keep[at, share:] = extra[...]
            give[at][share:] = extra[...]


def weight_half(tall_half, shards, kept, extra):
    total = kept.shape[1]
    rows = FF // shards + (extra.shape[0] if tall_half else 0)
    in_vmem = pl.BlockSpec(memory_space=pltpu.VMEM)
    shapes = [jax.ShapeDtypeStruct((shards // 2, rows, D), BF)] + [jax.ShapeDtypeStruct((rows, D), BF)] * (shards // 2)
    flops = 2 * PANELS * D * D * total
    results = pl.pallas_call(
        functools.partial(weight_kernel, tall_half, shards),
        out_shape=tuple(shapes),
        in_specs=[pl.BlockSpec(memory_space=pl.ANY)] + [in_vmem] * tall_half,
        out_specs=(in_vmem,) * len(shapes),
        scratch_shapes=[
            pltpu.VMEM((PANELS, total, D), BF),
            pltpu.VMEM((PANELS, total, D), BF),
            pltpu.SemaphoreType.DMA((2, PANELS)),
        ],
        cost_estimate=pl.CostEstimate(flops=flops, bytes_accessed=flops // total, transcendentals=0),
        compiler_params=pltpu.CompilerParams(vmem_limit_bytes=WEIGHT_LIMIT, has_side_effects=True),
        name="weights",
    )(kept, *([extra] * tall_half))
    return results


def after(value, other):
    return lax.optimization_barrier((value, other))[0]


def ring_scatter(kept, little, shards):
    chips, rows = shards // 2, FF // shards
    flip = [(d, d ^ 1) for d in range(shards)]
    onward = [(d, (d + 2) % shards) for d in range(shards)]
    sent = None

    def exchange(keep, *give):
        return [(keep[at], lax.ppermute(part, DP, flip)) for at, part in enumerate(give)]

    def add(parts, running):
        keep, got = parts
        if sent is not None and running is None:
            got = after(got, sent)
        elif sent is not None:
            running = after(running, sent)
        value = keep.astype(F32) + got.astype(F32)
        return value if running is None else value + running.astype(F32)

    def send(value):
        nonlocal sent
        sent = value.astype(BF)
        return lax.ppermute(sent, DP, onward)

    wide = exchange(*weight_half(False, shards, kept, None))
    running = send(add(wide[0], None))
    tall = exchange(*weight_half(True, shards, after(kept, sent), little))
    pieces = [slice(0, 256), slice(256, rows + little.shape[0])]
    running = send(add(wide[1], running))
    low = send(add(tall[0], None))
    low = [low[piece] for piece in pieces]
    for step in range(1, chips - 1):
        if step + 1 < chips - 1:
            running = send(add(wide[step + 1], running))
        low = [send(add([part[piece] for part in tall[step]], got)) for piece, got in zip(pieces, low)]
    wide = add(wide[-1], running)
    return [wide] + [add([part[piece] for part in tall[-1]], got) for piece, got in zip(pieces, low)]


def weight_part(i, kept):
    lefts, rights = ([t[side][i] for t in weight_operands()] for side in (0, 1))
    left, right = (lax.dynamic_index_in_dim(kept, by_section(values), 0, keepdims=False) for values in (lefts, rights))
    return tn(left, right).astype(BF)


def schedule():
    plan = [(0, 0, ENCODE, 1), (1, 2, ENCODE_MLP, 1), (2, 4, CROSS, 1), (3, 6, DECODE_MLP, -1), (2, 8, CROSS_BACK, -1),
            (1, 10, ENCODE_MLP_BACK, -1), (0, 12, ENCODE_BACK, 0), (2, 1, EARLY, 0), (2, 12, LATE, 0)]
    slots = []
    for k in range(MICRO + 12):
        work, sends = {}, []
        for section, begin, name, way in plan:
            if 0 <= k - begin < MICRO - (name == EARLY):
                assert section not in work
                work[section] = (name, k - begin)
                if way:
                    sends.append((section, section + way))
        slots.append((work, sends))
    return slots


def on_device(patches, text, lengths, cotangent, wide, tall, gain, shift):
    total = patches.shape[0]
    rows = total // MICRO
    shards = lax.axis_size(DP)
    wide, tall, gain, shift = wide[0], tall[0], gain[0], shift[0]
    anywhere = pl.BlockSpec(memory_space=pl.ANY)
    in_vmem = pl.BlockSpec(memory_space=pltpu.VMEM)
    in_smem = pl.BlockSpec(memory_space=pltpu.SMEM)
    specs = [in_smem] + [anywhere] * 3 + [in_vmem] * 6 + [anywhere] * 8 + [in_vmem] * 4
    shapes = [
        jax.ShapeDtypeStruct((SLOTS, total, D), BF),
        jax.ShapeDtypeStruct((total, D), F32),
        jax.ShapeDtypeStruct((total, D), BF),
        jax.ShapeDtypeStruct((total, D), F32),
        jax.ShapeDtypeStruct((rows, D), BF),
        jax.ShapeDtypeStruct((8, D), F32),
        jax.ShapeDtypeStruct(wide.shape, BF),
        jax.ShapeDtypeStruct(tall.shape, BF),
    ]
    state, messages, smalls, done, before = [None] * 4, [None, None], [], None, {}
    slots = schedule()
    for k, (work, sends) in enumerate(slots):
        now, old = {name for name, _ in work.values()}, {name for name, _ in before.values()}

        def given(value, *names):
            return value if now & set(names) else None

        operands = [
            given(lengths, EARLY, DECODE_MLP),
            given(patches, ENCODE),
            given(text, EARLY, LATE),
            given(cotangent, DECODE_MLP),
            wide, tall, gain, shift,
            given(messages[-2], ENCODE_MLP, CROSS, DECODE_MLP, CROSS_BACK, ENCODE_MLP_BACK, ENCODE_BACK),
            done if old - {EARLY, LATE} else None,
            *state,
        ]
        results = [True] * 4 + [bool(now - {EARLY, LATE}), bool(now & {DECODE_MLP, ENCODE_MLP_BACK, ENCODE_BACK, LATE})]
        results += [k == 0] * 2
        present = tuple(value is not None for value in operands) + tuple(results)
        places = [i for i, value in enumerate(operands) if value is not None]
        values = pl.pallas_call(
            functools.partial(slot_kernel, work, before, k + 1 == len(slots), rows, present),
            out_shape=tuple(shape for shape, here in zip(shapes, results) if here),
            in_specs=[anywhere if k == 0 and i in (4, 5) else specs[i] for i in places],
            out_specs=[spec for spec, here in zip(specs[14:], results) if here],
            input_output_aliases={places.index(10 + i): i for i in range(4)} if k else {},
            scratch_shapes=[
                pltpu.VMEM((rows, FF), BF),
                pltpu.VMEM((rows, FF), BF),
                pltpu.VMEM((rows, FF), BF),
                pltpu.VMEM((4, rows, D), BF),
                pltpu.VMEM((rows, D), F32),
                pltpu.VMEM((rows, D), F32),
                pltpu.VMEM((rows, D), F32),
                pltpu.SemaphoreType.DMA((48,)),
            ],
            compiler_params=pltpu.CompilerParams(vmem_limit_bytes=VMEM_LIMIT if k else FIRST_LIMIT, has_side_effects=True),
            cost_estimate=pl.CostEstimate(flops=9_000_000_000, bytes_accessed=4_000_000, transcendentals=0),
            name=f"slot_{k}",
        )(*(operands[i] for i in places))
        state, rest = list(values[:4]), list(values[4:])
        done = rest.pop(0) if results[4] else None
        if results[5]:
            smalls.append(rest.pop(0))
        if k == 0:
            wide, tall = rest
        messages.append(lax.ppermute(done, SECTION, sends) if sends else None)
        before = work
    kept, _, out, grads = state

    share = D // shards
    little = sum(smalls)
    high = little.astype(BF)
    little = jnp.concatenate([high, (little - high.astype(F32)).astype(BF)], axis=0)
    if share % 16 == 0 and shards % 2 == 0 and D % (2 * FF // shards) == 0:
        mine, low, high = ring_scatter(kept, little, shards)
        wide_grad = jnp.concatenate([mine[p * share : (p + 1) * share] for p in range(PANELS)], axis=1)
        tall_grad = jnp.concatenate([low, high[:-16]], axis=0)
        little = high[-16:]
    else:
        parts = [weight_part(i, kept) for i in range(2 * PANELS)]
        wide_grad = lax.psum_scatter(jnp.concatenate(parts[:PANELS], axis=1), DP, scatter_dimension=0, tiled=True)
        tall_grad = lax.psum_scatter(jnp.concatenate(parts[PANELS:], axis=0), DP, scatter_dimension=0, tiled=True)
        little = lax.psum(little, DP)
    little = little[:4].astype(F32) + little[8:12].astype(F32)
    little = lax.dynamic_slice_in_dim(little, lax.axis_index(DP) * share, share, axis=1)
    return (
        out[None],
        grads[None],
        wide_grad.astype(F32)[None],
        tall_grad.astype(F32)[None],
        little[None, :2],
        little[None, 2:],
    )


def solution(mesh):
    return jax.shard_map(
        on_device,
        mesh=mesh,
        in_specs=(
            P(DP, None),
            P(DP, None),
            P(DP),
            P(DP, None),
            P(SECTION, None, None),
            P(SECTION, None, None),
            P(SECTION, None, None),
            P(SECTION, None, None),
        ),
        out_specs=(
            P(SECTION, DP, None),
            P(SECTION, DP, None),
            P(SECTION, DP, None),
            P(SECTION, DP, None),
            P(SECTION, None, DP),
            P(SECTION, None, DP),
        ),
        check_vma=False,
    )
```

```python
import functools

import jax
import jax.numpy as jnp
from jax import lax
from jax.experimental import pallas as pl
from jax.experimental.pallas import tpu as pltpu
from jax.sharding import PartitionSpec as P

D = 768
HEADS = 12
FF = 3072
HEAD_DIM = 64
PREFIX = 64
PANELS = FF // D
GROUP = 4
LANES = GROUP * HEAD_DIM
GROUPS = HEADS // GROUP
EPS = 1e-05
NEG = -1e30
SCALE = HEAD_DIM ** (-0.5)
MICRO = 4
SLOTS = 15
VMEM_LIMIT = 24 * 1024 * 1024
FIRST_LIMIT = 38 * 1024 * 1024
LAST_LIMIT = 27 * 1024 * 1024
WEIGHT_LIMIT = 32 * 1024 * 1024
BF = jnp.bfloat16
F32 = jnp.float32

SECTION, DP = "section", "dp"
ENCODE, ENCODE_MLP, CROSS, DECODE_MLP, CROSS_BACK, ENCODE_MLP_BACK, ENCODE_BACK, EARLY, LATE = range(9)


class Enc:
    u, q, k, v, p, att, gfirst, gemb, x = range(9)


class Mlp:
    u, x, gb, a, gh = 0, 1, 2, 3, 7


class Dec:
    u, q, k, v, p, att, c, qc, mem, kc, vc, pc, cross, gsec, gmid = range(15)


def nn(left, right):
    return lax.dot_general(left, right, (((1,), (0,)), ((), ())), preferred_element_type=F32)


def nt(left, right):
    return lax.dot_general(left, right, (((1,), (1,)), ((), ())), preferred_element_type=F32)


def tn(left, right):
    return lax.dot_general(left, right, (((0,), (0,)), ((), ())), preferred_element_type=F32)


def standardize(values):
    center = values - jnp.mean(values, -1, keepdims=True)
    rstd = lax.rsqrt(jnp.mean(center * center, -1, keepdims=True) + EPS)
    return center * rstd, rstd


def norm_back(upstream, unit, rstd, gain_row):
    scaled = upstream * gain_row
    mean_one = jnp.mean(scaled, -1, keepdims=True)
    mean_two = jnp.mean(scaled * unit, -1, keepdims=True)
    grad = rstd * (scaled - mean_one - unit * mean_two)
    return grad, jnp.sum(upstream * unit, 0, keepdims=True), jnp.sum(upstream, 0, keepdims=True)


def gelu_pair(hidden):
    c = 0.7978845608028654
    square = hidden * hidden
    t = jnp.tanh(hidden * (c + (c * 0.044715) * square))
    half = 0.5 + 0.5 * t
    active = hidden * half
    slope = half + active * (1.0 - t) * (c + (3.0 * c * 0.044715) * square)
    return active, slope


def block_diagonal(rows):
    tiled = jnp.concatenate([rows] * GROUP, axis=0)
    at_row = lax.broadcasted_iota(jnp.int32, tiled.shape, 0) // HEAD_DIM
    at_lane = lax.broadcasted_iota(jnp.int32, tiled.shape, 1) // HEAD_DIM
    return jnp.where(at_row == at_lane, tiled, jnp.zeros_like(tiled))


def head_rows(pairs):
    low = lax.broadcasted_iota(jnp.int32, (PREFIX, 2 * HEAD_DIM), 1) < HEAD_DIM
    return jnp.concatenate([jnp.where(low, p[:PREFIX], p[PREFIX:]) for p in pairs], axis=1)


def units(count):
    return [
        (slice(b * PREFIX, (b + 1) * PREFIX), slice(g * LANES, (g + 1) * LANES)) for b in range(count) for g in range(GROUPS)
    ]


def pair_product(left, right):
    return head_rows([tn(left[:, i : i + 128], right[:, i : i + 128]) for i in range(0, LANES, 128)])


def attend(count, q_ref, k_ref, v_ref, p_ref, out_ref, length_of):
    at = units(count)
    scores = [nt(k_ref[u], block_diagonal(q_ref[u])) * SCALE for u in at]
    if length_of is not None:
        key_at = lax.broadcasted_iota(jnp.int32, (PREFIX, LANES), 0)
        query_at = lax.broadcasted_iota(jnp.int32, (PREFIX, LANES), 1) % PREFIX
        allowed = [(key_at <= query_at) & (key_at < length_of(b)) for b in range(count)]
        scores = [jnp.where(allowed[i // GROUPS], values, NEG) for i, values in enumerate(scores)]
    probs = []
    for u, values in zip(at, scores):
        e = jnp.exp(values - jnp.max(values, 0, keepdims=True))
        probs.append((e * (1.0 / jnp.sum(e, 0, keepdims=True))).astype(BF))
        p_ref[u] = probs[-1]
    for u, p in zip(at, probs):
        out_ref[u] = pair_product(p, v_ref[u]).astype(BF)


def attend_back(count, q_ref, k_ref, v_ref, p_ref, up_ref, gq_ref, gk_ref, gv_ref):
    at = units(count)
    ups = [block_diagonal(up_ref[u]) for u in at]
    grads = [nt(v_ref[u], up) for u, up in zip(at, ups)]
    for u, up in zip(at, ups):
        gv_ref[u] = nn(p_ref[u], up).astype(BF)
    scores = []
    for u, grad in zip(at, grads):
        p = p_ref[u].astype(F32)
        scores.append((p * (grad - jnp.sum(grad * p, 0, keepdims=True))).astype(BF))
    for u, grad in zip(at, scores):
        gk_ref[u] = (nn(grad, block_diagonal(q_ref[u])) * SCALE).astype(BF)
    for u, grad in zip(at, scores):
        gq_ref[u] = (pair_product(grad, k_ref[u]) * SCALE).astype(BF)


class Copies:
    def __init__(self, sems):
        self.sems, self.used, self.stores = sems, 0, []

    def start(self, source, target):
        copy = pltpu.make_async_copy(source, target, self.sems.at[self.used])
        self.used += 1
        copy.start()
        return copy

    def store(self, source, target):
        self.stores.append(self.start(source, target))

    def finish(self):
        for copy in self.stores:
            copy.wait()
        self.stores = []


def slot_kernel(work, before, shards, rows, present, *refs):
    taken = iter(refs)
    given = [next(taken) if here else None for here in present]
    lengths, patches, text, cotangent, wide, tall, gain, shift, message, done = given[:10]
    kept, kept32, out, grads, sent, small, wide_out, tall_out = given[14:]
    first = wide_out is not None
    if shards:
        keep, *give = (next(taken) for _ in range(1 + shards // 2))
        *taken, left_v, right_v, weight_sems = taken
    big_a, big_b, big_c, one, f32_a, f32_b, f32_c, sems = taken
    section = lax.axis_index(SECTION)
    seqs = rows // PREFIX

    def panel(big, p):
        return big.at[:, p * D : (p + 1) * D]

    def norm_rows(at):
        return gain[at : at + 1, :], shift[at : at + 1, :]

    def put_small(early, late):
        for i, row in enumerate((early[0], late[0], early[1], late[1])):
            small[i : i + 1, :] = small[i : i + 1, :] + row

    def finish_before(cp, name, m):
        mine = slice(m * rows, (m + 1) * rows)
        if name in (ENCODE, ENCODE_MLP, CROSS):
            cp.store(done, out.at[mine])
        if name in (DECODE_MLP, ENCODE_MLP_BACK, ENCODE_BACK):
            if name == ENCODE_BACK:
                cp.store(done, kept.at[Enc.gemb, mine])
            f32_c[...] = done[...].astype(F32)
            cp.store(f32_c, grads.at[mine])

    def encode(cp, m, loads=None):
        mine = slice(m * rows, (m + 1) * rows)
        (gain_0, shift_0), (gain_1, shift_1) = norm_rows(0), norm_rows(1)
        if first:
            for p in range(PANELS):
                cols = slice(p * D, (p + 1) * D)
                for copy in loads[p]:
                    copy.wait()
                part = nn(big_a[:, cols], tall[cols, :])
                f32_a[...] = part if p == 0 else f32_a[...] + part
            for p in range(PANELS):
                cp.store(panel(big_a, p), kept.at[Enc.x + p, mine])
            for copy in loads[PANELS]:
                copy.wait()
        else:
            load = cp.start(patches.at[mine], big_a)
            load.wait()
            for p in range(PANELS):
                cp.store(panel(big_a, p), kept.at[Enc.x + p, mine])
            f32_a[...] = nn(big_a[...], tall[...])
        cp.store(f32_a, kept32.at[mine])
        stream = standardize(f32_a[...])[0] * gain_0 + shift_0
        f32_b[...] = stream
        one[0] = (standardize(stream)[0] * gain_1 + shift_1).astype(BF)
        cp.store(one.at[0], kept.at[Enc.u, mine])
        for p in range(3):
            cols = slice(p * D, (p + 1) * D)
            big_b[:, cols] = nn(one[0], wide[:, cols]).astype(BF)
            cp.store(panel(big_b, p), kept.at[Enc.q + p, mine])
        attend(seqs, *(panel(big_b, p) for p in range(4)), one.at[1], None)
        cp.store(panel(big_b, 3), kept.at[Enc.p, mine])
        cp.store(one.at[1], kept.at[Enc.att, mine])
        sent[...] = (f32_b[...] + nn(one[1], wide[:, 3 * D :])).astype(BF)

    def encode_back(cp, m, hook=None):
        mine = slice(m * rows, (m + 1) * rows)
        loads = [cp.start(kept.at[Enc.q + p, mine], panel(big_b, p)) for p in range(4)]
        load_embedded = cp.start(kept32.at[mine], f32_a)
        if hook:
            hook()
        cp.store(message, kept.at[Enc.gfirst, mine])
        (gain_0, shift_0), (gain_1, shift_1) = norm_rows(0), norm_rows(1)
        one[0] = nt(message[...], wide[:, 3 * D :]).astype(BF)
        load_embedded.wait()
        for copy in loads:
            copy.wait()
        unit_0, rstd_0 = standardize(f32_a[...])
        f32_a[...] = unit_0
        unit_1, rstd_1 = standardize(unit_0 * gain_0 + shift_0)
        f32_b[...] = unit_1
        attend_back(seqs, *(panel(big_b, p) for p in range(4)), one.at[0], *(panel(big_a, p) for p in range(3)))
        for p in range(3):
            cp.store(panel(big_a, p), kept.at[Enc.q + p, mine])
        upstream = nt(big_a[:, : 3 * D], wide[:, : 3 * D])
        grad, *late = norm_back(upstream, f32_b[...], rstd_1, gain_1)
        grad, *early = norm_back(grad + message[...].astype(F32), f32_a[...], rstd_0, gain_0)
        sent[...] = grad.astype(BF)
        put_small(early, late)
        if hook:
            cp.store(sent, kept.at[Enc.gemb, mine])
            f32_b[...] = sent[...].astype(F32)
            cp.store(f32_b, grads.at[mine])

    def mlp_forward(cp, mine, keep):
        gain_0, shift_0 = norm_rows(0)
        unit, rstd = standardize(message[...].astype(F32))
        if not keep:
            f32_b[...] = unit
        one[0] = (unit * gain_0 + shift_0).astype(BF)
        cp.store(one.at[0], kept.at[Mlp.u, mine])
        for p in range(PANELS):
            cols = slice(p * D, (p + 1) * D)
            active, slope = gelu_pair(nn(one[0], wide[:, cols]))
            big_a[:, cols] = active.astype(BF)
            big_b[:, cols] = slope.astype(BF)
            cp.store(panel(big_a, p), kept.at[Mlp.a + p, mine])
            if keep:
                cp.store(panel(big_b, p), kept.at[Mlp.gh + p, mine])
        return message[...].astype(F32) + nn(big_a[...], tall[...]), rstd

    def mlp_backward(cp, mine, upstream, unit, rstd, loads):
        grad, *late = norm_back(upstream, unit, rstd, norm_rows(1)[0])
        f32_a[...] = grad
        one[1] = grad.astype(BF)
        cp.store(one.at[1], kept.at[Mlp.gb, mine])
        for copy in loads:
            copy.wait()
        for p in range(PANELS):
            cols = slice(p * D, (p + 1) * D)
            back = nt(one[1], tall[cols, :])
            big_c[:, cols] = (back * big_b[:, cols].astype(F32)).astype(BF)
            cp.store(panel(big_c, p), kept.at[Mlp.gh + p, mine])
        return nt(big_c[...], wide[...]), late

    def encode_mlp(cp, m):
        mine = slice(m * rows, (m + 1) * rows)
        cp.store(message, kept.at[Mlp.x, mine])
        summed, _ = mlp_forward(cp, mine, True)
        f32_a[...] = summed
        cp.store(f32_a, kept32.at[mine])
        gain_1, shift_1 = norm_rows(1)
        sent[...] = (standardize(f32_a[...])[0] * gain_1 + shift_1).astype(BF)

    def encode_mlp_back(cp, m):
        mine = slice(m * rows, (m + 1) * rows)
        load_summed = cp.start(kept32.at[mine], f32_a)
        loads = [cp.start(kept.at[Mlp.gh + p, mine], panel(big_b, p)) for p in range(PANELS)]
        loads.append(cp.start(kept.at[Mlp.x, mine], one.at[0]))
        load_summed.wait()
        unit, rstd = standardize(f32_a[...])
        upstream, late = mlp_backward(cp, mine, message[...].astype(F32), unit, rstd, loads)
        unit, rstd = standardize(one[0].astype(F32))
        grad, *early = norm_back(upstream, unit, rstd, norm_rows(0)[0])
        sent[...] = (grad + f32_a[...]).astype(BF)
        put_small(early, late)

    def decode_mlp(cp, m):
        mine = slice(m * rows, (m + 1) * rows)
        load = cp.start(cotangent.at[mine], one.at[2])
        summed, rstd_0 = mlp_forward(cp, mine, False)
        gain_1, shift_1 = norm_rows(1)
        unit, rstd = standardize(summed)
        one[3] = (unit * gain_1 + shift_1).astype(BF)
        cp.store(one.at[3], out.at[mine])
        load.wait()
        place = lax.broadcasted_iota(jnp.int32, (PREFIX, D), 0)
        masked = []
        for b in range(seqs):
            at = slice(b * PREFIX, (b + 1) * PREFIX)
            masked.append(jnp.where(place < lengths[m * seqs + b], one[2, at, :].astype(F32), 0.0))
        upstream, late = mlp_backward(cp, mine, jnp.concatenate(masked, axis=0), unit, rstd, [])
        grad, *early = norm_back(upstream, f32_b[...], rstd_0, norm_rows(0)[0])
        sent[...] = (grad + f32_a[...]).astype(BF)
        put_small(early, late)

    def decode_early(cp, m):
        if m < MICRO - 2:
            decode_early_one(cp, m)
            return

        def both(i, carry):
            own = Copies(sems)
            decode_early_one(own, m + i)
            own.finish()
            return carry

        lax.fori_loop(0, 2, both, 0)

    def decode_early_one(cp, m):
        mine = pl.ds(pl.multiple_of(m * rows, rows), rows)
        load = cp.start(text.at[mine], one.at[3])
        (gain_0, shift_0), (gain_1, shift_1) = norm_rows(0), norm_rows(1)
        load.wait()
        one[0] = (standardize(one[3].astype(F32))[0] * gain_0 + shift_0).astype(BF)
        cp.store(one.at[0], kept.at[Dec.u, mine])
        for p in range(3):
            cols = slice(p * D, (p + 1) * D)
            big_b[:, cols] = nn(one[0], wide[:, cols]).astype(BF)
            cp.store(panel(big_b, p), kept.at[Dec.q + p, mine])
        attend(seqs, *(panel(big_b, p) for p in range(4)), one.at[1], lambda b: lengths[m * seqs + b])
        cp.store(panel(big_b, 3), kept.at[Dec.p, mine])
        cp.store(one.at[1], kept.at[Dec.att, mine])
        f32_a[...] = one[3].astype(F32) + nn(one[1], wide[:, 3 * D :])
        cp.store(f32_a, kept32.at[mine])
        one[2] = (standardize(f32_a[...])[0] * gain_1 + shift_1).astype(BF)
        cp.store(one.at[2], kept.at[Dec.c, mine])
        big_c[:, :D] = nn(one[2], tall[:D, :]).astype(BF)
        cp.store(panel(big_c, 0), kept.at[Dec.qc, mine])

    def decode_cross(cp, m):
        mine = slice(m * rows, (m + 1) * rows)
        load_query = cp.start(kept.at[Dec.qc, mine], panel(big_a, 0))
        load_middle = cp.start(kept32.at[mine], f32_a)
        cp.store(message, kept.at[Dec.mem, mine])
        for p in (1, 2):
            cols = slice(p * D, (p + 1) * D)
            big_a[:, cols] = nn(message[...], tall[cols, :]).astype(BF)
            cp.store(panel(big_a, p), kept.at[Dec.kc + p - 1, mine])
        load_query.wait()
        attend(seqs, *(panel(big_a, p) for p in range(4)), one.at[1], None)
        cp.store(panel(big_a, 3), kept.at[Dec.pc, mine])
        cp.store(one.at[1], kept.at[Dec.cross, mine])
        load_middle.wait()
        sent[...] = (f32_a[...] + nn(one[1], tall[3 * D :, :])).astype(BF)

    def decode_cross_back(cp, m):
        mine = slice(m * rows, (m + 1) * rows)
        places = (Dec.qc, Dec.kc, Dec.vc, Dec.pc)
        loads = [cp.start(kept.at[place, mine], panel(big_b, p)) for p, place in enumerate(places)]
        cp.store(message, kept.at[Dec.gsec, mine])
        one[0] = nt(message[...], tall[3 * D :, :]).astype(BF)
        for copy in loads:
            copy.wait()
        attend_back(seqs, *(panel(big_b, p) for p in range(4)), one.at[0], *(panel(big_c, p) for p in range(3)))
        for p in range(3):
            cp.store(panel(big_c, p), kept.at[places[p], mine])
        back = nt(big_c[:, D : 2 * D], tall[D : 2 * D, :]) + nt(big_c[:, 2 * D : 3 * D], tall[2 * D : 3 * D, :])
        sent[...] = back.astype(BF)

    def decode_late(cp, m, hook=None):
        mine = slice(m * rows, (m + 1) * rows)
        load_query = cp.start(kept.at[Dec.qc, mine], one.at[0])
        load_middle = cp.start(kept32.at[mine], f32_a)
        load_second = cp.start(kept.at[Dec.gsec, mine], one.at[1])
        loads = [cp.start(kept.at[Dec.q + p, mine], panel(big_b, p)) for p in range(4)]
        load_text = cp.start(text.at[mine], one.at[3])
        if hook:
            hook()
        load_query.wait()
        upstream = nt(one[0], tall[:D, :])
        load_middle.wait()
        load_second.wait()
        grad, *late = norm_back(upstream, *standardize(f32_a[...]), norm_rows(1)[0])
        f32_b[...] = grad + one[1].astype(F32)
        one[2] = f32_b[...].astype(BF)
        cp.store(one.at[2], kept.at[Dec.gmid, mine])
        one[0] = nt(one[2], wide[:, 3 * D :]).astype(BF)
        for copy in loads:
            copy.wait()
        attend_back(seqs, *(panel(big_b, p) for p in range(4)), one.at[0], *(panel(big_a, p) for p in range(3)))
        for p in range(3):
            cp.store(panel(big_a, p), kept.at[Dec.q + p, mine])
        upstream = nt(big_a[:, : 3 * D], wide[:, : 3 * D])
        load_text.wait()
        grad, *early = norm_back(upstream, *standardize(one[3].astype(F32)), norm_rows(0)[0])
        f32_a[...] = grad + f32_b[...]
        cp.store(f32_a, grads.at[mine])
        put_small(early, late)

    steps = {
        ENCODE: encode, ENCODE_MLP: encode_mlp, CROSS: decode_cross, DECODE_MLP: decode_mlp, CROSS_BACK: decode_cross_back,
        ENCODE_MLP_BACK: encode_mlp_back, ENCODE_BACK: encode_back, EARLY: decode_early, LATE: decode_late,
    }
    def last_slot():
        chips, held = shards // 2, kept.shape[1] - rows
        for at, (left, right) in enumerate(weight_operands()):

            @pl.when(section == at)
            def _():
                cp, loads = Copies(sems), Copies(weight_sems)
                here = slice(0, held) if at in work else slice(0, held + rows)
                copies = []

                def hook():
                    for p in range(PANELS):
                        copies.append(loads.start(kept.at[right[p], here], right_v.at[p, here]))
                        if p == 0 or left[p] != left[p - 1]:
                            copies.append(loads.start(kept.at[left[p]], left_v.at[0 if p == 0 else 1]))

                if at in before:
                    finish_before(cp, *before[at])
                if at in work:
                    name, m = work[at]
                    steps[name](cp, m, hook)
                    for p in range(PANELS - 1):
                        right_v[p, held:] = panel(big_a, p)[...]
                    right_v[PANELS - 1, held:] = message[...] if at == 0 else one[2]
                else:
                    hook()
                for copy in copies:
                    copy.wait()
                cp.finish()

        alone = section % 2 == 0
        for p in range(PANELS):
            from_left = jnp.where(alone, 1, 0) if p == PANELS - 1 else 0
            done = tn(left_v[from_left], right_v[p]).astype(BF).reshape(chips, 2, D // shards, D)
            for at in range(chips):
                put_shares(shards, keep, give, at, slice(p * D // shards, (p + 1) * D // shards), done[at])

    if small is not None:
        small[...] = jnp.zeros_like(small)
    if first:
        wide_in, tall_in, wide, tall = wide, tall, wide_out, tall_out

        def weight_loads(cp):
            for p in range(PANELS):
                at = slice(p * D, (p + 1) * D)
                yield [cp.start(tall_in.at[at], tall.at[at])]
            yield [cp.start(wide_in.at[:, p * D : (p + 1) * D], wide.at[:, p * D : (p + 1) * D]) for p in range(PANELS)]

        @pl.when(section == 0)
        def _():
            cp = Copies(sems)
            loads = [[cp.start(patches.at[:rows, p * D : (p + 1) * D], panel(big_a, p))] for p in range(PANELS)]
            loads.append([])
            for mine, more in zip(loads, weight_loads(cp)):
                mine.extend(more)
            encode(cp, 0, loads)
            cp.finish()

        @pl.when(section != 0)
        def _():
            for loads in list(weight_loads(Copies(sems))):
                for copy in loads:
                    copy.wait()

        return
    if shards:
        last_slot()
        return
    for at in sorted(set(work) | set(before)):

        @pl.when(section == at)
        def _():
            cp = Copies(sems)
            if at in before:
                finish_before(cp, *before[at])
            if at in work:
                name, m = work[at]
                steps[name](cp, m)
            cp.finish()


def weight_operands():
    e, m, d = Enc, Mlp, Dec
    mlp = ([m.u] * 4 + [m.a + p for p in range(4)], [m.gh + p for p in range(4)] + [m.gb] * 4)
    encode = ([e.u] * 3 + [e.att] + [e.x + p for p in range(4)], [e.q, e.k, e.v, e.gfirst] + [e.gemb] * 4)
    decode = ([d.u] * 3 + [d.att, d.c, d.mem, d.mem, d.cross], [d.q, d.k, d.v, d.gmid, d.qc, d.kc, d.vc, d.gsec])
    return encode, mlp, decode, mlp


def by_section(values):
    section, chosen = lax.axis_index(SECTION), values[0]
    for at, value in enumerate(values[1:], 1):
        if value != values[0]:
            chosen = jnp.where(section == at, value, chosen)
    return chosen


def put_shares(shards, keep, give, at, rows, blocks):
    chips = shards // 2
    chip, core = lax.axis_index(DP) // 2, lax.axis_index(DP) % 2
    mine = jnp.where(core == 0, blocks[0], blocks[1])
    theirs = jnp.where(core == 0, blocks[1], blocks[0])
    keep[(chip - at + chips - 1) % chips, rows] = mine
    for here in range(chips):

        @pl.when(chip == here)
        def _():
            give[(here - at + chips - 1) % chips][rows] = theirs


def tall_kernel(shards, kept, extra, keep, *refs):
    *give, left_v, right_v, sems = refs
    section = lax.axis_index(SECTION)
    lefts = [[t[0][PANELS + p] for t in weight_operands()] for p in range(PANELS)]
    rights = [[t[1][PANELS + p] for t in weight_operands()] for p in range(PANELS)]
    alone = section == 2
    share = FF // shards

    def operands(p, begin):
        left = pltpu.make_async_copy(kept.at[by_section(lefts[p])], left_v.at[p], sems.at[0, p])
        right = pltpu.make_async_copy(kept.at[by_section(rights[p])], right_v.at[p], sems.at[1, p])
        for copy, always in ((left, True), (right, p == 0)):
            act = copy.start if begin else copy.wait
            act() if always else pl.when(alone)(act)

    for p in range(PANELS):
        operands(p, True)
    for p in range(PANELS):
        operands(p, False)
        done = tn(left_v[p], right_v[jnp.where(alone, p, 0) if p else 0]).astype(BF)
        done = done.reshape(D // share // 2, 2, share, D)
        for n in range(D // share // 2):
            put_shares(shards, keep, give, p * (D // share // 2) + n, slice(0, share), done[n])
    for at in range(shards // 2):
        keep[at, share:] = extra[...]
        give[at][share:] = extra[...]


def share_shapes(shards, rows):
    return [jax.ShapeDtypeStruct((shards // 2, rows, D), BF)] + [jax.ShapeDtypeStruct((rows, D), BF)] * (shards // 2)


def tall_half(shards, kept, extra):
    total = kept.shape[1]
    in_vmem = pl.BlockSpec(memory_space=pltpu.VMEM)
    shapes = share_shapes(shards, FF // shards + extra.shape[0])
    flops = 2 * PANELS * D * D * total
    return pl.pallas_call(
        functools.partial(tall_kernel, shards),
        out_shape=tuple(shapes),
        in_specs=[pl.BlockSpec(memory_space=pl.ANY), in_vmem],
        out_specs=(in_vmem,) * len(shapes),
        scratch_shapes=[
            pltpu.VMEM((PANELS, total, D), BF),
            pltpu.VMEM((PANELS, total, D), BF),
            pltpu.SemaphoreType.DMA((2, PANELS)),
        ],
        cost_estimate=pl.CostEstimate(flops=flops, bytes_accessed=flops // total, transcendentals=0),
        compiler_params=pltpu.CompilerParams(vmem_limit_bytes=WEIGHT_LIMIT, has_side_effects=True),
        name="tall_half",
    )(kept, extra)


def after(value, other):
    return lax.optimization_barrier((value, other))[0]


def ring_scatter(wide_half, kept, little, shards):
    chips, rows = shards // 2, FF // shards
    flip = [(d, d ^ 1) for d in range(shards)]
    onward = [(d, (d + 2) % shards) for d in range(shards)]
    sent = None

    def exchange(keep, *give):
        return [(keep[at], lax.ppermute(part, DP, flip)) for at, part in enumerate(give)]

    def add(parts, running):
        keep, got = parts
        if sent is not None and running is None:
            got = after(got, sent)
        elif sent is not None:
            running = after(running, sent)
        value = keep.astype(F32) + got.astype(F32)
        return value if running is None else value + running.astype(F32)

    def send(value):
        nonlocal sent
        sent = value.astype(BF)
        return lax.ppermute(sent, DP, onward)

    wide = exchange(*wide_half)
    running = send(add(wide[0], None))
    tall = exchange(*tall_half(shards, after(kept, sent), little))
    pieces = [slice(0, 256), slice(256, rows + little.shape[0])]
    running = send(add(wide[1], running))
    low = send(add(tall[0], None))
    low = [low[piece] for piece in pieces]
    for step in range(1, chips - 1):
        if step + 1 < chips - 1:
            running = send(add(wide[step + 1], running))
        else:
            wide = sent = add(wide[-1], running)
        low = [send(add([part[piece] for part in tall[step]], got)) for piece, got in zip(pieces, low)]
    return [wide] + [add([part[piece] for part in tall[-1]], got) for piece, got in zip(pieces, low)]


def weight_part(i, kept):
    lefts, rights = ([t[side][i] for t in weight_operands()] for side in (0, 1))
    left, right = (lax.dynamic_index_in_dim(kept, by_section(values), 0, keepdims=False) for values in (lefts, rights))
    return tn(left, right).astype(BF)


def schedule():
    plan = [(0, 0, ENCODE, 1), (1, 2, ENCODE_MLP, 1), (2, 4, CROSS, 1), (3, 6, DECODE_MLP, -1), (2, 8, CROSS_BACK, -1),
            (1, 10, ENCODE_MLP_BACK, -1), (0, 12, ENCODE_BACK, 0), (2, 1, EARLY, 0), (2, 12, LATE, 0)]
    slots = []
    for k in range(MICRO + 12):
        work, sends = {}, []
        for section, begin, name, way in plan:
            if 0 <= k - begin < MICRO - (name == EARLY):
                assert section not in work
                work[section] = (name, k - begin)
                if way:
                    sends.append((section, section + way))
        slots.append((work, sends))
    return slots


def on_device(patches, text, lengths, cotangent, wide, tall, gain, shift):
    total = patches.shape[0]
    rows = total // MICRO
    shards = lax.axis_size(DP)
    share = D // shards
    in_ring = share % 16 == 0 and shards % 2 == 0 and D % (2 * FF // shards) == 0
    wide, tall, gain, shift = wide[0], tall[0], gain[0], shift[0]
    anywhere = pl.BlockSpec(memory_space=pl.ANY)
    in_vmem = pl.BlockSpec(memory_space=pltpu.VMEM)
    in_smem = pl.BlockSpec(memory_space=pltpu.SMEM)
    specs = [in_smem] + [anywhere] * 3 + [in_vmem] * 6 + [anywhere] * 8 + [in_vmem] * 4
    shapes = [
        jax.ShapeDtypeStruct((SLOTS, total, D), BF),
        jax.ShapeDtypeStruct((total, D), F32),
        jax.ShapeDtypeStruct((total, D), BF),
        jax.ShapeDtypeStruct((total, D), F32),
        jax.ShapeDtypeStruct((rows, D), BF),
        jax.ShapeDtypeStruct((8, D), F32),
        jax.ShapeDtypeStruct(wide.shape, BF),
        jax.ShapeDtypeStruct(tall.shape, BF),
    ]
    state, messages, smalls, done, before = [None] * 4, [None, None], [], None, {}
    slots = schedule()
    for k, (work, sends) in enumerate(slots):
        now, old = {name for name, _ in work.values()}, {name for name, _ in before.values()}

        def given(value, *names):
            return value if now & set(names) else None

        operands = [
            given(lengths, EARLY, DECODE_MLP),
            given(patches, ENCODE),
            given(text, EARLY, LATE),
            given(cotangent, DECODE_MLP),
            wide, tall, gain, shift,
            given(messages[-2], ENCODE_MLP, CROSS, DECODE_MLP, CROSS_BACK, ENCODE_MLP_BACK, ENCODE_BACK),
            done if old - {EARLY, LATE} else None,
            *state,
        ]
        results = [True] * 4 + [bool(now - {EARLY, LATE}), bool(now & {DECODE_MLP, ENCODE_MLP_BACK, ENCODE_BACK, LATE})]
        results += [k == 0] * 2
        present = tuple(value is not None for value in operands) + tuple(results)
        places = [i for i, value in enumerate(operands) if value is not None]
        merged = in_ring and k + 1 == len(slots)
        more = share_shapes(shards, FF // shards) if merged else []
        values = pl.pallas_call(
            functools.partial(slot_kernel, work, before, shards if merged else 0, rows, present),
            out_shape=tuple(shape for shape, here in zip(shapes, results) if here) + tuple(more),
            in_specs=[anywhere if k == 0 and i in (4, 5) else specs[i] for i in places],
            out_specs=[spec for spec, here in zip(specs[14:], results) if here] + [in_vmem] * len(more),
            input_output_aliases={places.index(10 + i): i for i in range(4)} if k else {},
            scratch_shapes=[
                pltpu.VMEM((rows, FF), BF),
                pltpu.VMEM((rows, FF), BF),
                pltpu.VMEM((rows, FF), BF),
                pltpu.VMEM((4, rows, D), BF),
                pltpu.VMEM((rows, D), F32),
                pltpu.VMEM((rows, D), F32),
                pltpu.VMEM((rows, D), F32),
                pltpu.SemaphoreType.DMA((48,)),
                *(
                    [
                        pltpu.VMEM((2, total, D), BF),
                        pltpu.VMEM((PANELS, total, D), BF),
                        pltpu.SemaphoreType.DMA((2 * PANELS,)),
                    ]
                    if merged
                    else []
                ),
            ],
            compiler_params=pltpu.CompilerParams(vmem_limit_bytes=LAST_LIMIT if merged else VMEM_LIMIT if k else FIRST_LIMIT, has_side_effects=True),
            cost_estimate=pl.CostEstimate(flops=9_000_000_000, bytes_accessed=4_000_000, transcendentals=0),
            name=f"slot_{k}",
        )(*(operands[i] for i in places))
        state, rest = list(values[:4]), list(values[4:])
        done = rest.pop(0) if results[4] else None
        if results[5]:
            smalls.append(rest.pop(0))
        if k == 0:
            wide, tall = rest
        wide_half = rest
        messages.append(lax.ppermute(done, SECTION, sends) if sends else None)
        before = work
    kept, _, out, grads = state

    little = sum(smalls)
    high = little.astype(BF)
    little = jnp.concatenate([high, (little - high.astype(F32)).astype(BF)], axis=0)
    if in_ring:
        mine, low, high = ring_scatter(wide_half, kept, little, shards)
        wide_grad = jnp.concatenate([mine[p * share : (p + 1) * share] for p in range(PANELS)], axis=1)
        tall_grad = jnp.concatenate([low, high[:-16]], axis=0)
        little = high[-16:]
    else:
        parts = [weight_part(i, kept) for i in range(2 * PANELS)]
        wide_grad = lax.psum_scatter(jnp.concatenate(parts[:PANELS], axis=1), DP, scatter_dimension=0, tiled=True)
        tall_grad = lax.psum_scatter(jnp.concatenate(parts[PANELS:], axis=0), DP, scatter_dimension=0, tiled=True)
        little = lax.psum(little, DP)
    little = little[:4].astype(F32) + little[8:12].astype(F32)
    little = lax.dynamic_slice_in_dim(little, lax.axis_index(DP) * share, share, axis=1)
    return (
        out[None],
        grads[None],
        wide_grad.astype(F32)[None],
        tall_grad.astype(F32)[None],
        little[None, :2],
        little[None, 2:],
    )


def solution(mesh):
    return jax.shard_map(
        on_device,
        mesh=mesh,
        in_specs=(
            P(DP, None),
            P(DP, None),
            P(DP),
            P(DP, None),
            P(SECTION, None, None),
            P(SECTION, None, None),
            P(SECTION, None, None),
            P(SECTION, None, None),
        ),
        out_specs=(
            P(SECTION, DP, None),
            P(SECTION, DP, None),
            P(SECTION, DP, None),
            P(SECTION, DP, None),
            P(SECTION, None, DP),
            P(SECTION, None, DP),
        ),
        check_vma=False,
    )
```

```python
import functools

import jax
import jax.numpy as jnp
from jax import lax
from jax.experimental import pallas as pl
from jax.experimental.pallas import tpu as pltpu
from jax.sharding import PartitionSpec as P

D = 768
HEADS = 12
FF = 3072
HEAD_DIM = 64
PREFIX = 64
PANELS = FF // D
GROUP = 4
LANES = GROUP * HEAD_DIM
GROUPS = HEADS // GROUP
EPS = 1e-05
NEG = -1e30
SCALE = HEAD_DIM ** (-0.5)
MICRO = 4
SLOTS = 15
VMEM_LIMIT = 24 * 1024 * 1024
FIRST_LIMIT = 38 * 1024 * 1024
LAST_LIMIT = 29 * 1024 * 1024
WEIGHT_LIMIT = 32 * 1024 * 1024
BF = jnp.bfloat16
F32 = jnp.float32

SECTION, DP = "section", "dp"
ENCODE, ENCODE_MLP, CROSS, DECODE_MLP, CROSS_BACK, ENCODE_MLP_BACK, ENCODE_BACK, EARLY, LATE = range(9)


class Enc:
    u, q, k, v, p, att, gfirst, gemb, x = range(9)


class Mlp:
    u, x, gb, a, gh = 0, 1, 2, 3, 7


class Dec:
    u, q, k, v, p, att, c, qc, mem, kc, vc, pc, cross, gsec, gmid = range(15)


AHEAD = {
    CROSS_BACK: (Dec.qc, Dec.kc, Dec.vc, Dec.pc),
    ENCODE_MLP_BACK: (Mlp.gh, Mlp.gh + 1, Mlp.gh + 2, Mlp.gh + 3),
    ENCODE_BACK: (Enc.q, Enc.k, Enc.v, Enc.p),
}


def nn(left, right):
    return lax.dot_general(left, right, (((1,), (0,)), ((), ())), preferred_element_type=F32)


def nt(left, right):
    return lax.dot_general(left, right, (((1,), (1,)), ((), ())), preferred_element_type=F32)


def tn(left, right):
    return lax.dot_general(left, right, (((0,), (0,)), ((), ())), preferred_element_type=F32)


def standardize(values):
    center = values - jnp.mean(values, -1, keepdims=True)
    rstd = lax.rsqrt(jnp.mean(center * center, -1, keepdims=True) + EPS)
    return center * rstd, rstd


def norm_back(upstream, unit, rstd, gain_row):
    scaled = upstream * gain_row
    mean_one = jnp.mean(scaled, -1, keepdims=True)
    mean_two = jnp.mean(scaled * unit, -1, keepdims=True)
    grad = rstd * (scaled - mean_one - unit * mean_two)
    return grad, jnp.sum(upstream * unit, 0, keepdims=True), jnp.sum(upstream, 0, keepdims=True)


def gelu_pair(hidden):
    c = 0.7978845608028654
    square = hidden * hidden
    t = jnp.tanh(hidden * (c + (c * 0.044715) * square))
    half = 0.5 + 0.5 * t
    active = hidden * half
    slope = half + active * (1.0 - t) * (c + (3.0 * c * 0.044715) * square)
    return active, slope


def block_diagonal(rows):
    tiled = jnp.concatenate([rows] * GROUP, axis=0)
    at_row = lax.broadcasted_iota(jnp.int32, tiled.shape, 0) // HEAD_DIM
    at_lane = lax.broadcasted_iota(jnp.int32, tiled.shape, 1) // HEAD_DIM
    return jnp.where(at_row == at_lane, tiled, jnp.zeros_like(tiled))


def head_rows(pairs):
    low = lax.broadcasted_iota(jnp.int32, (PREFIX, 2 * HEAD_DIM), 1) < HEAD_DIM
    return jnp.concatenate([jnp.where(low, p[:PREFIX], p[PREFIX:]) for p in pairs], axis=1)


def units(count):
    return [
        (slice(b * PREFIX, (b + 1) * PREFIX), slice(g * LANES, (g + 1) * LANES)) for b in range(count) for g in range(GROUPS)
    ]


def pair_product(left, right):
    return head_rows([tn(left[:, i : i + 128], right[:, i : i + 128]) for i in range(0, LANES, 128)])


def attend(count, q_ref, k_ref, v_ref, p_ref, out_ref, length_of):
    at = units(count)
    scores = [nt(k_ref[u], block_diagonal(q_ref[u])) * SCALE for u in at]
    if length_of is not None:
        key_at = lax.broadcasted_iota(jnp.int32, (PREFIX, LANES), 0)
        query_at = lax.broadcasted_iota(jnp.int32, (PREFIX, LANES), 1) % PREFIX
        allowed = [(key_at <= query_at) & (key_at < length_of(b)) for b in range(count)]
        scores = [jnp.where(allowed[i // GROUPS], values, NEG) for i, values in enumerate(scores)]
    probs = []
    for u, values in zip(at, scores):
        e = jnp.exp(values - jnp.max(values, 0, keepdims=True))
        probs.append((e * (1.0 / jnp.sum(e, 0, keepdims=True))).astype(BF))
        p_ref[u] = probs[-1]
    for u, p in zip(at, probs):
        out_ref[u] = pair_product(p, v_ref[u]).astype(BF)


def attend_back(count, q_ref, k_ref, v_ref, p_ref, up_ref, gq_ref, gk_ref, gv_ref):
    at = units(count)
    ups = [block_diagonal(up_ref[u]) for u in at]
    grads = [nt(v_ref[u], up) for u, up in zip(at, ups)]
    for u, up in zip(at, ups):
        gv_ref[u] = nn(p_ref[u], up).astype(BF)
    scores = []
    for u, grad in zip(at, grads):
        p = p_ref[u].astype(F32)
        scores.append((p * (grad - jnp.sum(grad * p, 0, keepdims=True))).astype(BF))
    for u, grad in zip(at, scores):
        gk_ref[u] = (nn(grad, block_diagonal(q_ref[u])) * SCALE).astype(BF)
    for u, grad in zip(at, scores):
        gq_ref[u] = (pair_product(grad, k_ref[u]) * SCALE).astype(BF)


class Copies:
    def __init__(self, sems):
        self.sems, self.used, self.stores, self.sizes = sems, 0, [], []

    def start(self, source, target):
        copy = pltpu.make_async_copy(source, target, self.sems.at[self.used])
        self.used += 1
        copy.start()
        return copy

    def store(self, source, target):
        self.sizes.append((self.used, source.dtype))
        self.stores.append(self.start(source, target))

    def finish(self):
        for copy in self.stores:
            copy.wait()
        self.stores = []


def slot_kernel(work, before, coming, shards, rows, present, *refs):
    taken = iter(refs)
    given = [next(taken) if here else None for here in present]
    lengths, patches, text, cotangent, wide, tall, gain, shift, message, done = given[:10]
    fetched = given[14]
    kept, kept32, out, grads, sent, small, wide_out, tall_out, ahead = given[15:]
    first = wide_out is not None
    if shards:
        keep, *give = (next(taken) for _ in range(1 + shards // 2))
        *taken, left_v, right_v, done_v, weight_sems = taken
    big_a, big_b, big_c, one, f32_a, f32_b, f32_c, sems = taken
    section = lax.axis_index(SECTION)
    seqs = rows // PREFIX

    def panel(big, p):
        return big.at[:, p * D : (p + 1) * D]

    def norm_rows(at):
        return gain[at : at + 1, :], shift[at : at + 1, :]

    def put_small(early, late):
        for i, row in enumerate((early[0], late[0], early[1], late[1])):
            small[i : i + 1, :] = small[i : i + 1, :] + row

    def fetch_ahead(cp, name, m):
        mine = slice(m * rows, (m + 1) * rows)
        for p, place in enumerate(AHEAD[name]):
            cp.store(kept.at[place, mine], panel(ahead, p))

    def finish_before(cp, name, m):
        mine = slice(m * rows, (m + 1) * rows)
        if name in (ENCODE, ENCODE_MLP, CROSS):
            cp.store(done, out.at[mine])
        if name in (DECODE_MLP, ENCODE_MLP_BACK, ENCODE_BACK):
            if name == ENCODE_BACK:
                cp.store(done, kept.at[Enc.gemb, mine])
            f32_c[...] = done[...].astype(F32)
            cp.store(f32_c, grads.at[mine])

    def encode(cp, m, loads=None):
        mine = slice(m * rows, (m + 1) * rows)
        (gain_0, shift_0), (gain_1, shift_1) = norm_rows(0), norm_rows(1)
        if first:
            for p in range(PANELS):
                cols = slice(p * D, (p + 1) * D)
                for copy in loads[p]:
                    copy.wait()
                part = nn(big_a[:, cols], tall[cols, :])
                f32_a[...] = part if p == 0 else f32_a[...] + part
            for p in range(PANELS):
                cp.store(panel(big_a, p), kept.at[Enc.x + p, mine])
            for copy in loads[PANELS]:
                copy.wait()
        else:
            load = cp.start(patches.at[mine], big_a)
            load.wait()
            for p in range(PANELS):
                cp.store(panel(big_a, p), kept.at[Enc.x + p, mine])
            f32_a[...] = nn(big_a[...], tall[...])
        cp.store(f32_a, kept32.at[mine])
        stream = standardize(f32_a[...])[0] * gain_0 + shift_0
        f32_b[...] = stream
        one[0] = (standardize(stream)[0] * gain_1 + shift_1).astype(BF)
        cp.store(one.at[0], kept.at[Enc.u, mine])
        for p in range(3):
            cols = slice(p * D, (p + 1) * D)
            big_b[:, cols] = nn(one[0], wide[:, cols]).astype(BF)
            cp.store(panel(big_b, p), kept.at[Enc.q + p, mine])
        attend(seqs, *(panel(big_b, p) for p in range(4)), one.at[1], None)
        cp.store(panel(big_b, 3), kept.at[Enc.p, mine])
        cp.store(one.at[1], kept.at[Enc.att, mine])
        sent[...] = (f32_b[...] + nn(one[1], wide[:, 3 * D :])).astype(BF)

    def encode_back(cp, m, hook=None):
        mine = slice(m * rows, (m + 1) * rows)
        load_embedded = cp.start(kept32.at[mine], f32_a)
        if hook:
            hook()
        cp.store(message, kept.at[Enc.gfirst, mine])
        (gain_0, shift_0), (gain_1, shift_1) = norm_rows(0), norm_rows(1)
        one[0] = nt(message[...], wide[:, 3 * D :]).astype(BF)
        load_embedded.wait()
        unit_0, rstd_0 = standardize(f32_a[...])
        f32_a[...] = unit_0
        unit_1, rstd_1 = standardize(unit_0 * gain_0 + shift_0)
        f32_b[...] = unit_1
        attend_back(seqs, *(panel(fetched, p) for p in range(4)), one.at[0], *(panel(big_a, p) for p in range(3)))
        for p in range(3):
            cp.store(panel(big_a, p), kept.at[Enc.q + p, mine])
        upstream = nt(big_a[:, : 3 * D], wide[:, : 3 * D])
        grad, *late = norm_back(upstream, f32_b[...], rstd_1, gain_1)
        grad, *early = norm_back(grad + message[...].astype(F32), f32_a[...], rstd_0, gain_0)
        sent[...] = grad.astype(BF)
        put_small(early, late)
        if hook:
            cp.store(sent, kept.at[Enc.gemb, mine])
            f32_b[...] = sent[...].astype(F32)
            cp.store(f32_b, grads.at[mine])

    def mlp_forward(cp, mine, keep):
        gain_0, shift_0 = norm_rows(0)
        unit, rstd = standardize(message[...].astype(F32))
        if not keep:
            f32_b[...] = unit
        one[0] = (unit * gain_0 + shift_0).astype(BF)
        cp.store(one.at[0], kept.at[Mlp.u, mine])
        for p in range(PANELS):
            cols = slice(p * D, (p + 1) * D)
            active, slope = gelu_pair(nn(one[0], wide[:, cols]))
            big_a[:, cols] = active.astype(BF)
            big_b[:, cols] = slope.astype(BF)
            cp.store(panel(big_a, p), kept.at[Mlp.a + p, mine])
            if keep:
                cp.store(panel(big_b, p), kept.at[Mlp.gh + p, mine])
        return message[...].astype(F32) + nn(big_a[...], tall[...]), rstd

    def mlp_backward(cp, mine, upstream, unit, rstd, loads, slopes):
        grad, *late = norm_back(upstream, unit, rstd, norm_rows(1)[0])
        f32_a[...] = grad
        one[1] = grad.astype(BF)
        cp.store(one.at[1], kept.at[Mlp.gb, mine])
        for copy in loads:
            copy.wait()
        for p in range(PANELS):
            cols = slice(p * D, (p + 1) * D)
            back = nt(one[1], tall[cols, :])
            big_c[:, cols] = (back * slopes[:, cols].astype(F32)).astype(BF)
            cp.store(panel(big_c, p), kept.at[Mlp.gh + p, mine])
        return nt(big_c[...], wide[...]), late

    def encode_mlp(cp, m):
        mine = slice(m * rows, (m + 1) * rows)
        cp.store(message, kept.at[Mlp.x, mine])
        summed, _ = mlp_forward(cp, mine, True)
        f32_a[...] = summed
        cp.store(f32_a, kept32.at[mine])
        gain_1, shift_1 = norm_rows(1)
        sent[...] = (standardize(f32_a[...])[0] * gain_1 + shift_1).astype(BF)

    def encode_mlp_back(cp, m):
        mine = slice(m * rows, (m + 1) * rows)
        load_summed = cp.start(kept32.at[mine], f32_a)
        loads = [cp.start(kept.at[Mlp.x, mine], one.at[0])]
        load_summed.wait()
        unit, rstd = standardize(f32_a[...])
        upstream, late = mlp_backward(cp, mine, message[...].astype(F32), unit, rstd, loads, fetched)
        unit, rstd = standardize(one[0].astype(F32))
        grad, *early = norm_back(upstream, unit, rstd, norm_rows(0)[0])
        sent[...] = (grad + f32_a[...]).astype(BF)
        put_small(early, late)

    def decode_mlp(cp, m):
        mine = slice(m * rows, (m + 1) * rows)
        load = cp.start(cotangent.at[mine], one.at[2])
        summed, rstd_0 = mlp_forward(cp, mine, False)
        gain_1, shift_1 = norm_rows(1)
        unit, rstd = standardize(summed)
        one[3] = (unit * gain_1 + shift_1).astype(BF)
        cp.store(one.at[3], out.at[mine])
        load.wait()
        place = lax.broadcasted_iota(jnp.int32, (PREFIX, D), 0)
        masked = []
        for b in range(seqs):
            at = slice(b * PREFIX, (b + 1) * PREFIX)
            masked.append(jnp.where(place < lengths[m * seqs + b], one[2, at, :].astype(F32), 0.0))
        upstream, late = mlp_backward(cp, mine, jnp.concatenate(masked, axis=0), unit, rstd, [], big_b)
        grad, *early = norm_back(upstream, f32_b[...], rstd_0, norm_rows(0)[0])
        sent[...] = (grad + f32_a[...]).astype(BF)
        put_small(early, late)

    def decode_early(cp, m):
        if m < MICRO - 2:
            decode_early_one(cp, m)
            return

        def both(i, carry):
            own = Copies(sems)
            decode_early_one(own, m + i)
            own.finish()
            return carry

        lax.fori_loop(0, 2, both, 0)

    def decode_early_one(cp, m):
        mine = pl.ds(pl.multiple_of(m * rows, rows), rows)
        load = cp.start(text.at[mine], one.at[3])
        (gain_0, shift_0), (gain_1, shift_1) = norm_rows(0), norm_rows(1)
        load.wait()
        one[0] = (standardize(one[3].astype(F32))[0] * gain_0 + shift_0).astype(BF)
        cp.store(one.at[0], kept.at[Dec.u, mine])
        for p in range(3):
            cols = slice(p * D, (p + 1) * D)
            big_b[:, cols] = nn(one[0], wide[:, cols]).astype(BF)
            cp.store(panel(big_b, p), kept.at[Dec.q + p, mine])
        attend(seqs, *(panel(big_b, p) for p in range(4)), one.at[1], lambda b: lengths[m * seqs + b])
        cp.store(panel(big_b, 3), kept.at[Dec.p, mine])
        cp.store(one.at[1], kept.at[Dec.att, mine])
        f32_a[...] = one[3].astype(F32) + nn(one[1], wide[:, 3 * D :])
        cp.store(f32_a, kept32.at[mine])
        one[2] = (standardize(f32_a[...])[0] * gain_1 + shift_1).astype(BF)
        cp.store(one.at[2], kept.at[Dec.c, mine])
        big_c[:, :D] = nn(one[2], tall[:D, :]).astype(BF)
        cp.store(panel(big_c, 0), kept.at[Dec.qc, mine])

    def decode_cross(cp, m):
        mine = slice(m * rows, (m + 1) * rows)
        load_query = cp.start(kept.at[Dec.qc, mine], panel(big_a, 0))
        load_middle = cp.start(kept32.at[mine], f32_a)
        cp.store(message, kept.at[Dec.mem, mine])
        for p in (1, 2):
            cols = slice(p * D, (p + 1) * D)
            big_a[:, cols] = nn(message[...], tall[cols, :]).astype(BF)
            cp.store(panel(big_a, p), kept.at[Dec.kc + p - 1, mine])
        load_query.wait()
        attend(seqs, *(panel(big_a, p) for p in range(4)), one.at[1], None)
        cp.store(panel(big_a, 3), kept.at[Dec.pc, mine])
        cp.store(one.at[1], kept.at[Dec.cross, mine])
        load_middle.wait()
        sent[...] = (f32_a[...] + nn(one[1], tall[3 * D :, :])).astype(BF)

    def decode_cross_back(cp, m):
        mine = slice(m * rows, (m + 1) * rows)
        places = AHEAD[CROSS_BACK]
        cp.store(message, kept.at[Dec.gsec, mine])
        one[0] = nt(message[...], tall[3 * D :, :]).astype(BF)
        attend_back(seqs, *(panel(fetched, p) for p in range(4)), one.at[0], *(panel(big_c, p) for p in range(3)))
        for p in range(3):
            cp.store(panel(big_c, p), kept.at[places[p], mine])
        back = nt(big_c[:, D : 2 * D], tall[D : 2 * D, :]) + nt(big_c[:, 2 * D : 3 * D], tall[2 * D : 3 * D, :])
        sent[...] = back.astype(BF)

    def decode_late(cp, m, hook=None):
        mine = slice(m * rows, (m + 1) * rows)
        load_query = cp.start(kept.at[Dec.qc, mine], one.at[0])
        load_middle = cp.start(kept32.at[mine], f32_a)
        load_second = cp.start(kept.at[Dec.gsec, mine], one.at[1])
        loads = [cp.start(kept.at[Dec.q + p, mine], panel(big_b, p)) for p in range(4)]
        load_text = cp.start(text.at[mine], one.at[3])
        if hook:
            hook()
        load_query.wait()
        upstream = nt(one[0], tall[:D, :])
        load_middle.wait()
        load_second.wait()
        grad, *late = norm_back(upstream, *standardize(f32_a[...]), norm_rows(1)[0])
        f32_b[...] = grad + one[1].astype(F32)
        one[2] = f32_b[...].astype(BF)
        cp.store(one.at[2], kept.at[Dec.gmid, mine])
        one[0] = nt(one[2], wide[:, 3 * D :]).astype(BF)
        for copy in loads:
            copy.wait()
        attend_back(seqs, *(panel(big_b, p) for p in range(4)), one.at[0], *(panel(big_a, p) for p in range(3)))
        for p in range(3):
            cp.store(panel(big_a, p), kept.at[Dec.q + p, mine])
        upstream = nt(big_a[:, : 3 * D], wide[:, : 3 * D])
        load_text.wait()
        grad, *early = norm_back(upstream, *standardize(one[3].astype(F32)), norm_rows(0)[0])
        f32_a[...] = grad + f32_b[...]
        cp.store(f32_a, grads.at[mine])
        put_small(early, late)

    steps = {
        ENCODE: encode, ENCODE_MLP: encode_mlp, CROSS: decode_cross, DECODE_MLP: decode_mlp, CROSS_BACK: decode_cross_back,
        ENCODE_MLP_BACK: encode_mlp_back, ENCODE_BACK: encode_back, EARLY: decode_early, LATE: decode_late,
    }
    def last_slot():
        chips, held, left_over = shards // 2, kept.shape[1] - rows, {}
        for at, (left, right) in enumerate(weight_operands()):

            @pl.when(section == at)
            def _():
                cp, loads = Copies(sems), Copies(weight_sems)
                here = slice(0, held) if at in work else slice(0, held + rows)
                copies = []

                def hook():
                    for p in range(PANELS):
                        copies.append(loads.start(kept.at[right[p], here], right_v.at[p, here]))
                        if p == 0 or left[p] != left[p - 1]:
                            copies.append(loads.start(kept.at[left[p]], left_v.at[0 if p == 0 else 1]))

                if at in before:
                    finish_before(cp, *before[at])
                if at in work:
                    name, m = work[at]
                    steps[name](cp, m, hook)
                    for p in range(PANELS - 1):
                        right_v[p, held:] = panel(big_a, p)[...]
                    right_v[PANELS - 1, held:] = message[...] if at == 0 else one[2]
                else:
                    hook()
                for copy in copies:
                    copy.wait()
                left_over[at] = cp.sizes

        alone = section % 2 == 0
        for p in range(PANELS):
            from_left = jnp.where(alone, 1, 0) if p == PANELS - 1 else 0
            done_v[p % 2] = tn(left_v[from_left], right_v[p]).astype(BF).reshape(chips, 2, D // shards, D)
            rows_of_part = slice(p * D // shards, (p + 1) * D // shards)
            put_shares(shards, keep, give, rows_of_part, lambda chip, core: done_v[p % 2, chip, core])
        for at, stores in left_over.items():

            @pl.when(section == at)
            def _():
                for number, dtype in stores:
                    pair = (f32_a, f32_b) if dtype == F32 else (one.at[0], one.at[1])
                    pltpu.make_async_copy(*pair, sems.at[number]).wait()

    if small is not None:
        small[...] = jnp.zeros_like(small)
    if first:
        wide_in, tall_in, wide, tall = wide, tall, wide_out, tall_out

        def weight_loads(cp):
            for p in range(PANELS):
                at = slice(p * D, (p + 1) * D)
                yield [cp.start(tall_in.at[at], tall.at[at])]
            yield [cp.start(wide_in.at[:, p * D : (p + 1) * D], wide.at[:, p * D : (p + 1) * D]) for p in range(PANELS)]

        @pl.when(section == 0)
        def _():
            cp = Copies(sems)
            loads = []
            for p, more in enumerate(weight_loads(cp)):
                if p < PANELS:
                    more.append(cp.start(patches.at[:rows, p * D : (p + 1) * D], panel(big_a, p)))
                loads.append(more)
            encode(cp, 0, loads)
            cp.finish()

        @pl.when(section != 0)
        def _():
            for loads in list(weight_loads(Copies(sems))):
                for copy in loads:
                    copy.wait()

        return
    if shards:
        last_slot()
        return
    for at in sorted(set(work) | set(before) | set(coming)):

        @pl.when(section == at)
        def _():
            cp = Copies(sems)
            if at in coming:
                fetch_ahead(cp, *coming[at])
            if at in before:
                finish_before(cp, *before[at])
            if at in work:
                name, m = work[at]
                steps[name](cp, m)
            cp.finish()


def weight_operands():
    e, m, d = Enc, Mlp, Dec
    mlp = ([m.u] * 4 + [m.a + p for p in range(4)], [m.gh + p for p in range(4)] + [m.gb] * 4)
    encode = ([e.u] * 3 + [e.att] + [e.x + p for p in range(4)], [e.q, e.k, e.v, e.gfirst] + [e.gemb] * 4)
    decode = ([d.u] * 3 + [d.att, d.c, d.mem, d.mem, d.cross], [d.q, d.k, d.v, d.gmid, d.qc, d.kc, d.vc, d.gsec])
    return encode, mlp, decode, mlp


def by_section(values):
    section, chosen = lax.axis_index(SECTION), values[0]
    for at, value in enumerate(values[1:], 1):
        if value != values[0]:
            chosen = jnp.where(section == at, value, chosen)
    return chosen


def put_shares(shards, keep, give, rows, block):
    chips = shards // 2
    chip, core = lax.axis_index(DP) // 2, lax.axis_index(DP) % 2
    for step in range(chips):
        at = (chip + 2 * chips - 1 - step) % chips
        keep[step, rows] = block(at, core)
        give[step][rows] = block(at, 1 - core)


def tall_kernel(shards, kept, extra, keep, *refs):
    *give, left_v, right_v, done_v, sems = refs
    section = lax.axis_index(SECTION)
    lefts = [[t[0][PANELS + p] for t in weight_operands()] for p in range(PANELS)]
    rights = [[t[1][PANELS + p] for t in weight_operands()] for p in range(PANELS)]
    alone = section == 2
    share = FF // shards
    here = D // share // 2

    def operands(p, begin):
        left = pltpu.make_async_copy(kept.at[by_section(lefts[p])], left_v.at[p], sems.at[0, p])
        right = pltpu.make_async_copy(kept.at[by_section(rights[p])], right_v.at[p], sems.at[1, p])
        for copy, always in ((left, True), (right, p == 0)):
            act = copy.start if begin else copy.wait
            act() if always else pl.when(alone)(act)

    for p in range(PANELS):
        operands(p, True)
    for p in range(PANELS):
        operands(p, False)
        done = tn(left_v[p], right_v[jnp.where(alone, p, 0) if p else 0]).astype(BF)
        done_v[p * here : (p + 1) * here] = done.reshape(here, 2, share, D)
    put_shares(shards, keep, give, slice(0, share), lambda chip, core: done_v[chip, core])
    for at in range(shards // 2):
        keep[at, share:] = extra[...]
        give[at][share:] = extra[...]


def share_shapes(shards, rows):
    return [jax.ShapeDtypeStruct((shards // 2, rows, D), BF)] + [jax.ShapeDtypeStruct((rows, D), BF)] * (shards // 2)


def tall_half(shards, kept, extra):
    total = kept.shape[1]
    in_vmem = pl.BlockSpec(memory_space=pltpu.VMEM)
    shapes = share_shapes(shards, FF // shards + extra.shape[0])
    flops = 2 * PANELS * D * D * total
    return pl.pallas_call(
        functools.partial(tall_kernel, shards),
        out_shape=tuple(shapes),
        in_specs=[pl.BlockSpec(memory_space=pl.ANY), in_vmem],
        out_specs=(in_vmem,) * len(shapes),
        scratch_shapes=[
            pltpu.VMEM((PANELS, total, D), BF),
            pltpu.VMEM((PANELS, total, D), BF),
            pltpu.VMEM((shards // 2, 2, FF // shards, D), BF),
            pltpu.SemaphoreType.DMA((2, PANELS)),
        ],
        cost_estimate=pl.CostEstimate(flops=flops, bytes_accessed=flops // total, transcendentals=0),
        compiler_params=pltpu.CompilerParams(vmem_limit_bytes=WEIGHT_LIMIT, has_side_effects=True),
        name="tall_half",
    )(kept, extra)


def after(value, other):
    return lax.optimization_barrier((value, other))[0]


def ring_scatter(wide_half, kept, little, shards):
    chips, rows = shards // 2, FF // shards
    flip = [(d, d ^ 1) for d in range(shards)]
    onward = [(d, (d + 2) % shards) for d in range(shards)]
    sent = None

    def exchange(keep, *give):
        return [(keep[at], lax.ppermute(part, DP, flip)) for at, part in enumerate(give)]

    def add(parts, running, piece=slice(None), whole=False):
        keep, got = parts
        if sent is not None and running is None:
            got = after(got, sent)
        elif sent is not None:
            running = after(running, sent)
        value = keep[piece].astype(F32) + got[piece].astype(F32)
        if running is None:
            return value
        return value + (running[piece] if whole else running).astype(F32)

    def send(value):
        nonlocal sent
        sent = value.astype(BF)
        return lax.ppermute(sent, DP, onward)

    wide = exchange(*wide_half)
    running = send(add(wide[0], None))
    tall = exchange(*tall_half(shards, after(kept, sent), little))
    cut = (rows + little.shape[0]) * 3 // 8 // 16 * 16
    pieces = [slice(cut, rows + little.shape[0]), slice(0, cut)]
    running = send(add(wide[1], running))
    low = [send(add(tall[0], None))] * len(pieces)
    for step in range(1, chips - 1):
        if step + 1 < chips - 1:
            running = send(add(wide[step + 1], running))
        else:
            wide = sent = add(wide[-1], running)
        low = [send(add(tall[step], got, piece, step == 1)) for piece, got in zip(pieces, low)]
    return [wide] + [add(tall[-1], got, piece) for piece, got in zip(pieces, low)]


def weight_part(i, kept):
    lefts, rights = ([t[side][i] for t in weight_operands()] for side in (0, 1))
    left, right = (lax.dynamic_index_in_dim(kept, by_section(values), 0, keepdims=False) for values in (lefts, rights))
    return tn(left, right).astype(BF)


def schedule():
    plan = [(0, 0, ENCODE, 1), (1, 2, ENCODE_MLP, 1), (2, 4, CROSS, 1), (3, 6, DECODE_MLP, -1), (2, 8, CROSS_BACK, -1),
            (1, 10, ENCODE_MLP_BACK, -1), (0, 12, ENCODE_BACK, 0), (2, 1, EARLY, 0), (2, 12, LATE, 0)]
    slots = []
    for k in range(MICRO + 12):
        work, sends = {}, []
        for section, begin, name, way in plan:
            if 0 <= k - begin < MICRO - (name == EARLY):
                assert section not in work
                work[section] = (name, k - begin)
                if way:
                    sends.append((section, section + way))
        slots.append((work, sends))
    return slots


def on_device(patches, text, lengths, cotangent, wide, tall, gain, shift):
    total = patches.shape[0]
    rows = total // MICRO
    shards = lax.axis_size(DP)
    share = D // shards
    in_ring = share % 16 == 0 and shards % 2 == 0 and D % (2 * FF // shards) == 0
    wide, tall, gain, shift = wide[0], tall[0], gain[0], shift[0]
    anywhere = pl.BlockSpec(memory_space=pl.ANY)
    in_vmem = pl.BlockSpec(memory_space=pltpu.VMEM)
    in_smem = pl.BlockSpec(memory_space=pltpu.SMEM)
    specs = [in_smem] + [anywhere] * 3 + [in_vmem] * 6 + [anywhere] * 4 + [in_vmem] + [anywhere] * 4 + [in_vmem] * 5
    shapes = [
        jax.ShapeDtypeStruct((SLOTS, total, D), BF),
        jax.ShapeDtypeStruct((total, D), F32),
        jax.ShapeDtypeStruct((total, D), BF),
        jax.ShapeDtypeStruct((total, D), F32),
        jax.ShapeDtypeStruct((rows, D), BF),
        jax.ShapeDtypeStruct((8, D), F32),
        jax.ShapeDtypeStruct(wide.shape, BF),
        jax.ShapeDtypeStruct(tall.shape, BF),
        jax.ShapeDtypeStruct((rows, FF), BF),
    ]
    state, messages, smalls, done, before, fetched = [None] * 4, [None, None], [], None, {}, None
    slots = schedule()
    for k, (work, sends) in enumerate(slots):
        now, old = {name for name, _ in work.values()}, {name for name, _ in before.values()}

        def given(value, *names):
            return value if now & set(names) else None

        operands = [
            given(lengths, EARLY, DECODE_MLP),
            given(patches, ENCODE),
            given(text, EARLY, LATE),
            given(cotangent, DECODE_MLP),
            wide, tall, gain, shift,
            given(messages[-2], ENCODE_MLP, CROSS, DECODE_MLP, CROSS_BACK, ENCODE_MLP_BACK, ENCODE_BACK),
            done if old - {EARLY, LATE} else None,
            *state,
            given(fetched, *AHEAD),
        ]
        after_this = slots[k + 1][0] if k + 1 < len(slots) else {}
        coming = {at: (name, m) for at, (name, m) in after_this.items() if name in AHEAD}
        results = [True] * 4 + [bool(now - {EARLY, LATE}), bool(now & {DECODE_MLP, ENCODE_MLP_BACK, ENCODE_BACK, LATE})]
        results += [k == 0] * 2 + [bool(coming)]
        present = tuple(value is not None for value in operands) + tuple(results)
        places = [i for i, value in enumerate(operands) if value is not None]
        merged = in_ring and k + 1 == len(slots)
        more = share_shapes(shards, FF // shards) if merged else []
        values = pl.pallas_call(
            functools.partial(slot_kernel, work, before, coming, shards if merged else 0, rows, present),
            out_shape=tuple(shape for shape, here in zip(shapes, results) if here) + tuple(more),
            in_specs=[anywhere if k == 0 and i in (4, 5) else specs[i] for i in places],
            out_specs=[spec for spec, here in zip(specs[15:], results) if here] + [in_vmem] * len(more),
            input_output_aliases={places.index(10 + i): i for i in range(4)} if k else {},
            scratch_shapes=[
                pltpu.VMEM((rows, FF), BF),
                pltpu.VMEM((rows, FF), BF),
                pltpu.VMEM((rows, FF), BF),
                pltpu.VMEM((4, rows, D), BF),
                pltpu.VMEM((rows, D), F32),
                pltpu.VMEM((rows, D), F32),
                pltpu.VMEM((rows, D), F32),
                pltpu.SemaphoreType.DMA((48,)),
                *(
                    [
                        pltpu.VMEM((2, total, D), BF),
                        pltpu.VMEM((PANELS, total, D), BF),
                        pltpu.VMEM((2, shards // 2, 2, share, D), BF),
                        pltpu.SemaphoreType.DMA((2 * PANELS,)),
                    ]
                    if merged
                    else []
                ),
            ],
            compiler_params=pltpu.CompilerParams(vmem_limit_bytes=LAST_LIMIT if merged else VMEM_LIMIT if k else FIRST_LIMIT, has_side_effects=True),
            cost_estimate=pl.CostEstimate(flops=9_000_000_000, bytes_accessed=4_000_000, transcendentals=0),
            name=f"slot_{k}",
        )(*(operands[i] for i in places))
        state, rest = list(values[:4]), list(values[4:])
        done = rest.pop(0) if results[4] else None
        if results[5]:
            smalls.append(rest.pop(0))
        if k == 0:
            wide, tall = rest
        fetched = rest[-1] if coming else None
        wide_half = rest
        messages.append(lax.ppermute(done, SECTION, sends) if sends else None)
        before = work
    kept, _, out, grads = state

    little = sum(smalls)
    high = little.astype(BF)
    little = jnp.concatenate([high, (little - high.astype(F32)).astype(BF)], axis=0)
    if in_ring:
        mine, high, low = ring_scatter(wide_half, kept, little, shards)
        wide_grad = jnp.concatenate([mine[p * share : (p + 1) * share] for p in range(PANELS)], axis=1)
        tall_grad = jnp.concatenate([low, high[:-16]], axis=0)
        little = high[-16:]
    else:
        parts = [weight_part(i, kept) for i in range(2 * PANELS)]
        wide_grad = lax.psum_scatter(jnp.concatenate(parts[:PANELS], axis=1), DP, scatter_dimension=0, tiled=True)
        tall_grad = lax.psum_scatter(jnp.concatenate(parts[PANELS:], axis=0), DP, scatter_dimension=0, tiled=True)
        little = lax.psum(little, DP)
    little = little[:4].astype(F32) + little[8:12].astype(F32)
    little = lax.dynamic_slice_in_dim(little, lax.axis_index(DP) * share, share, axis=1)
    return (
        out[None],
        grads[None],
        wide_grad.astype(F32)[None],
        tall_grad.astype(F32)[None],
        little[None, :2],
        little[None, 2:],
    )


def solution(mesh):
    return jax.shard_map(
        on_device,
        mesh=mesh,
        in_specs=(
            P(DP, None),
            P(DP, None),
            P(DP),
            P(DP, None),
            P(SECTION, None, None),
            P(SECTION, None, None),
            P(SECTION, None, None),
            P(SECTION, None, None),
        ),
        out_specs=(
            P(SECTION, DP, None),
            P(SECTION, DP, None),
            P(SECTION, DP, None),
            P(SECTION, DP, None),
            P(SECTION, None, DP),
            P(SECTION, None, DP),
        ),
        check_vma=False,
    )
```

```python
import functools

import jax
import jax.numpy as jnp
from jax import lax
from jax.experimental import pallas as pl
from jax.experimental.pallas import tpu as pltpu
from jax.sharding import PartitionSpec as P

D = 768
HEADS = 12
FF = 3072
HEAD_DIM = 64
PREFIX = 64
PANELS = FF // D
GROUP = 4
LANES = GROUP * HEAD_DIM
GROUPS = HEADS // GROUP
EPS = 1e-05
NEG = -1e30
SCALE = HEAD_DIM ** (-0.5)
MICRO = 4
SLOTS = 15
VMEM_LIMIT = 24 * 1024 * 1024
FIRST_LIMIT = 38 * 1024 * 1024
LAST_LIMIT = 29 * 1024 * 1024
WEIGHT_LIMIT = 32 * 1024 * 1024
BF = jnp.bfloat16
F32 = jnp.float32

SECTION, DP = "section", "dp"
ENCODE, ENCODE_MLP, CROSS, DECODE_MLP, CROSS_BACK, ENCODE_MLP_BACK, ENCODE_BACK, EARLY, LATE = range(9)


class Enc:
    u, q, k, v, p, att, gfirst, gemb, x = range(9)


class Mlp:
    u, x, gb, a, gh = 0, 1, 2, 3, 7


class Dec:
    u, q, k, v, p, att, c, qc, mem, kc, vc, pc, cross, gsec, gmid = range(15)


AHEAD = {
    CROSS_BACK: (Dec.qc, Dec.kc, Dec.vc, Dec.pc),
    ENCODE_MLP_BACK: (Mlp.gh, Mlp.gh + 1, Mlp.gh + 2, Mlp.gh + 3),
    ENCODE_BACK: (Enc.q, Enc.k, Enc.v, Enc.p),
}


def nn(left, right):
    return lax.dot_general(left, right, (((1,), (0,)), ((), ())), preferred_element_type=F32)


def nt(left, right):
    return lax.dot_general(left, right, (((1,), (1,)), ((), ())), preferred_element_type=F32)


def tn(left, right):
    return lax.dot_general(left, right, (((0,), (0,)), ((), ())), preferred_element_type=F32)


def standardize(values):
    center = values - jnp.mean(values, -1, keepdims=True)
    rstd = lax.rsqrt(jnp.mean(center * center, -1, keepdims=True) + EPS)
    return center * rstd, rstd


def norm_back(upstream, unit, rstd, gain_row):
    scaled = upstream * gain_row
    mean_one = jnp.mean(scaled, -1, keepdims=True)
    mean_two = jnp.mean(scaled * unit, -1, keepdims=True)
    grad = rstd * (scaled - mean_one - unit * mean_two)
    return grad, jnp.sum(upstream * unit, 0, keepdims=True), jnp.sum(upstream, 0, keepdims=True)


def gelu_pair(hidden):
    c = 0.7978845608028654
    square = hidden * hidden
    t = jnp.tanh(hidden * (c + (c * 0.044715) * square))
    half = 0.5 + 0.5 * t
    active = hidden * half
    slope = half + active * (1.0 - t) * (c + (3.0 * c * 0.044715) * square)
    return active, slope


def block_diagonal(rows):
    tiled = jnp.concatenate([rows] * GROUP, axis=0)
    at_row = lax.broadcasted_iota(jnp.int32, tiled.shape, 0) // HEAD_DIM
    at_lane = lax.broadcasted_iota(jnp.int32, tiled.shape, 1) // HEAD_DIM
    return jnp.where(at_row == at_lane, tiled, jnp.zeros_like(tiled))


def head_rows(pairs):
    low = lax.broadcasted_iota(jnp.int32, (PREFIX, 2 * HEAD_DIM), 1) < HEAD_DIM
    return jnp.concatenate([jnp.where(low, p[:PREFIX], p[PREFIX:]) for p in pairs], axis=1)


def units(count):
    return [
        (slice(b * PREFIX, (b + 1) * PREFIX), slice(g * LANES, (g + 1) * LANES)) for b in range(count) for g in range(GROUPS)
    ]


def pair_product(left, right):
    return head_rows([tn(left[:, i : i + 128], right[:, i : i + 128]) for i in range(0, LANES, 128)])


def attend(count, q_ref, k_ref, v_ref, p_ref, out_ref, length_of):
    at = units(count)
    scores = [nt(k_ref[u], block_diagonal(q_ref[u])) * SCALE for u in at]
    if length_of is not None:
        key_at = lax.broadcasted_iota(jnp.int32, (PREFIX, LANES), 0)
        query_at = lax.broadcasted_iota(jnp.int32, (PREFIX, LANES), 1) % PREFIX
        allowed = [(key_at <= query_at) & (key_at < length_of(b)) for b in range(count)]
        scores = [jnp.where(allowed[i // GROUPS], values, NEG) for i, values in enumerate(scores)]
    probs = []
    for u, values in zip(at, scores):
        e = jnp.exp(values - jnp.max(values, 0, keepdims=True))
        probs.append((e * (1.0 / jnp.sum(e, 0, keepdims=True))).astype(BF))
        p_ref[u] = probs[-1]
    for u, p in zip(at, probs):
        out_ref[u] = pair_product(p, v_ref[u]).astype(BF)


def attend_back(count, q_ref, k_ref, v_ref, p_ref, up_ref, gq_ref, gk_ref, gv_ref):
    at = units(count)
    ups = [block_diagonal(up_ref[u]) for u in at]
    grads = [nt(v_ref[u], up) for u, up in zip(at, ups)]
    for u, up in zip(at, ups):
        gv_ref[u] = nn(p_ref[u], up).astype(BF)
    scores = []
    for u, grad in zip(at, grads):
        p = p_ref[u].astype(F32)
        scores.append((p * (grad - jnp.sum(grad * p, 0, keepdims=True))).astype(BF))
    for u, grad in zip(at, scores):
        gk_ref[u] = (nn(grad, block_diagonal(q_ref[u])) * SCALE).astype(BF)
    for u, grad in zip(at, scores):
        gq_ref[u] = (pair_product(grad, k_ref[u]) * SCALE).astype(BF)


class Copies:
    def __init__(self, sems):
        self.sems, self.used, self.stores, self.sizes = sems, 0, [], []

    def start(self, source, target):
        copy = pltpu.make_async_copy(source, target, self.sems.at[self.used])
        self.used += 1
        copy.start()
        return copy

    def store(self, source, target):
        self.sizes.append((self.used, source.dtype))
        self.stores.append(self.start(source, target))

    def finish(self):
        for copy in self.stores:
            copy.wait()
        self.stores = []


def slot_kernel(work, before, coming, shards, rows, present, *refs):
    taken = iter(refs)
    given = [next(taken) if here else None for here in present]
    lengths, patches, text, cotangent, wide, tall, norms, message, done = given[:9]
    gain, shift = norms.at[:2], norms.at[2:]
    fetched = given[13]
    kept, kept32, out, grads, sent, small, wide_out, tall_out, ahead = given[14:]
    first = wide_out is not None
    if shards:
        keep, *give = (next(taken) for _ in range(1 + shards // 2))
        *taken, left_v, right_v, done_v, weight_sems = taken
    big_a, big_b, big_c, one, f32_a, f32_b, f32_c, sems = taken
    section = lax.axis_index(SECTION)
    seqs = rows // PREFIX

    def panel(big, p):
        return big.at[:, p * D : (p + 1) * D]

    def norm_rows(at):
        return gain[at : at + 1, :], shift[at : at + 1, :]

    def put_small(early, late):
        for i, row in enumerate((early[0], late[0], early[1], late[1])):
            small[i : i + 1, :] = small[i : i + 1, :] + row

    def fetch_ahead(cp, name, m):
        mine = slice(m * rows, (m + 1) * rows)
        for p, place in enumerate(AHEAD[name]):
            cp.store(kept.at[place, mine], panel(ahead, p))

    def finish_before(cp, name, m):
        mine = slice(m * rows, (m + 1) * rows)
        if name in (ENCODE, ENCODE_MLP, CROSS):
            cp.store(done, out.at[mine])
        if name in (DECODE_MLP, ENCODE_MLP_BACK, ENCODE_BACK):
            if name == ENCODE_BACK:
                cp.store(done, kept.at[Enc.gemb, mine])
            f32_c[...] = done[...].astype(F32)
            cp.store(f32_c, grads.at[mine])

    def encode(cp, m, loads=None):
        mine = slice(m * rows, (m + 1) * rows)
        (gain_0, shift_0), (gain_1, shift_1) = norm_rows(0), norm_rows(1)
        if first:
            for p in range(PANELS):
                cols = slice(p * D, (p + 1) * D)
                for copy in loads[p]:
                    copy.wait()
                part = nn(big_a[:, cols], tall[cols, :])
                f32_a[...] = part if p == 0 else f32_a[...] + part
            for p in range(PANELS):
                cp.store(panel(big_a, p), kept.at[Enc.x + p, mine])
            for copy in loads[PANELS]:
                copy.wait()
        else:
            load = cp.start(patches.at[mine], big_a)
            load.wait()
            for p in range(PANELS):
                cp.store(panel(big_a, p), kept.at[Enc.x + p, mine])
            f32_a[...] = nn(big_a[...], tall[...])
        cp.store(f32_a, kept32.at[mine])
        stream = standardize(f32_a[...])[0] * gain_0 + shift_0
        f32_b[...] = stream
        one[0] = (standardize(stream)[0] * gain_1 + shift_1).astype(BF)
        cp.store(one.at[0], kept.at[Enc.u, mine])
        for p in range(3):
            cols = slice(p * D, (p + 1) * D)
            big_b[:, cols] = nn(one[0], wide[:, cols]).astype(BF)
            cp.store(panel(big_b, p), kept.at[Enc.q + p, mine])
        attend(seqs, *(panel(big_b, p) for p in range(4)), one.at[1], None)
        cp.store(panel(big_b, 3), kept.at[Enc.p, mine])
        cp.store(one.at[1], kept.at[Enc.att, mine])
        sent[...] = (f32_b[...] + nn(one[1], wide[:, 3 * D :])).astype(BF)

    def encode_back(cp, m, hook=None):
        mine = slice(m * rows, (m + 1) * rows)
        load_embedded = cp.start(kept32.at[mine], f32_a)
        if hook:
            hook()
        cp.store(message, kept.at[Enc.gfirst, mine])
        (gain_0, shift_0), (gain_1, shift_1) = norm_rows(0), norm_rows(1)
        one[0] = nt(message[...], wide[:, 3 * D :]).astype(BF)
        load_embedded.wait()
        unit_0, rstd_0 = standardize(f32_a[...])
        f32_a[...] = unit_0
        unit_1, rstd_1 = standardize(unit_0 * gain_0 + shift_0)
        f32_b[...] = unit_1
        attend_back(seqs, *(panel(fetched, p) for p in range(4)), one.at[0], *(panel(big_a, p) for p in range(3)))
        for p in range(3):
            cp.store(panel(big_a, p), kept.at[Enc.q + p, mine])
        upstream = nt(big_a[:, : 3 * D], wide[:, : 3 * D])
        grad, *late = norm_back(upstream, f32_b[...], rstd_1, gain_1)
        grad, *early = norm_back(grad + message[...].astype(F32), f32_a[...], rstd_0, gain_0)
        sent[...] = grad.astype(BF)
        put_small(early, late)
        if hook:
            cp.store(sent, kept.at[Enc.gemb, mine])
            f32_b[...] = sent[...].astype(F32)
            cp.store(f32_b, grads.at[mine])

    def mlp_forward(cp, mine, keep):
        gain_0, shift_0 = norm_rows(0)
        unit, rstd = standardize(message[...].astype(F32))
        if not keep:
            f32_b[...] = unit
        one[0] = (unit * gain_0 + shift_0).astype(BF)
        cp.store(one.at[0], kept.at[Mlp.u, mine])
        for p in range(PANELS):
            cols = slice(p * D, (p + 1) * D)
            active, slope = gelu_pair(nn(one[0], wide[:, cols]))
            big_a[:, cols] = active.astype(BF)
            big_b[:, cols] = slope.astype(BF)
            cp.store(panel(big_a, p), kept.at[Mlp.a + p, mine])
            if keep:
                cp.store(panel(big_b, p), kept.at[Mlp.gh + p, mine])
        return message[...].astype(F32) + nn(big_a[...], tall[...]), rstd

    def mlp_backward(cp, mine, upstream, unit, rstd, loads, slopes):
        grad, *late = norm_back(upstream, unit, rstd, norm_rows(1)[0])
        f32_a[...] = grad
        one[1] = grad.astype(BF)
        cp.store(one.at[1], kept.at[Mlp.gb, mine])
        for copy in loads:
            copy.wait()
        for p in range(PANELS):
            cols = slice(p * D, (p + 1) * D)
            back = nt(one[1], tall[cols, :])
            big_c[:, cols] = (back * slopes[:, cols].astype(F32)).astype(BF)
            cp.store(panel(big_c, p), kept.at[Mlp.gh + p, mine])
        return nt(big_c[...], wide[...]), late

    def encode_mlp(cp, m):
        mine = slice(m * rows, (m + 1) * rows)
        cp.store(message, kept.at[Mlp.x, mine])
        summed, _ = mlp_forward(cp, mine, True)
        f32_a[...] = summed
        cp.store(f32_a, kept32.at[mine])
        gain_1, shift_1 = norm_rows(1)
        sent[...] = (standardize(f32_a[...])[0] * gain_1 + shift_1).astype(BF)

    def encode_mlp_back(cp, m):
        mine = slice(m * rows, (m + 1) * rows)
        load_summed = cp.start(kept32.at[mine], f32_a)
        loads = [cp.start(kept.at[Mlp.x, mine], one.at[0])]
        load_summed.wait()
        unit, rstd = standardize(f32_a[...])
        upstream, late = mlp_backward(cp, mine, message[...].astype(F32), unit, rstd, loads, fetched)
        unit, rstd = standardize(one[0].astype(F32))
        grad, *early = norm_back(upstream, unit, rstd, norm_rows(0)[0])
        sent[...] = (grad + f32_a[...]).astype(BF)
        put_small(early, late)

    def decode_mlp(cp, m):
        mine = slice(m * rows, (m + 1) * rows)
        load = cp.start(cotangent.at[mine], one.at[2])
        summed, rstd_0 = mlp_forward(cp, mine, False)
        gain_1, shift_1 = norm_rows(1)
        unit, rstd = standardize(summed)
        one[3] = (unit * gain_1 + shift_1).astype(BF)
        cp.store(one.at[3], out.at[mine])
        load.wait()
        place = lax.broadcasted_iota(jnp.int32, (PREFIX, D), 0)
        masked = []
        for b in range(seqs):
            at = slice(b * PREFIX, (b + 1) * PREFIX)
            masked.append(jnp.where(place < lengths[m * seqs + b], one[2, at, :].astype(F32), 0.0))
        upstream, late = mlp_backward(cp, mine, jnp.concatenate(masked, axis=0), unit, rstd, [], big_b)
        grad, *early = norm_back(upstream, f32_b[...], rstd_0, norm_rows(0)[0])
        sent[...] = (grad + f32_a[...]).astype(BF)
        put_small(early, late)

    def decode_early(cp, m):
        if m < MICRO - 2:
            decode_early_one(cp, m)
            return

        def both(i, carry):
            own = Copies(sems)
            decode_early_one(own, m + i)
            own.finish()
            return carry

        lax.fori_loop(0, 2, both, 0)

    def decode_early_one(cp, m):
        mine = pl.ds(pl.multiple_of(m * rows, rows), rows)
        load = cp.start(text.at[mine], one.at[3])
        (gain_0, shift_0), (gain_1, shift_1) = norm_rows(0), norm_rows(1)
        load.wait()
        one[0] = (standardize(one[3].astype(F32))[0] * gain_0 + shift_0).astype(BF)
        cp.store(one.at[0], kept.at[Dec.u, mine])
        for p in range(3):
            cols = slice(p * D, (p + 1) * D)
            big_b[:, cols] = nn(one[0], wide[:, cols]).astype(BF)
            cp.store(panel(big_b, p), kept.at[Dec.q + p, mine])
        attend(seqs, *(panel(big_b, p) for p in range(4)), one.at[1], lambda b: lengths[m * seqs + b])
        cp.store(panel(big_b, 3), kept.at[Dec.p, mine])
        cp.store(one.at[1], kept.at[Dec.att, mine])
        f32_a[...] = one[3].astype(F32) + nn(one[1], wide[:, 3 * D :])
        cp.store(f32_a, kept32.at[mine])
        one[2] = (standardize(f32_a[...])[0] * gain_1 + shift_1).astype(BF)
        cp.store(one.at[2], kept.at[Dec.c, mine])
        big_c[:, :D] = nn(one[2], tall[:D, :]).astype(BF)
        cp.store(panel(big_c, 0), kept.at[Dec.qc, mine])

    def decode_cross(cp, m):
        mine = slice(m * rows, (m + 1) * rows)
        load_query = cp.start(kept.at[Dec.qc, mine], panel(big_a, 0))
        load_middle = cp.start(kept32.at[mine], f32_a)
        cp.store(message, kept.at[Dec.mem, mine])
        for p in (1, 2):
            cols = slice(p * D, (p + 1) * D)
            big_a[:, cols] = nn(message[...], tall[cols, :]).astype(BF)
            cp.store(panel(big_a, p), kept.at[Dec.kc + p - 1, mine])
        load_query.wait()
        attend(seqs, *(panel(big_a, p) for p in range(4)), one.at[1], None)
        cp.store(panel(big_a, 3), kept.at[Dec.pc, mine])
        cp.store(one.at[1], kept.at[Dec.cross, mine])
        load_middle.wait()
        sent[...] = (f32_a[...] + nn(one[1], tall[3 * D :, :])).astype(BF)

    def decode_cross_back(cp, m):
        mine = slice(m * rows, (m + 1) * rows)
        places = AHEAD[CROSS_BACK]
        cp.store(message, kept.at[Dec.gsec, mine])
        one[0] = nt(message[...], tall[3 * D :, :]).astype(BF)
        attend_back(seqs, *(panel(fetched, p) for p in range(4)), one.at[0], *(panel(big_c, p) for p in range(3)))
        for p in range(3):
            cp.store(panel(big_c, p), kept.at[places[p], mine])
        back = nt(big_c[:, D : 2 * D], tall[D : 2 * D, :]) + nt(big_c[:, 2 * D : 3 * D], tall[2 * D : 3 * D, :])
        sent[...] = back.astype(BF)

    def decode_late(cp, m, hook=None):
        mine = slice(m * rows, (m + 1) * rows)
        load_query = cp.start(kept.at[Dec.qc, mine], one.at[0])
        load_middle = cp.start(kept32.at[mine], f32_a)
        load_second = cp.start(kept.at[Dec.gsec, mine], one.at[1])
        loads = [cp.start(kept.at[Dec.q + p, mine], panel(big_b, p)) for p in range(4)]
        load_text = cp.start(text.at[mine], one.at[3])
        if hook:
            hook()
        load_query.wait()
        upstream = nt(one[0], tall[:D, :])
        load_middle.wait()
        load_second.wait()
        grad, *late = norm_back(upstream, *standardize(f32_a[...]), norm_rows(1)[0])
        f32_b[...] = grad + one[1].astype(F32)
        one[2] = f32_b[...].astype(BF)
        cp.store(one.at[2], kept.at[Dec.gmid, mine])
        one[0] = nt(one[2], wide[:, 3 * D :]).astype(BF)
        for copy in loads:
            copy.wait()
        attend_back(seqs, *(panel(big_b, p) for p in range(4)), one.at[0], *(panel(big_a, p) for p in range(3)))
        for p in range(3):
            cp.store(panel(big_a, p), kept.at[Dec.q + p, mine])
        upstream = nt(big_a[:, : 3 * D], wide[:, : 3 * D])
        load_text.wait()
        grad, *early = norm_back(upstream, *standardize(one[3].astype(F32)), norm_rows(0)[0])
        f32_a[...] = grad + f32_b[...]
        cp.store(f32_a, grads.at[mine])
        put_small(early, late)

    steps = {
        ENCODE: encode, ENCODE_MLP: encode_mlp, CROSS: decode_cross, DECODE_MLP: decode_mlp, CROSS_BACK: decode_cross_back,
        ENCODE_MLP_BACK: encode_mlp_back, ENCODE_BACK: encode_back, EARLY: decode_early, LATE: decode_late,
    }
    def last_slot():
        chips, held, left_over = shards // 2, kept.shape[1] - rows, {}
        for at, (left, right) in enumerate(weight_operands()):

            @pl.when(section == at)
            def _():
                cp, loads = Copies(sems), Copies(weight_sems)
                here = slice(0, held) if at in work else slice(0, held + rows)
                copies = []

                def hook():
                    for p in range(PANELS):
                        copies.append(loads.start(kept.at[right[p], here], right_v.at[p, here]))
                        if p == 0 or left[p] != left[p - 1]:
                            copies.append(loads.start(kept.at[left[p]], left_v.at[0 if p == 0 else 1]))

                if at in before:
                    finish_before(cp, *before[at])
                if at in work:
                    name, m = work[at]
                    steps[name](cp, m, hook)
                    for p in range(PANELS - 1):
                        right_v[p, held:] = panel(big_a, p)[...]
                    right_v[PANELS - 1, held:] = message[...] if at == 0 else one[2]
                else:
                    hook()
                for copy in copies:
                    copy.wait()
                left_over[at] = cp.sizes

        alone = section % 2 == 0
        for p in range(PANELS):
            from_left = jnp.where(alone, 1, 0) if p == PANELS - 1 else 0
            done_v[p % 2] = tn(left_v[from_left], right_v[p]).astype(BF).reshape(chips, 2, D // shards, D)
            rows_of_part = slice(p * D // shards, (p + 1) * D // shards)
            put_shares(shards, keep, give, rows_of_part, lambda chip, core: done_v[p % 2, chip, core])
        for at, stores in left_over.items():

            @pl.when(section == at)
            def _():
                for number, dtype in stores:
                    pair = (f32_a, f32_b) if dtype == F32 else (one.at[0], one.at[1])
                    pltpu.make_async_copy(*pair, sems.at[number]).wait()

    if small is not None:
        small[...] = jnp.zeros_like(small)
    if first:
        wide_in, tall_in, wide, tall = wide, tall, wide_out, tall_out

        def weight_loads(cp):
            for p in range(PANELS):
                at = slice(p * D, (p + 1) * D)
                yield [cp.start(tall_in.at[at], tall.at[at])]
            yield [cp.start(wide_in.at[:, p * D : (p + 1) * D], wide.at[:, p * D : (p + 1) * D]) for p in range(PANELS)]

        @pl.when(section == 0)
        def _():
            cp = Copies(sems)
            loads = []
            for p, more in enumerate(weight_loads(cp)):
                if p < PANELS:
                    more.append(cp.start(patches.at[:rows, p * D : (p + 1) * D], panel(big_a, p)))
                loads.append(more)
            encode(cp, 0, loads)
            cp.finish()

        @pl.when(section != 0)
        def _():
            for loads in list(weight_loads(Copies(sems))):
                for copy in loads:
                    copy.wait()

        return
    if shards:
        last_slot()
        return
    for at in sorted(set(work) | set(before) | set(coming)):

        @pl.when(section == at)
        def _():
            cp = Copies(sems)
            if at in coming:
                fetch_ahead(cp, *coming[at])
            if at in before:
                finish_before(cp, *before[at])
            if at in work:
                name, m = work[at]
                steps[name](cp, m)
            cp.finish()


def weight_operands():
    e, m, d = Enc, Mlp, Dec
    mlp = ([m.u] * 4 + [m.a + p for p in range(4)], [m.gh + p for p in range(4)] + [m.gb] * 4)
    encode = ([e.u] * 3 + [e.att] + [e.x + p for p in range(4)], [e.q, e.k, e.v, e.gfirst] + [e.gemb] * 4)
    decode = ([d.u] * 3 + [d.att, d.c, d.mem, d.mem, d.cross], [d.q, d.k, d.v, d.gmid, d.qc, d.kc, d.vc, d.gsec])
    return encode, mlp, decode, mlp


def by_section(values):
    section, chosen = lax.axis_index(SECTION), values[0]
    for at, value in enumerate(values[1:], 1):
        if value != values[0]:
            chosen = jnp.where(section == at, value, chosen)
    return chosen


def put_shares(shards, keep, give, rows, block):
    chips = shards // 2
    chip, core = lax.axis_index(DP) // 2, lax.axis_index(DP) % 2
    for step in range(chips):
        at = (chip + 2 * chips - 1 - step) % chips
        keep[step, rows] = block(at, core)
        give[step][rows] = block(at, 1 - core)


def tall_kernel(shards, kept, extra, keep, *refs):
    *give, left_v, right_v, done_v, sems = refs
    section = lax.axis_index(SECTION)
    lefts = [[t[0][PANELS + p] for t in weight_operands()] for p in range(PANELS)]
    rights = [[t[1][PANELS + p] for t in weight_operands()] for p in range(PANELS)]
    alone = section == 2
    share = FF // shards
    here = D // share // 2

    def operands(p, begin):
        left = pltpu.make_async_copy(kept.at[by_section(lefts[p])], left_v.at[p], sems.at[0, p])
        right = pltpu.make_async_copy(kept.at[by_section(rights[p])], right_v.at[p], sems.at[1, p])
        for copy, always in ((left, True), (right, p == 0)):
            act = copy.start if begin else copy.wait
            act() if always else pl.when(alone)(act)

    for p in range(PANELS):
        operands(p, True)
    for p in range(PANELS):
        operands(p, False)
        done = tn(left_v[p], right_v[jnp.where(alone, p, 0) if p else 0]).astype(BF)
        done_v[p * here : (p + 1) * here] = done.reshape(here, 2, share, D)
    put_shares(shards, keep, give, slice(0, share), lambda chip, core: done_v[chip, core])
    for at in range(shards // 2):
        keep[at, share:] = extra[...]
        give[at][share:] = extra[...]


def share_shapes(shards, rows):
    return [jax.ShapeDtypeStruct((shards // 2, rows, D), BF)] + [jax.ShapeDtypeStruct((rows, D), BF)] * (shards // 2)


def tall_half(shards, kept, extra):
    total = kept.shape[1]
    in_vmem = pl.BlockSpec(memory_space=pltpu.VMEM)
    shapes = share_shapes(shards, FF // shards + extra.shape[0])
    flops = 2 * PANELS * D * D * total
    return pl.pallas_call(
        functools.partial(tall_kernel, shards),
        out_shape=tuple(shapes),
        in_specs=[pl.BlockSpec(memory_space=pl.ANY), in_vmem],
        out_specs=(in_vmem,) * len(shapes),
        scratch_shapes=[
            pltpu.VMEM((PANELS, total, D), BF),
            pltpu.VMEM((PANELS, total, D), BF),
            pltpu.VMEM((shards // 2, 2, FF // shards, D), BF),
            pltpu.SemaphoreType.DMA((2, PANELS)),
        ],
        cost_estimate=pl.CostEstimate(flops=flops, bytes_accessed=flops // total, transcendentals=0),
        compiler_params=pltpu.CompilerParams(vmem_limit_bytes=WEIGHT_LIMIT, has_side_effects=True),
        name="tall_half",
    )(kept, extra)


def after(value, other):
    return lax.optimization_barrier((value, other))[0]


def ring_scatter(wide_half, kept, little, shards, finish):
    chips, rows = shards // 2, FF // shards
    flip = [(d, d ^ 1) for d in range(shards)]
    onward = [(d, (d + 2) % shards) for d in range(shards)]
    sent = None

    def exchange(keep, *give):
        return [(keep[at], lax.ppermute(part, DP, flip)) for at, part in enumerate(give)]

    def add(parts, running, piece=slice(None), whole=False):
        keep, got = parts
        if sent is not None and running is None:
            got = after(got, sent)
        elif sent is not None:
            running = after(running, sent)
        value = keep[piece].astype(F32) + got[piece].astype(F32)
        if running is None:
            return value
        return value + (running[piece] if whole else running).astype(F32)

    def send(value):
        nonlocal sent
        sent = value.astype(BF)
        return lax.ppermute(sent, DP, onward)

    wide = exchange(*wide_half)
    running = send(add(wide[0], None))
    tall = exchange(*tall_half(shards, after(kept, sent), little))
    cut = (rows + little.shape[0]) * 3 // 8 // 16 * 16
    pieces = [slice(cut, rows + little.shape[0]), slice(0, cut)]
    running = send(add(wide[1], running))
    low = [send(add(tall[0], None))] * len(pieces)
    for step in range(1, chips - 1):
        if step + 1 < chips - 1:
            running = send(add(wide[step + 1], running))
        else:
            wide = sent = add(wide[-1], running)
        low = [send(add(tall[step], got, piece, step == 1)) for piece, got in zip(pieces, low)]
    high = add(tall[-1], low[0], pieces[0])
    small = sent = finish(high[-little.shape[0] :])
    return wide, high, add(tall[-1], low[1], pieces[1]), small


def weight_part(i, kept):
    lefts, rights = ([t[side][i] for t in weight_operands()] for side in (0, 1))
    left, right = (lax.dynamic_index_in_dim(kept, by_section(values), 0, keepdims=False) for values in (lefts, rights))
    return tn(left, right).astype(BF)


def schedule():
    plan = [(0, 0, ENCODE, 1), (1, 2, ENCODE_MLP, 1), (2, 4, CROSS, 1), (3, 6, DECODE_MLP, -1), (2, 8, CROSS_BACK, -1),
            (1, 10, ENCODE_MLP_BACK, -1), (0, 12, ENCODE_BACK, 0), (2, 1, EARLY, 0), (2, 12, LATE, 0)]
    slots = []
    for k in range(MICRO + 12):
        work, sends = {}, []
        for section, begin, name, way in plan:
            if 0 <= k - begin < MICRO - (name == EARLY):
                assert section not in work
                work[section] = (name, k - begin)
                if way:
                    sends.append((section, section + way))
        slots.append((work, sends))
    return slots


def on_device(patches, text, lengths, cotangent, wide, tall, gain, shift):
    total = patches.shape[0]
    rows = total // MICRO
    shards = lax.axis_size(DP)
    share = D // shards
    in_ring = share % 16 == 0 and shards % 2 == 0 and D % (2 * FF // shards) == 0
    wide, tall, norms = wide[0], tall[0], jnp.concatenate([gain[0], shift[0]], axis=0)
    anywhere = pl.BlockSpec(memory_space=pl.ANY)
    in_vmem = pl.BlockSpec(memory_space=pltpu.VMEM)
    in_smem = pl.BlockSpec(memory_space=pltpu.SMEM)
    specs = [in_smem] + [anywhere] * 3 + [in_vmem] * 5 + [anywhere] * 4 + [in_vmem] + [anywhere] * 4 + [in_vmem] * 5
    shapes = [
        jax.ShapeDtypeStruct((SLOTS, total, D), BF),
        jax.ShapeDtypeStruct((total, D), F32),
        jax.ShapeDtypeStruct((total, D), BF),
        jax.ShapeDtypeStruct((total, D), F32),
        jax.ShapeDtypeStruct((rows, D), BF),
        jax.ShapeDtypeStruct((8, D), F32),
        jax.ShapeDtypeStruct(wide.shape, BF),
        jax.ShapeDtypeStruct(tall.shape, BF),
        jax.ShapeDtypeStruct((rows, FF), BF),
    ]
    state, messages, smalls, done, before, fetched = [None] * 4, [None, None], [], None, {}, None
    slots = schedule()
    for k, (work, sends) in enumerate(slots):
        now, old = {name for name, _ in work.values()}, {name for name, _ in before.values()}

        def given(value, *names):
            return value if now & set(names) else None

        operands = [
            given(lengths, EARLY, DECODE_MLP),
            given(patches, ENCODE),
            given(text, EARLY, LATE),
            given(cotangent, DECODE_MLP),
            wide, tall, norms,
            given(messages[-2], ENCODE_MLP, CROSS, DECODE_MLP, CROSS_BACK, ENCODE_MLP_BACK, ENCODE_BACK),
            done if old - {EARLY, LATE} else None,
            *state,
            given(fetched, *AHEAD),
        ]
        after_this = slots[k + 1][0] if k + 1 < len(slots) else {}
        coming = {at: (name, m) for at, (name, m) in after_this.items() if name in AHEAD}
        results = [True] * 4 + [bool(now - {EARLY, LATE}), bool(now & {DECODE_MLP, ENCODE_MLP_BACK, ENCODE_BACK, LATE})]
        results += [k == 0] * 2 + [bool(coming)]
        present = tuple(value is not None for value in operands) + tuple(results)
        places = [i for i, value in enumerate(operands) if value is not None]
        merged = in_ring and k + 1 == len(slots)
        more = share_shapes(shards, FF // shards) if merged else []
        values = pl.pallas_call(
            functools.partial(slot_kernel, work, before, coming, shards if merged else 0, rows, present),
            out_shape=tuple(shape for shape, here in zip(shapes, results) if here) + tuple(more),
            in_specs=[anywhere if k == 0 and i in (4, 5) else specs[i] for i in places],
            out_specs=[spec for spec, here in zip(specs[14:], results) if here] + [in_vmem] * len(more),
            input_output_aliases={places.index(9 + i): i for i in range(4)} if k else {},
            scratch_shapes=[
                pltpu.VMEM((rows, FF), BF),
                pltpu.VMEM((rows, FF), BF),
                pltpu.VMEM((rows, FF), BF),
                pltpu.VMEM((4, rows, D), BF),
                pltpu.VMEM((rows, D), F32),
                pltpu.VMEM((rows, D), F32),
                pltpu.VMEM((rows, D), F32),
                pltpu.SemaphoreType.DMA((48,)),
                *(
                    [
                        pltpu.VMEM((2, total, D), BF),
                        pltpu.VMEM((PANELS, total, D), BF),
                        pltpu.VMEM((2, shards // 2, 2, share, D), BF),
                        pltpu.SemaphoreType.DMA((2 * PANELS,)),
                    ]
                    if merged
                    else []
                ),
            ],
            compiler_params=pltpu.CompilerParams(vmem_limit_bytes=LAST_LIMIT if merged else VMEM_LIMIT if k else FIRST_LIMIT, has_side_effects=True),
            cost_estimate=pl.CostEstimate(flops=9_000_000_000, bytes_accessed=4_000_000, transcendentals=0),
            name=f"slot_{k}",
        )(*(operands[i] for i in places))
        state, rest = list(values[:4]), list(values[4:])
        done = rest.pop(0) if results[4] else None
        if results[5]:
            smalls.append(rest.pop(0))
        if k == 0:
            wide, tall = rest
        fetched = rest[-1] if coming else None
        wide_half = rest
        messages.append(lax.ppermute(done, SECTION, sends) if sends else None)
        before = work
    kept, _, out, grads = state

    little = sum(smalls)
    high = little.astype(BF)
    little = jnp.concatenate([high, (little - high.astype(F32)).astype(BF)], axis=0)

    def norm_grads(sums):
        sums = sums[:4].astype(F32) + sums[8:12].astype(F32)
        sums = lax.dynamic_slice_in_dim(sums, lax.axis_index(DP) * share, share, axis=1)
        return sums[None, :2], sums[None, 2:]

    if in_ring:
        mine, high, low, (gain_grad, shift_grad) = ring_scatter(wide_half, kept, little, shards, norm_grads)
        wide_grad = jnp.concatenate([mine[p * share : (p + 1) * share] for p in range(PANELS)], axis=1)
        tall_grad = jnp.concatenate([low, high[:-16]], axis=0)
    else:
        parts = [weight_part(i, kept) for i in range(2 * PANELS)]
        wide_grad = lax.psum_scatter(jnp.concatenate(parts[:PANELS], axis=1), DP, scatter_dimension=0, tiled=True)
        tall_grad = lax.psum_scatter(jnp.concatenate(parts[PANELS:], axis=0), DP, scatter_dimension=0, tiled=True)
        gain_grad, shift_grad = norm_grads(lax.psum(little, DP))
    return (
        out[None],
        grads[None],
        wide_grad.astype(F32)[None],
        tall_grad.astype(F32)[None],
        gain_grad,
        shift_grad,
    )


def solution(mesh):
    return jax.shard_map(
        on_device,
        mesh=mesh,
        in_specs=(
            P(DP, None),
            P(DP, None),
            P(DP),
            P(DP, None),
            P(SECTION, None, None),
            P(SECTION, None, None),
            P(SECTION, None, None),
            P(SECTION, None, None),
        ),
        out_specs=(
            P(SECTION, DP, None),
            P(SECTION, DP, None),
            P(SECTION, DP, None),
            P(SECTION, DP, None),
            P(SECTION, None, DP),
            P(SECTION, None, DP),
        ),
        check_vma=False,
    )
```

```python
import functools

import jax
import jax.numpy as jnp
from jax import lax
from jax.experimental import pallas as pl
from jax.experimental.pallas import tpu as pltpu
from jax.sharding import PartitionSpec as P

D = 768
HEADS = 12
FF = 3072
HEAD_DIM = 64
PREFIX = 64
PANELS = FF // D
GROUP = 4
LANES = GROUP * HEAD_DIM
GROUPS = HEADS // GROUP
EPS = 1e-05
NEG = -1e30
SCALE = HEAD_DIM ** (-0.5)
MICRO = 4
SLOTS = 15
VMEM_LIMIT = 24 * 1024 * 1024
FIRST_LIMIT = 38 * 1024 * 1024
LAST_LIMIT = 29 * 1024 * 1024
WEIGHT_LIMIT = 32 * 1024 * 1024
BF = jnp.bfloat16
F32 = jnp.float32

SECTION, DP = "section", "dp"
ENCODE, ENCODE_MLP, CROSS, DECODE_MLP, CROSS_BACK, ENCODE_MLP_BACK, ENCODE_BACK, EARLY, LATE = range(9)


class Enc:
    u, q, k, v, p, att, gfirst, gemb, x = range(9)


class Mlp:
    u, x, gb, a, gh = 0, 1, 2, 3, 7


class Dec:
    u, q, k, v, p, att, c, qc, mem, kc, vc, pc, cross, gsec, gmid = range(15)


AHEAD = {
    CROSS_BACK: (Dec.qc, Dec.kc, Dec.vc, Dec.pc),
    ENCODE_MLP_BACK: (Mlp.gh, Mlp.gh + 1, Mlp.gh + 2, Mlp.gh + 3),
    ENCODE_BACK: (Enc.q, Enc.k, Enc.v, Enc.p),
}


def nn(left, right):
    return lax.dot_general(left, right, (((1,), (0,)), ((), ())), preferred_element_type=F32)


def nt(left, right):
    return lax.dot_general(left, right, (((1,), (1,)), ((), ())), preferred_element_type=F32)


def tn(left, right):
    return lax.dot_general(left, right, (((0,), (0,)), ((), ())), preferred_element_type=F32)


def standardize(values):
    center = values - jnp.mean(values, -1, keepdims=True)
    rstd = lax.rsqrt(jnp.mean(center * center, -1, keepdims=True) + EPS)
    return center * rstd, rstd


def norm_back(upstream, unit, rstd, gain_row):
    scaled = upstream * gain_row
    mean_one = jnp.mean(scaled, -1, keepdims=True)
    mean_two = jnp.mean(scaled * unit, -1, keepdims=True)
    grad = rstd * (scaled - mean_one - unit * mean_two)
    return grad, jnp.sum(upstream * unit, 0, keepdims=True), jnp.sum(upstream, 0, keepdims=True)


def gelu_pair(hidden):
    c = 0.7978845608028654
    square = hidden * hidden
    t = jnp.tanh(hidden * (c + (c * 0.044715) * square))
    half = 0.5 + 0.5 * t
    active = hidden * half
    slope = half + active * (1.0 - t) * (c + (3.0 * c * 0.044715) * square)
    return active, slope


def block_diagonal(rows):
    tiled = jnp.concatenate([rows] * GROUP, axis=0)
    at_row = lax.broadcasted_iota(jnp.int32, tiled.shape, 0) // HEAD_DIM
    at_lane = lax.broadcasted_iota(jnp.int32, tiled.shape, 1) // HEAD_DIM
    return jnp.where(at_row == at_lane, tiled, jnp.zeros_like(tiled))


def head_rows(pairs):
    low = lax.broadcasted_iota(jnp.int32, (PREFIX, 2 * HEAD_DIM), 1) < HEAD_DIM
    return jnp.concatenate([jnp.where(low, p[:PREFIX], p[PREFIX:]) for p in pairs], axis=1)


def units(count):
    return [
        (slice(b * PREFIX, (b + 1) * PREFIX), slice(g * LANES, (g + 1) * LANES)) for b in range(count) for g in range(GROUPS)
    ]


def pair_product(left, right):
    return head_rows([tn(left[:, i : i + 128], right[:, i : i + 128]) for i in range(0, LANES, 128)])


def attend(count, q_ref, k_ref, v_ref, p_ref, out_ref, length_of):
    at = units(count)
    scores = [nt(k_ref[u], block_diagonal(q_ref[u])) * SCALE for u in at]
    if length_of is not None:
        key_at = lax.broadcasted_iota(jnp.int32, (PREFIX, LANES), 0)
        query_at = lax.broadcasted_iota(jnp.int32, (PREFIX, LANES), 1) % PREFIX
        allowed = [(key_at <= query_at) & (key_at < length_of(b)) for b in range(count)]
        scores = [jnp.where(allowed[i // GROUPS], values, NEG) for i, values in enumerate(scores)]
    probs = []
    for u, values in zip(at, scores):
        e = jnp.exp(values - jnp.max(values, 0, keepdims=True))
        probs.append((e * (1.0 / jnp.sum(e, 0, keepdims=True))).astype(BF))
        p_ref[u] = probs[-1]
    for u, p in zip(at, probs):
        out_ref[u] = pair_product(p, v_ref[u]).astype(BF)


def attend_back(count, q_ref, k_ref, v_ref, p_ref, up_ref, gq_ref, gk_ref, gv_ref):
    at = units(count)
    ups = [block_diagonal(up_ref[u]) for u in at]
    grads = [nt(v_ref[u], up) for u, up in zip(at, ups)]
    for u, up in zip(at, ups):
        gv_ref[u] = nn(p_ref[u], up).astype(BF)
    scores = []
    for u, grad in zip(at, grads):
        p = p_ref[u].astype(F32)
        scores.append((p * (grad - jnp.sum(grad * p, 0, keepdims=True))).astype(BF))
    for u, grad in zip(at, scores):
        gk_ref[u] = (nn(grad, block_diagonal(q_ref[u])) * SCALE).astype(BF)
    for u, grad in zip(at, scores):
        gq_ref[u] = (pair_product(grad, k_ref[u]) * SCALE).astype(BF)


class Copies:
    def __init__(self, sems):
        self.sems, self.used, self.stores, self.sizes = sems, 0, [], []

    def start(self, source, target):
        copy = pltpu.make_async_copy(source, target, self.sems.at[self.used])
        self.used += 1
        copy.start()
        return copy

    def store(self, source, target):
        self.sizes.append((self.used, source.dtype))
        self.stores.append(self.start(source, target))

    def finish(self):
        for copy in self.stores:
            copy.wait()
        self.stores = []


def slot_kernel(work, before, coming, shards, rows, present, *refs):
    taken = iter(refs)
    given = [next(taken) if here else None for here in present]
    lengths, patches, text, cotangent, wide, tall, norms, message, done = given[:9]
    gain, shift = norms.at[:2], norms.at[2:]
    fetched = given[13]
    kept, kept32, out, grads, sent, small, wide_out, tall_out, ahead = given[14:]
    first = wide_out is not None
    if shards:
        keep, *give = (next(taken) for _ in range(1 + shards // 2))
        *taken, left_v, right_v, done_v, weight_sems = taken
    big_a, big_b, big_c, one, f32_a, f32_b, f32_c, sems = taken
    section = lax.axis_index(SECTION)
    seqs = rows // PREFIX

    def panel(big, p):
        return big.at[:, p * D : (p + 1) * D]

    def norm_rows(at):
        return gain[at : at + 1, :], shift[at : at + 1, :]

    def put_small(early, late):
        for i, row in enumerate((early[0], late[0], early[1], late[1])):
            small[i : i + 1, :] = small[i : i + 1, :] + row

    def fetch_ahead(cp, name, m):
        mine = slice(m * rows, (m + 1) * rows)
        for p, place in enumerate(AHEAD[name]):
            cp.store(kept.at[place, mine], panel(ahead, p))

    def finish_before(cp, name, m):
        mine = slice(m * rows, (m + 1) * rows)
        if name in (ENCODE, ENCODE_MLP, CROSS):
            cp.store(done, out.at[mine])
        if name in (DECODE_MLP, ENCODE_MLP_BACK, ENCODE_BACK):
            if name == ENCODE_BACK:
                cp.store(done, kept.at[Enc.gemb, mine])
            f32_c[...] = done[...].astype(F32)
            cp.store(f32_c, grads.at[mine])

    def encode(cp, m, loads=None):
        mine = slice(m * rows, (m + 1) * rows)
        (gain_0, shift_0), (gain_1, shift_1) = norm_rows(0), norm_rows(1)
        if first:
            for p in range(PANELS):
                cols = slice(p * D, (p + 1) * D)
                for copy in loads[p]:
                    copy.wait()
                part = nn(big_a[:, cols], tall[cols, :])
                f32_a[...] = part if p == 0 else f32_a[...] + part
            for p in range(PANELS):
                cp.store(panel(big_a, p), kept.at[Enc.x + p, mine])
            for copy in loads[PANELS]:
                copy.wait()
        else:
            load = cp.start(patches.at[mine], big_a)
            load.wait()
            for p in range(PANELS):
                cp.store(panel(big_a, p), kept.at[Enc.x + p, mine])
            f32_a[...] = nn(big_a[...], tall[...])
        cp.store(f32_a, kept32.at[mine])
        stream = standardize(f32_a[...])[0] * gain_0 + shift_0
        f32_b[...] = stream
        one[0] = (standardize(stream)[0] * gain_1 + shift_1).astype(BF)
        cp.store(one.at[0], kept.at[Enc.u, mine])
        for p in range(3):
            cols = slice(p * D, (p + 1) * D)
            big_b[:, cols] = nn(one[0], wide[:, cols]).astype(BF)
            cp.store(panel(big_b, p), kept.at[Enc.q + p, mine])
        attend(seqs, *(panel(big_b, p) for p in range(4)), one.at[1], None)
        cp.store(panel(big_b, 3), kept.at[Enc.p, mine])
        cp.store(one.at[1], kept.at[Enc.att, mine])
        sent[...] = (f32_b[...] + nn(one[1], wide[:, 3 * D :])).astype(BF)

    def encode_back(cp, m, hook=None):
        mine = slice(m * rows, (m + 1) * rows)
        load_embedded = cp.start(kept32.at[mine], f32_a)
        if hook:
            hook()
        cp.store(message, kept.at[Enc.gfirst, mine])
        (gain_0, shift_0), (gain_1, shift_1) = norm_rows(0), norm_rows(1)
        one[0] = nt(message[...], wide[:, 3 * D :]).astype(BF)
        load_embedded.wait()
        unit_0, rstd_0 = standardize(f32_a[...])
        f32_a[...] = unit_0
        unit_1, rstd_1 = standardize(unit_0 * gain_0 + shift_0)
        f32_b[...] = unit_1
        attend_back(seqs, *(panel(fetched, p) for p in range(4)), one.at[0], *(panel(big_a, p) for p in range(3)))
        for p in range(3):
            cp.store(panel(big_a, p), kept.at[Enc.q + p, mine])
        upstream = nt(big_a[:, : 3 * D], wide[:, : 3 * D])
        grad, *late = norm_back(upstream, f32_b[...], rstd_1, gain_1)
        grad, *early = norm_back(grad + message[...].astype(F32), f32_a[...], rstd_0, gain_0)
        sent[...] = grad.astype(BF)
        put_small(early, late)
        if m == MICRO - 1:
            cp.store(sent, kept.at[Enc.gemb, mine])
            f32_b[...] = sent[...].astype(F32)
            cp.store(f32_b, grads.at[mine])

    def mlp_forward(cp, mine, keep):
        gain_0, shift_0 = norm_rows(0)
        unit, rstd = standardize(message[...].astype(F32))
        if not keep:
            f32_b[...] = unit
        one[0] = (unit * gain_0 + shift_0).astype(BF)
        cp.store(one.at[0], kept.at[Mlp.u, mine])
        for p in range(PANELS):
            cols = slice(p * D, (p + 1) * D)
            active, slope = gelu_pair(nn(one[0], wide[:, cols]))
            big_a[:, cols] = active.astype(BF)
            big_b[:, cols] = slope.astype(BF)
            cp.store(panel(big_a, p), kept.at[Mlp.a + p, mine])
            if keep:
                cp.store(panel(big_b, p), kept.at[Mlp.gh + p, mine])
        return message[...].astype(F32) + nn(big_a[...], tall[...]), rstd

    def mlp_backward(cp, mine, upstream, unit, rstd, loads, slopes):
        grad, *late = norm_back(upstream, unit, rstd, norm_rows(1)[0])
        f32_a[...] = grad
        one[1] = grad.astype(BF)
        cp.store(one.at[1], kept.at[Mlp.gb, mine])
        for copy in loads:
            copy.wait()
        for p in range(PANELS):
            cols = slice(p * D, (p + 1) * D)
            back = nt(one[1], tall[cols, :])
            big_c[:, cols] = (back * slopes[:, cols].astype(F32)).astype(BF)
            cp.store(panel(big_c, p), kept.at[Mlp.gh + p, mine])
        return nt(big_c[...], wide[...]), late

    def encode_mlp(cp, m):
        mine = slice(m * rows, (m + 1) * rows)
        cp.store(message, kept.at[Mlp.x, mine])
        summed, _ = mlp_forward(cp, mine, True)
        f32_a[...] = summed
        cp.store(f32_a, kept32.at[mine])
        gain_1, shift_1 = norm_rows(1)
        sent[...] = (standardize(f32_a[...])[0] * gain_1 + shift_1).astype(BF)

    def encode_mlp_back(cp, m):
        mine = slice(m * rows, (m + 1) * rows)
        load_summed = cp.start(kept32.at[mine], f32_a)
        loads = [cp.start(kept.at[Mlp.x, mine], one.at[0])]
        load_summed.wait()
        unit, rstd = standardize(f32_a[...])
        upstream, late = mlp_backward(cp, mine, message[...].astype(F32), unit, rstd, loads, fetched)
        unit, rstd = standardize(one[0].astype(F32))
        grad, *early = norm_back(upstream, unit, rstd, norm_rows(0)[0])
        sent[...] = (grad + f32_a[...]).astype(BF)
        put_small(early, late)

    def decode_mlp(cp, m):
        mine = slice(m * rows, (m + 1) * rows)
        load = cp.start(cotangent.at[mine], one.at[2])
        summed, rstd_0 = mlp_forward(cp, mine, False)
        gain_1, shift_1 = norm_rows(1)
        unit, rstd = standardize(summed)
        one[3] = (unit * gain_1 + shift_1).astype(BF)
        cp.store(one.at[3], out.at[mine])
        load.wait()
        place = lax.broadcasted_iota(jnp.int32, (PREFIX, D), 0)
        masked = []
        for b in range(seqs):
            at = slice(b * PREFIX, (b + 1) * PREFIX)
            masked.append(jnp.where(place < lengths[m * seqs + b], one[2, at, :].astype(F32), 0.0))
        upstream, late = mlp_backward(cp, mine, jnp.concatenate(masked, axis=0), unit, rstd, [], big_b)
        grad, *early = norm_back(upstream, f32_b[...], rstd_0, norm_rows(0)[0])
        sent[...] = (grad + f32_a[...]).astype(BF)
        put_small(early, late)

    def decode_early(cp, m):
        if m < MICRO - 2:
            decode_early_one(cp, m)
            return

        def both(i, carry):
            own = Copies(sems)
            decode_early_one(own, m + i)
            own.finish()
            return carry

        lax.fori_loop(0, 2, both, 0)

    def decode_early_one(cp, m):
        mine = pl.ds(pl.multiple_of(m * rows, rows), rows)
        load = cp.start(text.at[mine], one.at[3])
        (gain_0, shift_0), (gain_1, shift_1) = norm_rows(0), norm_rows(1)
        load.wait()
        one[0] = (standardize(one[3].astype(F32))[0] * gain_0 + shift_0).astype(BF)
        cp.store(one.at[0], kept.at[Dec.u, mine])
        for p in range(3):
            cols = slice(p * D, (p + 1) * D)
            big_b[:, cols] = nn(one[0], wide[:, cols]).astype(BF)
            cp.store(panel(big_b, p), kept.at[Dec.q + p, mine])
        attend(seqs, *(panel(big_b, p) for p in range(4)), one.at[1], lambda b: lengths[m * seqs + b])
        cp.store(panel(big_b, 3), kept.at[Dec.p, mine])
        cp.store(one.at[1], kept.at[Dec.att, mine])
        f32_a[...] = one[3].astype(F32) + nn(one[1], wide[:, 3 * D :])
        cp.store(f32_a, kept32.at[mine])
        one[2] = (standardize(f32_a[...])[0] * gain_1 + shift_1).astype(BF)
        cp.store(one.at[2], kept.at[Dec.c, mine])
        big_c[:, :D] = nn(one[2], tall[:D, :]).astype(BF)
        cp.store(panel(big_c, 0), kept.at[Dec.qc, mine])

    def decode_cross(cp, m):
        mine = slice(m * rows, (m + 1) * rows)
        load_query = cp.start(kept.at[Dec.qc, mine], panel(big_a, 0))
        load_middle = cp.start(kept32.at[mine], f32_a)
        cp.store(message, kept.at[Dec.mem, mine])
        for p in (1, 2):
            cols = slice(p * D, (p + 1) * D)
            big_a[:, cols] = nn(message[...], tall[cols, :]).astype(BF)
            cp.store(panel(big_a, p), kept.at[Dec.kc + p - 1, mine])
        load_query.wait()
        attend(seqs, *(panel(big_a, p) for p in range(4)), one.at[1], None)
        cp.store(panel(big_a, 3), kept.at[Dec.pc, mine])
        cp.store(one.at[1], kept.at[Dec.cross, mine])
        load_middle.wait()
        sent[...] = (f32_a[...] + nn(one[1], tall[3 * D :, :])).astype(BF)

    def decode_cross_back(cp, m):
        mine = slice(m * rows, (m + 1) * rows)
        places = AHEAD[CROSS_BACK]
        cp.store(message, kept.at[Dec.gsec, mine])
        one[0] = nt(message[...], tall[3 * D :, :]).astype(BF)
        attend_back(seqs, *(panel(fetched, p) for p in range(4)), one.at[0], *(panel(big_c, p) for p in range(3)))
        for p in range(3):
            cp.store(panel(big_c, p), kept.at[places[p], mine])
        back = nt(big_c[:, D : 2 * D], tall[D : 2 * D, :]) + nt(big_c[:, 2 * D : 3 * D], tall[2 * D : 3 * D, :])
        sent[...] = back.astype(BF)

    def decode_late(cp, m, hook=None):
        mine = slice(m * rows, (m + 1) * rows)
        load_query = cp.start(kept.at[Dec.qc, mine], one.at[0])
        load_middle = cp.start(kept32.at[mine], f32_a)
        load_second = cp.start(kept.at[Dec.gsec, mine], one.at[1])
        loads = [cp.start(kept.at[Dec.q + p, mine], panel(big_b, p)) for p in range(4)]
        load_text = cp.start(text.at[mine], one.at[3])
        if hook:
            hook()
        load_query.wait()
        upstream = nt(one[0], tall[:D, :])
        load_middle.wait()
        load_second.wait()
        grad, *late = norm_back(upstream, *standardize(f32_a[...]), norm_rows(1)[0])
        f32_b[...] = grad + one[1].astype(F32)
        one[2] = f32_b[...].astype(BF)
        cp.store(one.at[2], kept.at[Dec.gmid, mine])
        one[0] = nt(one[2], wide[:, 3 * D :]).astype(BF)
        for copy in loads:
            copy.wait()
        attend_back(seqs, *(panel(big_b, p) for p in range(4)), one.at[0], *(panel(big_a, p) for p in range(3)))
        for p in range(3):
            cp.store(panel(big_a, p), kept.at[Dec.q + p, mine])
        upstream = nt(big_a[:, : 3 * D], wide[:, : 3 * D])
        load_text.wait()
        grad, *early = norm_back(upstream, *standardize(one[3].astype(F32)), norm_rows(0)[0])
        f32_a[...] = grad + f32_b[...]
        cp.store(f32_a, grads.at[mine])
        put_small(early, late)

    steps = {
        ENCODE: encode, ENCODE_MLP: encode_mlp, CROSS: decode_cross, DECODE_MLP: decode_mlp, CROSS_BACK: decode_cross_back,
        ENCODE_MLP_BACK: encode_mlp_back, ENCODE_BACK: encode_back, EARLY: decode_early, LATE: decode_late,
    }
    def last_slot():
        chips, held, left_over = shards // 2, kept.shape[1] - rows, {}
        for at, (left, right) in enumerate(weight_operands()):

            @pl.when(section == at)
            def _():
                cp, loads = Copies(sems), Copies(weight_sems)
                here = slice(0, held) if at in work else slice(0, held + rows)
                copies = []

                def hook():
                    for p in range(PANELS):
                        copies.append(loads.start(kept.at[right[p], here], right_v.at[p, here]))
                        if p == 0 or left[p] != left[p - 1]:
                            copies.append(loads.start(kept.at[left[p]], left_v.at[0 if p == 0 else 1]))

                if at in before:
                    finish_before(cp, *before[at])
                if at in work:
                    name, m = work[at]
                    steps[name](cp, m, hook)
                    for p in range(PANELS - 1):
                        right_v[p, held:] = panel(big_a, p)[...]
                    right_v[PANELS - 1, held:] = message[...] if at == 0 else one[2]
                else:
                    hook()
                for copy in copies:
                    copy.wait()
                left_over[at] = cp.sizes

        alone = section % 2 == 0
        for p in range(PANELS):
            from_left = jnp.where(alone, 1, 0) if p == PANELS - 1 else 0
            done_v[p % 2] = tn(left_v[from_left], right_v[p]).astype(BF).reshape(chips, 2, D // shards, D)
            rows_of_part = slice(p * D // shards, (p + 1) * D // shards)
            put_shares(shards, keep, give, rows_of_part, lambda chip, core: done_v[p % 2, chip, core])
        for at, stores in left_over.items():

            @pl.when(section == at)
            def _():
                for number, dtype in stores:
                    pair = (f32_a, f32_b) if dtype == F32 else (one.at[0], one.at[1])
                    pltpu.make_async_copy(*pair, sems.at[number]).wait()

    if small is not None:
        small[...] = jnp.zeros_like(small)
    if first:
        wide_in, tall_in, wide, tall = wide, tall, wide_out, tall_out

        def weight_loads(cp):
            for p in range(PANELS):
                at = slice(p * D, (p + 1) * D)
                yield [cp.start(tall_in.at[at], tall.at[at])]
            yield [cp.start(wide_in.at[:, p * D : (p + 1) * D], wide.at[:, p * D : (p + 1) * D]) for p in range(PANELS)]

        @pl.when(section == 0)
        def _():
            cp = Copies(sems)
            loads = []
            for p, more in enumerate(weight_loads(cp)):
                if p < PANELS:
                    more.append(cp.start(patches.at[:rows, p * D : (p + 1) * D], panel(big_a, p)))
                loads.append(more)
            encode(cp, 0, loads)
            cp.finish()

        @pl.when(section != 0)
        def _():
            for loads in list(weight_loads(Copies(sems))):
                for copy in loads:
                    copy.wait()

        return
    if shards:
        last_slot()
        return
    for at in sorted(set(work) | set(before) | set(coming)):

        @pl.when(section == at)
        def _():
            cp = Copies(sems)
            if at in coming:
                fetch_ahead(cp, *coming[at])
            if at in before:
                finish_before(cp, *before[at])
            if at in work:
                name, m = work[at]
                steps[name](cp, m)
            cp.finish()


def weight_operands():
    e, m, d = Enc, Mlp, Dec
    mlp = ([m.u] * 4 + [m.a + p for p in range(4)], [m.gh + p for p in range(4)] + [m.gb] * 4)
    encode = ([e.u] * 3 + [e.att] + [e.x + p for p in range(4)], [e.q, e.k, e.v, e.gfirst] + [e.gemb] * 4)
    decode = ([d.u] * 3 + [d.att, d.c, d.mem, d.mem, d.cross], [d.q, d.k, d.v, d.gmid, d.qc, d.kc, d.vc, d.gsec])
    return encode, mlp, decode, mlp


def by_section(values):
    section, chosen = lax.axis_index(SECTION), values[0]
    for at, value in enumerate(values[1:], 1):
        if value != values[0]:
            chosen = jnp.where(section == at, value, chosen)
    return chosen


def put_shares(shards, keep, give, rows, block):
    chips = shards // 2
    chip, core = lax.axis_index(DP) // 2, lax.axis_index(DP) % 2
    for step in range(chips):
        at = (chip + 2 * chips - 1 - step) % chips
        keep[step, rows] = block(at, core)
        give[step][rows] = block(at, 1 - core)


def tall_kernel(shards, kept, extra, keep, *refs):
    *give, left_v, right_v, done_v, sems = refs
    section = lax.axis_index(SECTION)
    lefts = [[t[0][PANELS + p] for t in weight_operands()] for p in range(PANELS)]
    rights = [[t[1][PANELS + p] for t in weight_operands()] for p in range(PANELS)]
    alone = section == 2
    share = FF // shards
    here = D // share // 2

    def operands(p, begin):
        left = pltpu.make_async_copy(kept.at[by_section(lefts[p])], left_v.at[p], sems.at[0, p])
        right = pltpu.make_async_copy(kept.at[by_section(rights[p])], right_v.at[p], sems.at[1, p])
        for copy, always in ((left, True), (right, p == 0)):
            act = copy.start if begin else copy.wait
            act() if always else pl.when(alone)(act)

    for p in range(PANELS):
        operands(p, True)
    for p in range(PANELS):
        operands(p, False)
        done = tn(left_v[p], right_v[jnp.where(alone, p, 0) if p else 0]).astype(BF)
        done_v[p * here : (p + 1) * here] = done.reshape(here, 2, share, D)
    put_shares(shards, keep, give, slice(0, share), lambda chip, core: done_v[chip, core])
    for at in range(shards // 2):
        keep[at, share:] = extra[...]
        give[at][share:] = extra[...]


def share_shapes(shards, rows):
    return [jax.ShapeDtypeStruct((shards // 2, rows, D), BF)] + [jax.ShapeDtypeStruct((rows, D), BF)] * (shards // 2)


def tall_half(shards, kept, extra):
    total = kept.shape[1]
    in_vmem = pl.BlockSpec(memory_space=pltpu.VMEM)
    shapes = share_shapes(shards, FF // shards + extra.shape[0])
    flops = 2 * PANELS * D * D * total
    return pl.pallas_call(
        functools.partial(tall_kernel, shards),
        out_shape=tuple(shapes),
        in_specs=[pl.BlockSpec(memory_space=pl.ANY), in_vmem],
        out_specs=(in_vmem,) * len(shapes),
        scratch_shapes=[
            pltpu.VMEM((PANELS, total, D), BF),
            pltpu.VMEM((PANELS, total, D), BF),
            pltpu.VMEM((shards // 2, 2, FF // shards, D), BF),
            pltpu.SemaphoreType.DMA((2, PANELS)),
        ],
        cost_estimate=pl.CostEstimate(flops=flops, bytes_accessed=flops // total, transcendentals=0),
        compiler_params=pltpu.CompilerParams(vmem_limit_bytes=WEIGHT_LIMIT, has_side_effects=True),
        name="tall_half",
    )(kept, extra)


def after(value, other):
    return lax.optimization_barrier((value, other))[0]


def ring_scatter(wide_half, kept, little, shards, finish):
    chips, rows = shards // 2, FF // shards
    flip = [(d, d ^ 1) for d in range(shards)]
    onward = [(d, (d + 2) % shards) for d in range(shards)]
    sent = None

    def exchange(keep, *give):
        return [(keep[at], lax.ppermute(part, DP, flip)) for at, part in enumerate(give)]

    def add(parts, running, piece=slice(None), whole=False):
        keep, got = parts
        if sent is not None and running is None:
            got = after(got, sent)
        elif sent is not None:
            running = after(running, sent)
        value = keep[piece].astype(F32) + got[piece].astype(F32)
        if running is None:
            return value
        return value + (running[piece] if whole else running).astype(F32)

    def send(value):
        nonlocal sent
        sent = value.astype(BF)
        return lax.ppermute(sent, DP, onward)

    wide = exchange(*wide_half)
    running = send(add(wide[0], None))
    tall = exchange(*tall_half(shards, after(kept, sent), little))
    cut = (rows + little.shape[0]) * 3 // 8 // 16 * 16
    pieces = [slice(cut, rows + little.shape[0]), slice(0, cut)]
    running = send(add(wide[1], running))
    low = [send(add(tall[0], None))] * len(pieces)
    for step in range(1, chips - 1):
        if step + 1 < chips - 1:
            running = send(add(wide[step + 1], running))
        else:
            wide = sent = add(wide[-1], running)
        low = [send(add(tall[step], got, piece, step == 1)) for piece, got in zip(pieces, low)]
    high = add(tall[-1], low[0], pieces[0])
    small = sent = finish(high[-little.shape[0] :])
    return wide, high, add(tall[-1], low[1], pieces[1]), small


def weight_part(i, kept):
    lefts, rights = ([t[side][i] for t in weight_operands()] for side in (0, 1))
    left, right = (lax.dynamic_index_in_dim(kept, by_section(values), 0, keepdims=False) for values in (lefts, rights))
    return tn(left, right).astype(BF)


def schedule():
    plan = [(0, 0, ENCODE, 1), (1, 2, ENCODE_MLP, 1), (2, 4, CROSS, 1), (3, 6, DECODE_MLP, -1), (2, 8, CROSS_BACK, -1),
            (1, 10, ENCODE_MLP_BACK, -1), (0, 12, ENCODE_BACK, 0), (2, 1, EARLY, 0), (2, 12, LATE, 0)]
    slots = []
    for k in range(MICRO + 12):
        work, sends = {}, []
        for section, begin, name, way in plan:
            if 0 <= k - begin < MICRO - (name == EARLY):
                assert section not in work
                work[section] = (name, k - begin)
                if way:
                    sends.append((section, section + way))
        slots.append((work, sends))
    return slots


def on_device(patches, text, lengths, cotangent, wide, tall, gain, shift):
    total = patches.shape[0]
    rows = total // MICRO
    shards = lax.axis_size(DP)
    share = D // shards
    in_ring = share % 16 == 0 and shards % 2 == 0 and D % (2 * FF // shards) == 0
    wide, tall, norms = wide[0], tall[0], jnp.concatenate([gain[0], shift[0]], axis=0)
    anywhere = pl.BlockSpec(memory_space=pl.ANY)
    in_vmem = pl.BlockSpec(memory_space=pltpu.VMEM)
    in_smem = pl.BlockSpec(memory_space=pltpu.SMEM)
    specs = [in_smem] + [anywhere] * 3 + [in_vmem] * 5 + [anywhere] * 4 + [in_vmem] + [anywhere] * 4 + [in_vmem] * 5
    shapes = [
        jax.ShapeDtypeStruct((SLOTS, total, D), BF),
        jax.ShapeDtypeStruct((total, D), F32),
        jax.ShapeDtypeStruct((total, D), BF),
        jax.ShapeDtypeStruct((total, D), F32),
        jax.ShapeDtypeStruct((rows, D), BF),
        jax.ShapeDtypeStruct((8, D), F32),
        jax.ShapeDtypeStruct(wide.shape, BF),
        jax.ShapeDtypeStruct(tall.shape, BF),
        jax.ShapeDtypeStruct((rows, FF), BF),
    ]
    state, messages, smalls, done, before, fetched = [None] * 4, [None, None], [], None, {}, None
    slots = schedule()
    for k, (work, sends) in enumerate(slots):
        now, old = {name for name, _ in work.values()}, {name for name, _ in before.values()}

        def given(value, *names):
            return value if now & set(names) else None

        operands = [
            given(lengths, EARLY, DECODE_MLP),
            given(patches, ENCODE),
            given(text, EARLY, LATE),
            given(cotangent, DECODE_MLP),
            wide, tall, norms,
            given(messages[-2], ENCODE_MLP, CROSS, DECODE_MLP, CROSS_BACK, ENCODE_MLP_BACK, ENCODE_BACK),
            done if old - {EARLY, LATE} else None,
            *state,
            given(fetched, *AHEAD),
        ]
        after_this = slots[k + 1][0] if k + 1 < len(slots) else {}
        coming = {at: (name, m) for at, (name, m) in after_this.items() if name in AHEAD}
        results = [True] * 4 + [bool(now - {EARLY, LATE}), bool(now & {DECODE_MLP, ENCODE_MLP_BACK, ENCODE_BACK, LATE})]
        results += [k == 0] * 2 + [bool(coming)]
        present = tuple(value is not None for value in operands) + tuple(results)
        places = [i for i, value in enumerate(operands) if value is not None]
        merged = in_ring and k + 1 == len(slots)
        more = share_shapes(shards, FF // shards) if merged else []
        values = pl.pallas_call(
            functools.partial(slot_kernel, work, before, coming, shards if merged else 0, rows, present),
            out_shape=tuple(shape for shape, here in zip(shapes, results) if here) + tuple(more),
            in_specs=[anywhere if k == 0 and i in (4, 5) else specs[i] for i in places],
            out_specs=[spec for spec, here in zip(specs[14:], results) if here] + [in_vmem] * len(more),
            input_output_aliases={places.index(9 + i): i for i in range(4)} if k else {},
            scratch_shapes=[
                pltpu.VMEM((rows, FF), BF),
                pltpu.VMEM((rows, FF), BF),
                pltpu.VMEM((rows, FF), BF),
                pltpu.VMEM((4, rows, D), BF),
                pltpu.VMEM((rows, D), F32),
                pltpu.VMEM((rows, D), F32),
                pltpu.VMEM((rows, D), F32),
                pltpu.SemaphoreType.DMA((48,)),
                *(
                    [
                        pltpu.VMEM((2, total, D), BF),
                        pltpu.VMEM((PANELS, total, D), BF),
                        pltpu.VMEM((2, shards // 2, 2, share, D), BF),
                        pltpu.SemaphoreType.DMA((2 * PANELS,)),
                    ]
                    if merged
                    else []
                ),
            ],
            compiler_params=pltpu.CompilerParams(vmem_limit_bytes=LAST_LIMIT if merged else VMEM_LIMIT if k else FIRST_LIMIT, has_side_effects=True),
            cost_estimate=pl.CostEstimate(flops=9_000_000_000, bytes_accessed=4_000_000, transcendentals=0),
            name=f"slot_{k}",
        )(*(operands[i] for i in places))
        state, rest = list(values[:4]), list(values[4:])
        done = rest.pop(0) if results[4] else None
        if results[5]:
            smalls.append(rest.pop(0))
        if k == 0:
            wide, tall = rest
        fetched = rest[-1] if coming else None
        wide_half = rest
        messages.append(lax.ppermute(done, SECTION, sends) if sends else None)
        before = work
    kept, _, out, grads = state

    little = sum(smalls)
    high = little.astype(BF)
    little = jnp.concatenate([high, (little - high.astype(F32)).astype(BF)], axis=0)

    def norm_grads(sums):
        sums = sums[:4].astype(F32) + sums[8:12].astype(F32)
        sums = lax.dynamic_slice_in_dim(sums, lax.axis_index(DP) * share, share, axis=1)
        return sums[None, :2], sums[None, 2:]

    if in_ring:
        mine, high, low, (gain_grad, shift_grad) = ring_scatter(wide_half, kept, little, shards, norm_grads)
        wide_grad = jnp.concatenate([mine[p * share : (p + 1) * share] for p in range(PANELS)], axis=1)
        tall_grad = jnp.concatenate([low, high[:-16]], axis=0)
    else:
        parts = [weight_part(i, kept) for i in range(2 * PANELS)]
        wide_grad = lax.psum_scatter(jnp.concatenate(parts[:PANELS], axis=1), DP, scatter_dimension=0, tiled=True)
        tall_grad = lax.psum_scatter(jnp.concatenate(parts[PANELS:], axis=0), DP, scatter_dimension=0, tiled=True)
        gain_grad, shift_grad = norm_grads(lax.psum(little, DP))
    return (
        out[None],
        grads[None],
        wide_grad.astype(F32)[None],
        tall_grad.astype(F32)[None],
        gain_grad,
        shift_grad,
    )


def solution(mesh):
    return jax.shard_map(
        on_device,
        mesh=mesh,
        in_specs=(
            P(DP, None),
            P(DP, None),
            P(DP),
            P(DP, None),
            P(SECTION, None, None),
            P(SECTION, None, None),
            P(SECTION, None, None),
            P(SECTION, None, None),
        ),
        out_specs=(
            P(SECTION, DP, None),
            P(SECTION, DP, None),
            P(SECTION, DP, None),
            P(SECTION, DP, None),
            P(SECTION, None, DP),
            P(SECTION, None, DP),
        ),
        check_vma=False,
    )
```
